256 devices in a mesh: seq: 128 (over z, x, y), ch: 2 (over core).
Axes of the slice: x: 4, y: 4, z: 8, core: 2. Of those that a mesh axis runs over, the one named last changes fastest.
Arguments:
- tokens: bfloat16 [16384, 1536], P('seq', 'ch'), may hold values from -24 to 24
- cotangent: bfloat16 [16384, 1536], P('seq', 'ch'), may hold values from -6 to 6
- proj_u: bfloat16 [1536, 1536], P('seq', 'ch'), may hold values from -0.15625 to 0.15625
- proj_v: bfloat16 [1536, 1536], P('seq', 'ch'), may hold values from -0.15625 to 0.15625
- right_factor: bfloat16 [128, 128, 128], P('seq'), may hold values from -0.5 to 0.5
- left_factor: bfloat16 [128, 128, 128], P('seq'), may hold values from -0.5 to 0.5
- conv_u: float32 [3, 1536], P(None, 'ch'), may hold values from -3 to 3
- conv_v: float32 [3, 1536], P(None, 'ch'), may hold values from -3 to 3
Outputs:
- mixed: bfloat16 [16384, 1536], P('seq', 'ch')
- tokens_grad: bfloat16 [16384, 1536], P('seq', 'ch')
- proj_u_grad: float32 [1536, 1536], P('seq', 'ch')
- proj_v_grad: float32 [1536, 1536], P('seq', 'ch')
- right_grad: float32 [128, 128, 128], P('seq')
- left_grad: float32 [128, 128, 128], P('seq')
- conv_u_grad: float32 [3, 1536], P(None, 'ch')
- conv_v_grad: float32 [3, 1536], P(None, 'ch')
The draws below stay inside these ranges and needn't reach their ends.
All inputs are finite; a program needn't handle non-finite values.
Results may differ from the reference program's by a relative error of at most 0.01.
Values may be sent and summed in bfloat16 or wider, within the bound.
A program may use at most 128 MiB of HBM per device.

```python
import jax
import jax.numpy as jnp
from jax import lax

D = 1536
BLK = 128
TOKENS = 16384
GROUPS = 128


def spiked(values, key, source, target, blocks, factor):
    def block_of(axis_at):
        return (jnp.arange(values.shape[axis_at]) // (values.shape[axis_at] // blocks)).reshape((-1,) + (1,) * (values.ndim - 1 - axis_at))

    first = jax.random.permutation(key, blocks)[block_of(target)]
    other_side = (block_of(target) + blocks // 2) % blocks
    return jnp.where((block_of(source) == first) | (block_of(source) == other_side), factor * values, values)


def levels(stream_key, extent, split, low, top_value):
    factor_of, own = 1.0, jax.random.fold_in(stream_key, 6)
    for position, parts in split:
        heights = jnp.exp(jax.random.uniform(jax.random.fold_in(own, position), (parts,), jnp.float32, low / len(split), top_value / len(split)))
        factor_of = factor_of * jnp.repeat(heights, extent[position] // parts).reshape([-1 if axis == position else 1 for axis in range(len(extent))])
    return factor_of


def gaussian(stream_key, shape, deviation, bound, cuts=(), kind=jnp.bfloat16):
    result = jax.random.normal(stream_key, shape, jnp.float32) * deviation
    if len(cuts) > 0:
        result = levels(stream_key, shape, cuts, -0.22, 0.18) * result
    return jnp.clip(result, min=-bound, max=bound).astype(kind)


def bell_draw_with(stream_key, extent, scale, most, split, heavy, kind=jnp.bfloat16):
    result = scale * jax.random.normal(stream_key, extent, jnp.float32)
    if split:
        result = result * levels(stream_key, extent, split, -0.22, 0.18)
    return jnp.clip(spiked(result, jax.random.fold_in(stream_key, 3), *heavy), -most, most).astype(kind)


def setup_inputs(seed: int = 0) -> dict:
    splits = jax.random.split(jax.random.key(seed), 9)
    return {
        "tokens": bell_draw_with(splits[0], (TOKENS, D), 1.0, 24.0, ((0, 128), (1, 2)), (0, 1, 128, 5.5)),
        "cotangent": gaussian(splits[1], (TOKENS, D), 1.0, 6.0, ((0, 128), (1, 2))),
        "proj_u": gaussian(splits[2], (D, D), D ** -0.5, 0.15625, ((0, 128), (1, 2))),
        "proj_v": gaussian(splits[3], (D, D), D ** -0.5, 0.15625, ((0, 128), (1, 2))),
        "right_factor": gaussian(splits[4], (GROUPS, BLK, BLK), BLK ** -0.5, 0.5, ((0, 128),)),
        "left_factor": gaussian(splits[5], (BLK, GROUPS, GROUPS), GROUPS ** -0.5, 0.5, ((0, 128),)),
        "conv_u": gaussian(splits[6], (3, D), 0.5, 3.0, ((1, 2),), jnp.float32),
        "conv_v": gaussian(splits[7], (3, D), 0.5, 3.0, ((1, 2),), jnp.float32),
    }


def earlier(values, offset_rows):
    zero_rows = jnp.zeros((offset_rows, values.shape[1]), values.dtype)
    return jnp.concatenate([zero_rows, values[: values.shape[0] - offset_rows]], axis=0)


def later(values, offset_rows):
    zero_rows = jnp.zeros((offset_rows, values.shape[1]), values.dtype)
    return jnp.concatenate([values[offset_rows:], zero_rows], axis=0)


def rounded(values):
    return lax.optimization_barrier(values.astype(jnp.bfloat16)).astype(jnp.float32)


def reference(tokens, cotangent, proj_u, proj_v, right_factor, left_factor, conv_u, conv_v):
    seq_len, chan_count = tokens.shape
    block_size = right_factor.shape[1]
    groups = seq_len // block_size
    chan_blocks = chan_count // block_size
    right_f = right_factor.astype(jnp.float32)
    left_f = left_factor.astype(jnp.float32)

    def one_block(state_tuple, block_index):
        tokens_grad, right_grad, left_grad = state_tuple
        first_col = block_index * block_size
        w_u = lax.dynamic_slice_in_dim(proj_u, first_col, block_size, 1)
        w_v = lax.dynamic_slice_in_dim(proj_v, first_col, block_size, 1)
        k_u = lax.dynamic_slice_in_dim(conv_u, first_col, block_size, 1)
        k_v = lax.dynamic_slice_in_dim(conv_v, first_col, block_size, 1)
        grad_out = lax.dynamic_slice_in_dim(cotangent, first_col, block_size, 1).astype(jnp.float32)
        pre_u = jnp.dot(tokens, w_u, preferred_element_type=jnp.float32).astype(jnp.bfloat16)
        pre_v = jnp.dot(tokens, w_v, preferred_element_type=jnp.float32).astype(jnp.bfloat16)
        conv_cu = (k_u[0] * pre_u + k_u[1] * earlier(pre_u, 1) + k_u[2] * earlier(pre_u, 2)).astype(jnp.bfloat16)
        gate_v = k_v[0] * pre_v + k_v[1] * earlier(pre_v, 1) + k_v[2] * earlier(pre_v, 2)
        shaped = conv_cu.reshape(groups, block_size, block_size).astype(jnp.float32)
        rows_mix = rounded(jnp.einsum("jpi,jic->jpc", right_f, shaped))
        seq_mix = rounded(jnp.einsum("iab,bic->aic", left_f, rows_mix)).reshape(seq_len, block_size)
        out_block = (gate_v * seq_mix).astype(jnp.bfloat16)
        grad_mix = rounded(grad_out * gate_v).reshape(groups, block_size, block_size)
        grad_gate = grad_out * seq_mix
        left_grad = left_grad + jnp.einsum("aic,bic->iab", grad_mix, rows_mix)
        grad_rows = rounded(jnp.einsum("iab,aic->bic", left_f, grad_mix))
        right_grad = right_grad + jnp.einsum("jpc,jic->jpi", grad_rows, shaped)
        grad_conv = jnp.einsum("jpi,jpc->jic", right_f, grad_rows).reshape(seq_len, block_size)
        grad_pu = (k_u[0] * grad_conv + k_u[1] * later(grad_conv, 1) + k_u[2] * later(grad_conv, 2)).astype(jnp.bfloat16)
        grad_pv = (k_v[0] * grad_gate + k_v[1] * later(grad_gate, 1) + k_v[2] * later(grad_gate, 2)).astype(jnp.bfloat16)
        pre_uf = pre_u.astype(jnp.float32)
        pre_vf = pre_v.astype(jnp.float32)
        kernel_u = jnp.stack([jnp.sum(grad_conv * earlier(pre_uf, lag_index), axis=0) if lag_index > 0 else jnp.sum(grad_conv * pre_uf, axis=0) for lag_index in range(3)])
        kernel_v = jnp.stack([jnp.sum(grad_gate * earlier(pre_vf, lag_index), axis=0) if lag_index > 0 else jnp.sum(grad_gate * pre_vf, axis=0) for lag_index in range(3)])
        tokens_grad = tokens_grad + jnp.dot(grad_pu, w_u.T, preferred_element_type=jnp.float32) + jnp.dot(grad_pv, w_v.T, preferred_element_type=jnp.float32)
        weight_u = jnp.dot(tokens.T, grad_pu, preferred_element_type=jnp.float32)
        weight_v = jnp.dot(tokens.T, grad_pv, preferred_element_type=jnp.float32)
        return (tokens_grad, right_grad, left_grad), (out_block, weight_u, weight_v, kernel_u, kernel_v)

    start_state = (jnp.zeros((seq_len, chan_count), jnp.float32),
                   jnp.zeros((groups, block_size, block_size), jnp.float32),
                   jnp.zeros((block_size, groups, groups), jnp.float32))
    final_state, stacked = lax.scan(one_block, start_state, jnp.arange(chan_blocks, dtype=jnp.int32))
    tokens_grad, right_grad, left_grad = final_state
    out_blocks, weight_u, weight_v, kernel_u, kernel_v = stacked
    mixed = out_blocks.transpose(1, 0, 2).reshape(seq_len, chan_count)
    proj_u_grad = weight_u.transpose(1, 0, 2).reshape(chan_count, chan_count)
    proj_v_grad = weight_v.transpose(1, 0, 2).reshape(chan_count, chan_count)
    conv_u_grad = kernel_u.transpose(1, 0, 2).reshape(3, chan_count)
    conv_v_grad = kernel_v.transpose(1, 0, 2).reshape(3, chan_count)
    return (mixed, tokens_grad.astype(jnp.bfloat16), proj_u_grad, proj_v_grad,
            right_grad, left_grad, conv_u_grad, conv_v_grad)
```

```python
import functools
import types

import jax
import jax.numpy as jnp
from jax import lax
from jax.experimental import pallas as pl
from jax.experimental.pallas import tpu as pltpu
from jax.sharding import PartitionSpec as P

MESH = pl.DeviceIdType.MESH
BF = jnp.bfloat16
F32 = jnp.float32
Y = 4
X = 4


def dot(a, b):
    return jnp.dot(a, b, preferred_element_type=F32)


def dot_nt(a, b):
    return lax.dot_general(a, b, (((1,), (1,)), ((), ())), preferred_element_type=F32)


def transposed(a):
    return a.astype(F32).T.astype(BF)


def by_distance(n):
    return sorted(range(1, n), key=lambda k: (min(k, n - k), k))


def kernel(Z, X, r):
    NG = Z * X
    BLK, chans = r.tok_in.shape
    W2 = chans // 2
    HW = W2 // 2
    HB = BLK // 2
    N = Y * BLK
    R = r.pu_in.shape[0]
    RB = Y * R

    s = lax.axis_index("seq")
    c = lax.axis_index("ch")
    g = s // Y
    y = lax.rem(s, Y)
    z = g // X
    x = lax.rem(g, X)
    sib = 1 - c

    def dev(gg, yy):
        return gg * Y + yy

    def in_u(shape):
        return lax.broadcasted_iota(jnp.int32, shape, len(shape) - 1) < HW

    def pick(u, v):
        return jnp.where(in_u(u.shape), u, v)

    def swap(v):
        return pltpu.roll(v, HW, 1)

    def rc(src, dst, send_sem, recv_sem, seq, ch):
        return pltpu.make_async_remote_copy(
            src_ref=src,
            dst_ref=dst,
            send_sem=send_sem,
            recv_sem=recv_sem,
            device_id=(seq, ch),
            device_id_type=MESH,
        )

    pending = []

    def go(copy):
        copy.start()
        pending.append(copy)

    def y_send(src_of, dst, send, recv):
        for k in (2, 1, 3):
            to = lax.rem(y + k, Y)
            go(rc(src_of(to), dst.at[y], send.at[to], recv.at[y], dev(g, to), c))

    def y_wait(dst, send, recv):
        for k in (1, 3, 2):
            of = lax.rem(y + k, Y)
            rc(dst.at[of], dst.at[of], send.at[of], recv.at[of], s, c).wait_recv()

    barrier = pltpu.get_barrier_semaphore()

    def greet(k, carry):
        pl.semaphore_signal(
            barrier, inc=1, device_id=(dev(lax.rem(g + k, NG), y), c), device_id_type=MESH
        )
        return carry

    for k in (1, 2, 3):
        pl.semaphore_signal(
            barrier, inc=1, device_id=(dev(g, lax.rem(y + k, Y)), c), device_id_type=MESH
        )
    pl.semaphore_signal(barrier, inc=1, device_id=(s, sib), device_id_type=MESH)
    lax.fori_loop(1, NG, greet, 0)

    wpad = r.wpad
    wpad[...] = jnp.zeros_like(wpad)
    wpad[0, 0:R, :] = r.pu_in[...].astype(F32)
    wpad[1, 0:R, :] = r.pv_in[...].astype(F32)
    for h in range(2):
        uh = wpad[0, :, h * W2 : (h + 1) * W2]
        vh = wpad[1, :, h * W2 : (h + 1) * W2]
        r.wmsg[2 * h] = pick(uh, swap(vh)).astype(BF)
        r.wmsg[2 * h + 1] = pick(swap(uh), vh).astype(BF)
        xh = r.cot_in[:, h * W2 : (h + 1) * W2].astype(F32)
        top, bottom = xh[:HB], xh[HB:]
        r.cmsg[2 * h] = pick(top, swap(bottom)).astype(BF)
        r.cmsg[2 * h + 1] = pick(swap(top), bottom).astype(BF)

    pl.semaphore_wait(barrier, NG - 1 + Y)

    y_send(lambda to: r.wmsg.at[to], r.wland, r.wy_s, r.wy_r)
    r.wland[y] = r.wmsg[y]
    tokbuf = r.tokbuf
    go(rc(r.tok_in, tokbuf.at[c, y], r.ts_s.at[y], r.tok_r.at[c, y], s, sib))
    for k in (2, 1, 3):
        to = lax.rem(y + k, Y)
        go(rc(r.tok_in, tokbuf.at[c, y], r.ty_s.at[to], r.tok_r.at[c, y], dev(g, to), c))
    y_send(lambda to: r.rf_in.at[0], r.rbuf, r.rf_s, r.rf_r)
    y_send(lambda to: r.cmsg.at[to], r.cland, r.cy_s, r.cy_r)
    y_send(lambda to: r.lf_in.at[0], r.lbuf, r.lf_s, r.lf_r)
    tokbuf[c, y] = r.tok_in[...]
    r.rbuf[y] = r.rf_in[0]
    r.lbuf[y] = r.lf_in[0]
    r.cland[y] = r.cmsg[y]

    row = lax.broadcasted_iota(jnp.int32, (RB, Y * 16), 0)
    col = lax.broadcasted_iota(jnp.int32, (RB, Y * 16), 1)
    sel = jnp.zeros((RB, Y * 16), F32)
    for a in range(Y):
        hit = (row >= R * a) & (row < R * (a + 1)) & (col - row == (16 - R) * a)
        sel = jnp.where(hit, 1.0, sel)
    sel = sel.astype(BF)
    y_wait(r.wland, r.wy_s, r.wy_r)
    wbuf = r.wbuf
    wbuf[z, x] = dot(sel, r.wland[...].reshape(Y * 16, W2)).astype(BF)

    for k in reversed(by_distance(Z)):
        to = lax.rem(z + k, Z)
        go(rc(wbuf.at[z, x], wbuf.at[z, x], r.gz_s.at[to], r.g_r.at[z, x], dev(to * X + x, y), c))

    def along_x(of):
        for k in (2, 1, 3):
            to = lax.rem(x + k, X)
            go(rc(wbuf.at[of, x], wbuf.at[of, x], r.gx_s.at[of, to], r.g_r.at[of, x], dev(z * X + to, y), c))

    along_x(z)
    for k in by_distance(Z):
        of = lax.rem(z + k, Z)
        rc(wbuf.at[of, x], wbuf.at[of, x], r.gz_s.at[of], r.g_r.at[of, x], s, c).wait_recv()
        along_x(of)

    for k in (1, 3, 2):
        of = lax.rem(y + k, Y)
        rc(tokbuf.at[c, of], tokbuf.at[c, of], r.ty_s.at[of], r.tok_r.at[c, of], s, c).wait_recv()
        go(rc(tokbuf.at[c, of], tokbuf.at[c, of], r.ts_s.at[of], r.tok_r.at[c, of], s, sib))

    out_i = lax.broadcasted_iota(jnp.int32, (N, N), 0)
    in_i = lax.broadcasted_iota(jnp.int32, (N, N), 1)

    def hits(a, b):
        return jnp.where(a == b, 1.0, 0.0).astype(BF)

    def swapped_index(v):
        return (lax.rem(v // 4, 4)) * BLK + (v // 16) * 4 + lax.rem(v, 4)

    def rotated_index(v):
        return lax.rem(v, 4) * BLK + (v // 16) * 4 + lax.rem(v // 4, 4)

    r.to_msg1[...] = hits(in_i, rotated_index(out_i))
    r.from_msg1[...] = hits(out_i, swapped_index(in_i))
    r.to_msg2[...] = hits(in_i, swapped_index(out_i))
    r.from_msg2[...] = hits(out_i, rotated_index(in_i))

    kpad = r.kpad
    kpad[...] = jnp.zeros_like(kpad)
    kpad[0, 0:3, :] = r.cu_in[...]
    kpad[1, 0:3, :] = r.cv_in[...]
    kk = jnp.zeros((8, W2), F32)
    for h in range(2):
        uh = kpad[0, :, h * W2 : (h + 1) * W2]
        vh = kpad[1, :, h * W2 : (h + 1) * W2]
        kk = jnp.where(y == 2 * h, pick(uh, swap(vh)), kk)
        kk = jnp.where(y == 2 * h + 1, pick(swap(uh), vh), kk)
    k0, k1, k2 = kk[0:1], kk[1:2], kk[2:3]

    y_wait(r.cland, r.cy_s, r.cy_r)
    cot2 = r.cot2
    for j in range(Y):
        m = r.cland[j].astype(F32)
        cot2[j * BLK : j * BLK + HB, :] = swap(m)
        cot2[j * BLK + HB : (j + 1) * BLK, :] = m
    y_wait(r.rbuf, r.rf_s, r.rf_r)
    for j in range(Y):
        r.rt[j] = transposed(r.rbuf[j])

    for kx in (1, 3, 2):
        ofx = lax.rem(x + kx, X)
        for kz in [0] + by_distance(Z):
            of = lax.rem(z + kz, Z)
            rc(wbuf.at[of, ofx], wbuf.at[of, ofx], r.gx_s.at[of, ofx], r.g_r.at[of, ofx], s, c).wait_recv()
    for of in range(Y):
        rc(tokbuf.at[sib, of], tokbuf.at[sib, of], r.ts_s.at[of], r.tok_r.at[sib, of], s, c).wait_recv()

    half = Z // 2
    pre = dot(tokbuf[0].reshape(N, chans), wbuf[0:half].reshape(chans, W2))
    pre = pre + dot(tokbuf[1].reshape(N, chans), wbuf[half:].reshape(chans, W2))
    ext = r.ext
    ext[8 : 8 + N, :] = pre.astype(BF).astype(F32)
    go(rc(ext.at[pl.ds(N, 8)], ext.at[pl.ds(0, 8)], r.h_s.at[0], r.h_r.at[0], dev(lax.rem(g + 1, NG), y), c))
    rc(ext.at[pl.ds(0, 8)], ext.at[pl.ds(0, 8)], r.h_s.at[0], r.h_r.at[0], s, c).wait_recv()

    @pl.when(g == 0)
    def _():
        ext[0:8, :] = jnp.zeros((8, W2), F32)

    cvs, ccb, vb = r.cvs, r.ccb, r.vb
    for j in range(Y):
        at = j * BLK
        cv = k0 * ext[8 + at : 8 + at + BLK, :] + k1 * ext[7 + at : 7 + at + BLK, :] + k2 * ext[6 + at : 6 + at + BLK, :]
        cvs[at : at + BLK, :] = cv
        ccb[j] = cv.astype(BF)
        vb[at : at + BLK, :] = pick(dot(r.rbuf[j], ccb[j]), cot2[at : at + BLK, :] * cv).astype(BF)

    def exchange(src, dst, send, recv):
        def start(k, carry):
            to = lax.rem(g + k, NG)
            rc(src.at[to], dst.at[g], send.at[to], recv.at[g], dev(to, y), c).start()
            return carry

        lax.fori_loop(1, NG, start, 0)
        dst[g] = src[g]

    def exchange_wait(src, dst, send, recv):
        def wait(k, carry):
            of = lax.rem(g + NG - k, NG)
            rc(dst.at[of], dst.at[of], send.at[of], recv.at[of], s, c).wait_recv()
            return carry

        lax.fori_loop(1, NG, wait, 0)

    def exchange_sent(src, send):
        def wait(k, carry):
            to = lax.rem(g + k, NG)
            rc(src.at[to], src.at[to], send.at[to], send.at[to], s, c).wait_send()
            return carry

        lax.fori_loop(1, NG, wait, 0)

    r.a1s[...] = dot(r.to_msg1[...], vb[...]).astype(BF).reshape(NG, 16, W2)
    exchange(r.a1s, r.a1r, r.a1_s, r.a1_r)

    tokt = r.tokt
    for i in range(2):
        tokt[i * half : (i + 1) * half] = transposed(tokbuf[i].reshape(N, chans)).reshape(half, X * RB, N)
    y_wait(r.lbuf, r.lf_s, r.lf_r)
    for j in range(Y):
        r.lt[j] = transposed(r.lbuf[j])

    exchange_wait(r.a1s, r.a1r, r.a1_s, r.a1_r)
    xb = r.xb
    xb[...] = dot(r.from_msg1[...], r.a1r[...].reshape(N, W2)).astype(BF)
    for i in range(Y):
        xi = xb[i * BLK : (i + 1) * BLK, :]
        vb[i * BLK : (i + 1) * BLK, :] = pick(dot(r.lbuf[i], xi), dot(r.lt[i], xi)).astype(BF)
    r.a2s[...] = dot(r.to_msg2[...], vb[...]).astype(BF).reshape(NG, 16, W2)
    exchange(r.a2s, r.a2r, r.a2_s, r.a2_r)

    for i in range(Y):
        xi = xb[i * BLK : (i + 1) * BLK, :]
        xs = swap(xi.astype(F32))
        xs = pick(xs, jnp.zeros_like(xs)).astype(BF)
        r.lgs[i] = dot_nt(xs, xi).astype(BF)
    y_send(lambda to: r.lgs.at[to], r.lgl, r.lg_s, r.lg_r)
    r.lgl[y] = r.lgs[y]

    def y_sum(land):
        return (land[0].astype(F32) + land[1].astype(F32)) + (land[2].astype(F32) + land[3].astype(F32))

    exchange_wait(r.a2s, r.a2r, r.a2_s, r.a2_r)
    extg = r.extg
    zs = r.zs
    zs[...] = swap(dot(r.from_msg2[...], r.a2r[...].reshape(N, W2)))
    for j in range(Y):
        at = j * BLK
        zj = zs[at : at + BLK, :]
        extg[at : at + BLK, :] = pick(dot(r.rt[j], zj.astype(BF)), cot2[at : at + BLK, :] * zj)
    go(rc(extg.at[pl.ds(0, 8)], extg.at[pl.ds(N, 8)], r.h_s.at[1], r.h_r.at[1], dev(lax.rem(g + NG - 1, NG), y), c))

    for j in range(Y):
        at = j * BLK
        zj = zs[at : at + BLK, :]
        m = cvs[at : at + BLK, :] * zj
        r.mmsg[j] = pick(swap(m[:HB]), m[HB:]).astype(BF)
        zu = pick(zj, jnp.zeros_like(zj)).astype(BF)
        r.rgs[j] = dot_nt(zu, ccb[j]).astype(BF)
    kgs = r.kgs
    kgs[...] = jnp.zeros_like(kgs)
    for lag in range(3):
        kgs[lag : lag + 1, :] = jnp.sum(extg[0:N, :] * ext[8 - lag : 8 - lag + N, :], axis=0, keepdims=True)

    rc(extg.at[pl.ds(N, 8)], extg.at[pl.ds(N, 8)], r.h_s.at[1], r.h_r.at[1], s, c).wait_recv()

    @pl.when(g == NG - 1)
    def _():
        extg[N : N + 8, :] = jnp.zeros((8, W2), F32)

    gpb = r.gpb
    for j in range(Y):
        at = j * BLK
        gpb[j] = (
            k0 * extg[at : at + BLK, :] + k1 * extg[at + 1 : at + 1 + BLK, :] + k2 * extg[at + 2 : at + 2 + BLK, :]
        ).astype(BF)

    wgs, wgx, zsend, zland = r.wgs, r.wgx, r.zsend, r.zland
    z_order = list(reversed(by_distance(Z))) + [0]
    for k in z_order:
        to = lax.rem(z + k, Z)
        wgs[to] = dot(tokt[to], gpb[...].reshape(N, W2)).astype(BF).reshape(X, RB, W2)
        for kx in (2, 1, 3):
            tox = lax.rem(x + kx, X)
            go(rc(wgs.at[to, tox], wgx.at[to, x], r.wx_s.at[to, tox], r.wx_r.at[to, x], dev(z * X + tox, y), c))
        wgx[to, x] = wgs[to, x]

    tgs, tgl, tgy, tgr = r.tgs, r.tgl, r.tgy, r.tgr
    w_sib = wbuf[pl.ds(sib * half, half)].reshape(chans, W2)
    for k in (2, 1, 3, 0):
        of = lax.rem(y + k, Y)
        tgs[of] = dot_nt(gpb[of], w_sib).astype(BF)
        go(rc(tgs.at[of], tgl.at[of], r.tgs_s.at[of], r.tgs_r.at[of], s, sib))

    y_send(lambda to: r.mmsg.at[to], r.mland, r.mm_s, r.mm_r)
    r.mland[y] = r.mmsg[y]
    y_send(lambda to: r.rgs.at[to], r.rgl, r.rg_s, r.rg_r)
    r.rgl[y] = r.rgs[y]
    for k in (2, 1, 3):
        to = lax.rem(x + k, X)
        go(rc(kgs, r.kgx.at[x], r.kx_s.at[to], r.kx_r.at[x], dev(z * X + to, y), c))
    r.kgx[x] = kgs[...]

    w_own = wbuf[pl.ds(c * half, half)].reshape(chans, W2)
    for k in (2, 1, 3, 0):
        of = lax.rem(y + k, Y)
        part = dot_nt(gpb[of], w_own)
        rc(tgl.at[of], tgl.at[of], r.tgs_s.at[of], r.tgs_r.at[of], s, c).wait_recv()
        tgy[of] = (part + tgl[of].astype(F32)).astype(BF)
        if k:
            go(rc(tgy.at[of], tgr.at[y], r.tg_s.at[of], r.tg_r.at[y], dev(g, of), c))
    tgr[y] = tgy[y]

    for k in (1, 3, 2):
        of = lax.rem(x + k, X)
        rc(r.kgx.at[of], r.kgx.at[of], r.kx_s.at[of], r.kx_r.at[of], s, c).wait_recv()
    kgz = r.kgz
    kgz_own = r.kgz_own
    kgz_own[...] = (r.kgx[0] + r.kgx[1]) + (r.kgx[2] + r.kgx[3])
    for k in reversed(by_distance(Z)):
        to = lax.rem(z + k, Z)
        go(rc(kgz_own, kgz.at[z], r.kz_s.at[to], r.kz_r.at[z], dev(to * X + x, y), c))
    kgz[z] = kgz_own[...]

    for k in z_order:
        to = lax.rem(z + k, Z)
        for kx in (1, 3, 2):
            ofx = lax.rem(x + kx, X)
            rc(wgx.at[to, ofx], wgx.at[to, ofx], r.wx_s.at[to, ofx], r.wx_r.at[to, ofx], s, c).wait_recv()
        zsend[to] = y_sum(wgx[to]).astype(BF)
        if k:
            go(rc(zsend.at[to], zland.at[z], r.wz_s.at[to], r.wz_r.at[z], dev(to * X + x, y), c))
    zland[z] = zsend[z]

    y_wait(r.lgl, r.lg_s, r.lg_r)
    r.lgc[0] = y_sum(r.lgl).astype(BF)
    go(rc(r.lgc.at[0], r.lgc.at[1], r.fc_s.at[0], r.fc_r.at[0], s, sib))
    y_wait(r.rgl, r.rg_s, r.rg_r)
    r.rgc[0] = y_sum(r.rgl).astype(BF)
    go(rc(r.rgc.at[0], r.rgc.at[1], r.fc_s.at[1], r.fc_r.at[1], s, sib))

    for k in by_distance(Z):
        of = lax.rem(z + k, Z)
        rc(kgz.at[of], kgz.at[of], r.kz_s.at[of], r.kz_r.at[of], s, c).wait_recv()
    kgy = r.kgy
    total = kgz[0]
    for i in range(1, Z):
        total = total + kgz[i]
    kgy_own = r.kgy_own
    kgy_own[...] = total
    y_send(lambda to: kgy_own, kgy, r.ky_s, r.ky_r)
    kgy[y] = total

    def whole_rows(land, h):
        a, b = land[2 * h].astype(F32), land[2 * h + 1].astype(F32)
        return pick(a, swap(b)), pick(swap(a), b)

    y_wait(r.mland, r.mm_s, r.mm_r)
    for h in range(2):
        top, bottom = whole_rows(r.mland, h)
        r.mixed_out[0:HB, h * W2 : (h + 1) * W2] = top.astype(BF)
        r.mixed_out[HB:BLK, h * W2 : (h + 1) * W2] = bottom.astype(BF)

    for k in by_distance(Z):
        of = lax.rem(z + k, Z)
        rc(zland.at[of], zland.at[of], r.wz_s.at[of], r.wz_r.at[of], s, c).wait_recv()
    total = zland[0].astype(F32)
    for i in range(1, Z):
        total = total + zland[i].astype(F32)
    row = lax.broadcasted_iota(jnp.int32, (Y * 16, RB), 0)
    col = lax.broadcasted_iota(jnp.int32, (Y * 16, RB), 1)
    sel = jnp.zeros((Y * 16, RB), F32)
    for a in range(Y):
        hit = (col >= R * a) & (col < R * (a + 1)) & (row - col == (16 - R) * a)
        sel = jnp.where(hit, 1.0, sel)
    r.ymsg[...] = dot(sel.astype(BF), total.astype(BF)).astype(BF).reshape(Y, 16, W2)
    y_send(lambda to: r.ymsg.at[to], r.yland, r.wb_s, r.wb_r)
    r.yland[y] = r.ymsg[y]

    y_wait(tgr, r.tg_s, r.tg_r)
    r.tg_out[...] = y_sum(tgr).astype(BF)
    rc(r.lgc.at[1], r.lgc.at[1], r.fc_s.at[0], r.fc_r.at[0], s, c).wait_recv()
    r.lg_out[0] = r.lgc[0].astype(F32) + r.lgc[1].astype(F32)
    rc(r.rgc.at[1], r.rgc.at[1], r.fc_s.at[1], r.fc_r.at[1], s, c).wait_recv()
    r.rg_out[0] = r.rgc[0].astype(F32) + r.rgc[1].astype(F32)

    y_wait(kgy, r.ky_s, r.ky_r)
    for h in range(2):
        u, v = whole_rows(kgy, h)
        r.cug_out[:, h * W2 : (h + 1) * W2] = u[0:3]
        r.cvg_out[:, h * W2 : (h + 1) * W2] = v[0:3]

    y_wait(r.yland, r.wb_s, r.wb_r)
    for h in range(2):
        u, v = whole_rows(r.yland, h)
        r.pug_out[:, h * W2 : (h + 1) * W2] = u[0:R]
        r.pvg_out[:, h * W2 : (h + 1) * W2] = v[0:R]

    for copy in pending:
        copy.wait_send()
    exchange_sent(r.a1s, r.a1_s)
    exchange_sent(r.a2s, r.a2_s)


def layer(Z, X, tokens, cotangent, proj_u, proj_v, right_factor, left_factor, conv_u, conv_v):
    BLK, chans = tokens.shape
    R = proj_u.shape[0]
    NG = Z * X
    W2 = chans // 2
    HB = BLK // 2
    N = Y * BLK
    RB = Y * R
    ins = dict(
        tok_in=tokens,
        cot_in=cotangent,
        pu_in=proj_u,
        pv_in=proj_v,
        rf_in=right_factor,
        lf_in=left_factor,
        cu_in=conv_u,
        cv_in=conv_v,
    )
    shape = jax.ShapeDtypeStruct
    outs = dict(
        mixed_out=shape(tokens.shape, BF),
        tg_out=shape(tokens.shape, BF),
        pug_out=shape(proj_u.shape, F32),
        pvg_out=shape(proj_v.shape, F32),
        rg_out=shape(right_factor.shape, F32),
        lg_out=shape(left_factor.shape, F32),
        cug_out=shape(conv_u.shape, F32),
        cvg_out=shape(conv_v.shape, F32),
    )
    scratch = dict(
        wpad=((2, 16, chans), F32),
        wmsg=((Y, 16, W2), BF),
        wland=((Y, 16, W2), BF),
        cmsg=((Y, HB, W2), BF),
        cland=((Y, HB, W2), BF),
        tokbuf=((2, Y, BLK, chans), BF),
        rbuf=((Y, BLK, BLK), BF),
        lbuf=((Y, BLK, BLK), BF),
        rt=((Y, BLK, BLK), BF),
        lt=((Y, BLK, BLK), BF),
        wbuf=((Z, X, RB, W2), BF),
        to_msg1=((N, N), BF),
        from_msg1=((N, N), BF),
        to_msg2=((N, N), BF),
        from_msg2=((N, N), BF),
        kpad=((2, 8, chans), F32),
        cot2=((N, W2), F32),
        ext=((N + 8, W2), F32),
        extg=((N + 8, W2), F32),
        cvs=((N, W2), F32),
        zs=((N, W2), F32),
        ccb=((Y, BLK, W2), BF),
        gpb=((Y, BLK, W2), BF),
        vb=((N, W2), BF),
        xb=((N, W2), BF),
        a1s=((NG, 16, W2), BF),
        a1r=((NG, 16, W2), BF),
        a2s=((NG, 16, W2), BF),
        a2r=((NG, 16, W2), BF),
        tokt=((Z, X * RB, N), BF),
        lgs=((Y, BLK, BLK), BF),
        lgl=((Y, BLK, BLK), BF),
        lgc=((2, BLK, BLK), BF),
        rgs=((Y, BLK, BLK), BF),
        rgl=((Y, BLK, BLK), BF),
        rgc=((2, BLK, BLK), BF),
        mmsg=((Y, HB, W2), BF),
        mland=((Y, HB, W2), BF),
        kgs=((8, W2), F32),
        kgx=((X, 8, W2), F32),
        kgz_own=((8, W2), F32),
        kgz=((Z, 8, W2), F32),
        kgy_own=((8, W2), F32),
        kgy=((Y, 8, W2), F32),
        tgs=((Y, BLK, chans), BF),
        tgl=((Y, BLK, chans), BF),
        tgy=((Y, BLK, chans), BF),
        tgr=((Y, BLK, chans), BF),
        wgs=((Z, X, RB, W2), BF),
        wgx=((Z, X, RB, W2), BF),
        zsend=((Z, RB, W2), BF),
        zland=((Z, RB, W2), BF),
        ymsg=((Y, 16, W2), BF),
        yland=((Y, 16, W2), BF),
    )
    sems = dict(
        tok_r=(2, Y),
        ts_s=(Y,),
        ty_s=(Y,),
        gz_s=(Z,),
        gx_s=(Z, X),
        g_r=(Z, X),
        h_s=(2,),
        h_r=(2,),
        kx_s=(X,),
        kx_r=(X,),
        kz_s=(Z,),
        kz_r=(Z,),
        wx_s=(Z, X),
        wx_r=(Z, X),
        wz_s=(Z,),
        wz_r=(Z,),
        tgs_s=(Y,),
        tgs_r=(Y,),
        fc_s=(2,),
        fc_r=(2,),
        wy_s=(Y,),
        wy_r=(Y,),
        rf_s=(Y,),
        rf_r=(Y,),
        cy_s=(Y,),
        cy_r=(Y,),
        lf_s=(Y,),
        lf_r=(Y,),
        lg_s=(Y,),
        lg_r=(Y,),
        rg_s=(Y,),
        rg_r=(Y,),
        mm_s=(Y,),
        mm_r=(Y,),
        ky_s=(Y,),
        ky_r=(Y,),
        tg_s=(Y,),
        tg_r=(Y,),
        wb_s=(Y,),
        wb_r=(Y,),
        a1_s=(NG,),
        a1_r=(NG,),
        a2_s=(NG,),
        a2_r=(NG,),
    )
    names = list(ins) + list(outs) + list(scratch) + list(sems)

    def body(*refs):
        kernel(Z, X, types.SimpleNamespace(**dict(zip(names, refs))))

    vmem = pl.BlockSpec(memory_space=pltpu.VMEM)
    return pl.pallas_call(
        body,
        out_shape=list(outs.values()),
        in_specs=[vmem] * len(ins),
        out_specs=[vmem] * len(outs),
        scratch_shapes=[pltpu.VMEM(sh, dt) for sh, dt in scratch.values()]
        + [pltpu.SemaphoreType.DMA(sh) for sh in sems.values()],
        compiler_params=pltpu.CompilerParams(
            collective_id=0, has_side_effects=True, vmem_limit_bytes=48 * 1024 * 1024
        ),
    )(*ins.values())


def solution(mesh):
    groups = mesh.shape["seq"] // Y
    specs = (
        P("seq", "ch"),
        P("seq", "ch"),
        P("seq", "ch"),
        P("seq", "ch"),
        P("seq", None, None),
        P("seq", None, None),
        P(None, "ch"),
        P(None, "ch"),
    )
    return jax.shard_map(
        functools.partial(layer, groups // X, X),
        mesh=mesh,
        in_specs=specs,
        out_specs=specs,
        check_vma=False,
    )
```

```python
import functools
import types

import jax
import jax.numpy as jnp
from jax import lax
from jax.experimental import pallas as pl
from jax.experimental.pallas import tpu as pltpu
from jax.sharding import PartitionSpec as P

MESH = pl.DeviceIdType.MESH
BF = jnp.bfloat16
F32 = jnp.float32
Y = 4
X = 4
T = 3


def dot(a, b):
    return jnp.dot(a, b, preferred_element_type=F32)


def dot_nt(a, b):
    return lax.dot_general(a, b, (((1,), (1,)), ((), ())), preferred_element_type=F32)


def transposed(a):
    return a.astype(F32).T.astype(BF)


def by_distance(n):
    return sorted(range(1, n), key=lambda k: (min(k, n - k), k))


def kernel(Z, X, r):
    NG = Z * X
    BLK, chans = r.tok_in.shape
    HC = chans // (Y * T)
    CW = 2 * HC
    HB = BLK // 2
    N = Y * BLK
    R = r.pu_in.shape[0]
    RB = Y * R
    half = Z // 2

    s = lax.axis_index("seq")
    c = lax.axis_index("ch")
    g = s // Y
    y = lax.rem(s, Y)
    z = g // X
    x = lax.rem(g, X)
    sib = 1 - c

    def dev(gg, yy):
        return gg * Y + yy

    def in_u(shape):
        return lax.broadcasted_iota(jnp.int32, shape, len(shape) - 1) < HC

    def pick(u, v):
        return jnp.where(in_u(u.shape), u, v)

    def swap(v):
        return pltpu.roll(v, HC, 1)

    def rc(src, dst, send_sem, recv_sem, seq, ch):
        return pltpu.make_async_remote_copy(
            src_ref=src,
            dst_ref=dst,
            send_sem=send_sem,
            recv_sem=recv_sem,
            device_id=(seq, ch),
            device_id_type=MESH,
        )

    def got(ref, sem):
        rc(ref, ref, sem, sem, s, c).wait_recv()

    def sent(ref, sem):
        rc(ref, ref, sem, sem, s, c).wait_send()

    def part(u, v, yy, t):
        q = yy * T + t
        uq = u[:, q // 2 * CW : (q // 2 + 1) * CW]
        vq = v[:, q // 2 * CW : (q // 2 + 1) * CW]
        return pick(uq, swap(vq)) if q % 2 == 0 else pick(swap(uq), vq)

    def whole(land, tile):
        q = 2 * tile
        a = land(q // T, q % T).astype(F32)
        b = land((q + 1) // T, (q + 1) % T).astype(F32)
        return pick(a, swap(b)), pick(swap(a), b)

    def y_send(src_of, dst, send, recv):
        for k in (2, 1, 3):
            to = lax.rem(y + k, Y)
            rc(src_of(to), dst.at[y], send.at[0], recv.at[0], dev(g, to), c).start()

    def y_got(dst, recv):
        got(dst.at[pl.ds(0, Y - 1)], recv.at[0])

    def y_sent(like, send):
        sent(like.at[pl.ds(0, Y - 1)], send.at[0])

    barrier = pltpu.get_barrier_semaphore()

    def greet(k, carry):
        pl.semaphore_signal(
            barrier, inc=1, device_id=(dev(lax.rem(g + k, NG), y), c), device_id_type=MESH
        )
        return carry

    for k in (1, 2, 3):
        pl.semaphore_signal(
            barrier, inc=1, device_id=(dev(g, lax.rem(y + k, Y)), c), device_id_type=MESH
        )
    pl.semaphore_signal(barrier, inc=1, device_id=(s, sib), device_id_type=MESH)
    lax.fori_loop(1, NG, greet, 0)

    def load(src, dst, i):
        copy = pltpu.make_async_copy(src, dst, r.in_s.at[i])
        copy.start()
        return copy

    tokbuf = r.tokbuf
    in_pu = load(r.pu_in, r.pu, 0)
    in_pv = load(r.pv_in, r.pv, 1)
    in_tok = load(r.tok_in, tokbuf.at[c, y], 2)
    in_cot = load(r.cot_in, r.cot, 3)
    in_cu = load(r.cu_in, r.cu, 4)
    in_cv = load(r.cv_in, r.cv, 5)
    in_factors = [
        load(a.at[0, pl.ds(h * HB, HB)], b.at[y, h], 6 + 2 * i + h)
        for i, (a, b) in enumerate(((r.rf_in, r.rbuf), (r.lf_in, r.lbuf)))
        for h in range(2)
    ]

    wpad = r.wpad
    wpad[...] = jnp.zeros_like(wpad)
    kpad = r.kpad
    kpad[...] = jnp.zeros_like(kpad)
    in_pu.wait()
    in_pv.wait()
    wpad[0, 0:R, :] = r.pu[...].astype(F32)
    wpad[1, 0:R, :] = r.pv[...].astype(F32)
    for yy in range(Y):
        for t in range(T):
            r.wmsg[yy, t] = part(wpad[0], wpad[1], yy, t).astype(BF)
    in_tok.wait()
    in_cot.wait()
    cot = r.cot[...].astype(F32)
    for yy in range(Y):
        for t in range(T):
            r.cmsg[yy, t] = part(cot[:HB], cot[HB:], yy, t).astype(BF)
    for copy in in_factors:
        copy.wait()

    out_i = lax.broadcasted_iota(jnp.int32, (N, N), 0)
    in_i = lax.broadcasted_iota(jnp.int32, (N, N), 1)

    def hits(a, b):
        return jnp.where(a == b, 1.0, 0.0).astype(BF)

    def swapped_index(v):
        return lax.rem(v // 4, 4) * BLK + (v // 16) * 4 + lax.rem(v, 4)

    def rotated_index(v):
        return lax.rem(v, 4) * BLK + (v // 16) * 4 + lax.rem(v // 4, 4)

    r.to_msg1[...] = hits(in_i, rotated_index(out_i))
    r.from_msg1[...] = hits(out_i, swapped_index(in_i))
    r.to_msg2[...] = hits(in_i, swapped_index(out_i))
    r.from_msg2[...] = hits(out_i, rotated_index(in_i))

    in_cu.wait()
    in_cv.wait()
    kpad[0, 0:3, :] = r.cu[...]
    kpad[1, 0:3, :] = r.cv[...]
    for t in range(T):
        kt = part(kpad[0], kpad[1], 0, t)
        for yy in range(1, Y):
            kt = jnp.where(y == yy, part(kpad[0], kpad[1], yy, t), kt)
        r.kk[t] = kt

    def conv(t, first, second, third):
        return r.kk[t, 0:1] * first + r.kk[t, 1:2] * second + r.kk[t, 2:3] * third

    row = lax.broadcasted_iota(jnp.int32, (RB, Y * 16), 0)
    col = lax.broadcasted_iota(jnp.int32, (RB, Y * 16), 1)
    sel = jnp.zeros((RB, Y * 16), F32)
    for a in range(Y):
        hit = (row >= R * a) & (row < R * (a + 1)) & (col - row == (16 - R) * a)
        sel = jnp.where(hit, 1.0, sel)
    sel = sel.astype(BF)

    pl.semaphore_wait(barrier, NG - 1 + Y)

    y_send(lambda to: r.wmsg.at[to], r.wland, r.wy_s, r.wy_r)
    rc(tokbuf.at[c, y], tokbuf.at[c, y], r.ts_s.at[0], r.ts_r.at[0], s, sib).start()
    for k in (2, 1, 3):
        to = lax.rem(y + k, Y)
        rc(tokbuf.at[c, y], tokbuf.at[c, y], r.ty_s.at[0], r.ty_r.at[y], dev(g, to), c).start()
    y_send(lambda to: r.cmsg.at[to], r.cland, r.cy_s, r.cy_r)

    def factor_send(buf, send, recv):
        for k in (2, 1, 3):
            to = lax.rem(y + k, Y)
            rc(buf.at[y, c], buf.at[y, c], send.at[0], recv.at[0], dev(g, to), c).start()

    def factor_hand_on(buf, send, recv):
        got(buf.at[pl.ds(0, Y - 1), 0], recv.at[0])
        for k in (1, 3, 2):
            of = lax.rem(y + k, Y)
            rc(buf.at[of, c], buf.at[of, c], send.at[1], recv.at[1], s, sib).start()

    def factor(buf, recv):
        got(buf.at[pl.ds(0, Y - 1), 0], recv.at[1])
        return [buf[j].reshape(BLK, BLK) for j in range(Y)]

    factor_send(r.rbuf, r.rf_s, r.rf_r)
    factor_send(r.lbuf, r.lf_s, r.lf_r)
    r.wland[y] = r.wmsg[y]
    r.cland[y] = r.cmsg[y]

    wbuf = r.wbuf
    y_got(r.wland, r.wy_r)
    for t in range(T):
        wbuf[t, z, x] = dot(sel, r.wland[:, t].reshape(Y * 16, CW)).astype(BF)
        for k in reversed(by_distance(Z)):
            to = lax.rem(z + k, Z)
            block = wbuf.at[t, z, x]
            rc(block, block, r.gz_s.at[t], r.gz_r.at[t, z], dev(to * X + x, y), c).start()

    def along_x(t, of):
        for k in (2, 1, 3):
            to = lax.rem(x + k, X)
            block = wbuf.at[t, of, x]
            rc(block, block, r.gx_s.at[t], r.gx_r.at[t, x], dev(z * X + to, y), c).start()

    def gather_x(t):
        along_x(t, z)
        for k in by_distance(Z):
            of = lax.rem(z + k, Z)
            got(wbuf.at[t, of, x], r.gz_r.at[t, of])
            along_x(t, of)

    ext, cvs, ccb, vb, xb = r.ext, r.cvs, r.ccb, r.vb, r.xb
    cot2, extg, zs, gpb = r.cot2, r.extg, r.zs, r.gpb

    def project(t):
        for k in (1, 3, 2):
            of = lax.rem(x + k, X)
            got(wbuf.at[t, :, of], r.gx_r.at[t, of])
        pre = dot(tokbuf[0].reshape(N, chans), wbuf[t, 0:half].reshape(chans, CW))
        pre = pre + dot(tokbuf[1].reshape(N, chans), wbuf[t, half:].reshape(chans, CW))
        ext[t, 8 : 8 + N, :] = pre.astype(BF).astype(F32)
        rc(ext.at[t, pl.ds(N, 8)], ext.at[t, pl.ds(0, 8)], r.h_s.at[t], r.h_r.at[t], dev(lax.rem(g + 1, NG), y), c).start()

    def exchange(src, dst, send, recv):
        def start(k, carry):
            to = lax.rem(g + k, NG)
            rc(src.at[to], dst.at[g], send, recv, dev(to, y), c).start()
            return carry

        lax.fori_loop(1, NG, start, 0)
        dst[g] = src[g]

    def mix_rows(t):
        got(ext.at[t, pl.ds(0, 8)], r.h_r.at[t])

        @pl.when(g == 0)
        def _():
            ext[t, 0:8, :] = jnp.zeros((8, CW), F32)

        for j in range(Y):
            at = j * BLK
            cv = conv(
                t,
                ext[t, 8 + at : 8 + at + BLK, :],
                ext[t, 7 + at : 7 + at + BLK, :],
                ext[t, 6 + at : 6 + at + BLK, :],
            )
            cvs[t, at : at + BLK, :] = cv
            cb = cv.astype(BF)
            ccb[t, j] = cb
            vb[at : at + BLK, :] = pick(dot(r.rbuf[j].reshape(BLK, BLK), cb), cot2[t, at : at + BLK, :] * cv).astype(BF)
        r.a1s[t] = dot(r.to_msg1[...], vb[...]).astype(BF).reshape(NG, 16, CW)
        exchange(r.a1s.at[t], r.a1r.at[t], r.a1_s.at[t], r.a1_r.at[t])

    def mix_columns(t):
        got(r.a1r.at[t, pl.ds(0, NG - 1)], r.a1_r.at[t])
        xb[t] = dot(r.from_msg1[...], r.a1r[t].reshape(N, CW)).astype(BF)
        for i in range(Y):
            xi = xb[t, i * BLK : (i + 1) * BLK, :]
            vb[i * BLK : (i + 1) * BLK, :] = pick(dot(r.lbuf[i].reshape(BLK, BLK), xi), dot(r.lt[i], xi)).astype(BF)
        r.a2s[t] = dot(r.to_msg2[...], vb[...]).astype(BF).reshape(NG, 16, CW)
        exchange(r.a2s.at[t], r.a2r.at[t], r.a2_s.at[t], r.a2_r.at[t])

    def back_rows(t):
        got(r.a2r.at[t, pl.ds(0, NG - 1)], r.a2_r.at[t])
        zs[t] = swap(dot(r.from_msg2[...], r.a2r[t].reshape(N, CW)))
        for j in range(Y):
            at = j * BLK
            zj = zs[t, at : at + BLK, :]
            extg[t, at : at + BLK, :] = pick(dot(r.rt[j], zj.astype(BF)), cot2[t, at : at + BLK, :] * zj)
            m = cvs[t, at : at + BLK, :] * zj
            r.mmsg[t, j] = pick(swap(m[:HB]), m[HB:]).astype(BF)
        rc(extg.at[t, pl.ds(0, 8)], extg.at[t, pl.ds(N, 8)], r.h_s.at[T + t], r.h_r.at[T + t], dev(lax.rem(g + NG - 1, NG), y), c).start()
        for k in (2, 1, 3):
            to = lax.rem(y + k, Y)
            rc(r.mmsg.at[t, to], r.mland.at[t, y], r.mm_s.at[t], r.mm_r.at[t], dev(g, to), c).start()
        r.mland[t, y] = r.mmsg[t, y]

    wgs, wgx, zsend, zland = r.wgs, r.wgx, r.zsend, r.zland
    z_order = list(reversed(by_distance(Z))) + [0]

    def weight_grads(t):
        got(extg.at[t, pl.ds(N, 8)], r.h_r.at[T + t])

        @pl.when(g == NG - 1)
        def _():
            extg[t, N : N + 8, :] = jnp.zeros((8, CW), F32)

        for j in range(Y):
            at = j * BLK
            gpb[t, j] = conv(
                t,
                extg[t, at : at + BLK, :],
                extg[t, at + 1 : at + 1 + BLK, :],
                extg[t, at + 2 : at + 2 + BLK, :],
            ).astype(BF)
        gp = gpb[t].reshape(N, CW)
        for k in z_order:
            to = lax.rem(z + k, Z)
            wgs[t, to] = dot(r.tokt[to], gp).astype(BF).reshape(X, RB, CW)
            for kx in (2, 1, 3):
                tox = lax.rem(x + kx, X)
                rc(wgs.at[t, to, tox], wgx.at[t, to, x], r.wx_s.at[t], r.wx_r.at[t, to], dev(z * X + tox, y), c).start()
            wgx[t, to, x] = wgs[t, to, x]

    def sum4(land):
        return (land[0].astype(F32) + land[1].astype(F32)) + (land[2].astype(F32) + land[3].astype(F32))

    def weight_sums(t):
        for k in z_order:
            to = lax.rem(z + k, Z)
            got(wgx.at[t, to, pl.ds(0, X - 1)], r.wx_r.at[t, to])
            zsend[t, to] = sum4(wgx[t, to]).astype(BF)
            if k:
                rc(zsend.at[t, to], zland.at[t, z], r.wz_s.at[t], r.wz_r.at[t], dev(to * X + x, y), c).start()
        zland[t, z] = zsend[t, z]

    def left_grads():
        for i in range(Y):
            grads, cols = [], []
            for t in range(T):
                xi = xb[t, i * BLK : (i + 1) * BLK, :]
                xs = swap(xi.astype(F32))
                grads.append(pick(xs, jnp.zeros_like(xs)).astype(BF))
                cols.append(xi)
            r.lgs[i] = dot_nt(jnp.concatenate(grads, axis=1), jnp.concatenate(cols, axis=1)).astype(BF)
        y_send(lambda to: r.lgs.at[to], r.lgl, r.lg_s, r.lg_r)
        r.lgl[y] = r.lgs[y]

    def right_grads():
        for j in range(Y):
            rows = []
            for t in range(T):
                zj = zs[t, j * BLK : (j + 1) * BLK, :]
                rows.append(pick(zj, jnp.zeros_like(zj)).astype(BF))
            r.rgs[j] = dot_nt(
                jnp.concatenate(rows, axis=1), jnp.concatenate([ccb[t, j] for t in range(T)], axis=1)
            ).astype(BF)
        y_send(lambda to: r.rgs.at[to], r.rgl, r.rg_s, r.rg_r)
        r.rgl[y] = r.rgs[y]

    kgs = r.kgs

    def conv_grads():
        kgs[...] = jnp.zeros_like(kgs)
        for t in range(T):
            for lag in range(3):
                kgs[t, lag : lag + 1, :] = jnp.sum(
                    extg[t, 0:N, :] * ext[t, 8 - lag : 8 - lag + N, :], axis=0, keepdims=True
                )
        for k in (2, 1, 3):
            to = lax.rem(x + k, X)
            rc(kgs, r.kgx.at[x], r.kx_s.at[0], r.kx_r.at[0], dev(z * X + to, y), c).start()
        r.kgx[x] = kgs[...]

    gather_x(0)
    for k in (1, 3, 2):
        of = lax.rem(y + k, Y)
        block = tokbuf.at[c, of]
        got(block, r.ty_r.at[of])
        rc(block, block, r.ts_s.at[0], r.ts_r.at[0], s, sib).start()
    gather_x(1)
    gather_x(2)
    got(tokbuf.at[0], r.ts_r.at[0])
    project(0)
    project(1)
    y_got(r.cland, r.cy_r)
    for t in range(T):
        for j in range(Y):
            m = r.cland[j, t].astype(F32)
            cot2[t, j * BLK : j * BLK + HB, :] = swap(m)
            cot2[t, j * BLK + HB : (j + 1) * BLK, :] = m
    factor_hand_on(r.rbuf, r.rf_s, r.rf_r)
    factor_hand_on(r.lbuf, r.lf_s, r.lf_r)
    project(2)
    right = factor(r.rbuf, r.rf_r)
    mix_rows(0)
    mix_rows(1)
    mix_rows(2)
    left = factor(r.lbuf, r.lf_r)
    for j in range(Y):
        r.rt[j] = transposed(right[j])
        r.lt[j] = transposed(left[j])
    for i in range(2):
        r.tokt[i * half : (i + 1) * half] = transposed(tokbuf[i].reshape(N, chans)).reshape(half, X * RB, N)
    mix_columns(0)
    mix_columns(1)
    mix_columns(2)
    left_grads()
    back_rows(0)
    back_rows(1)
    weight_grads(0)
    back_rows(2)
    weight_grads(1)
    right_grads()
    conv_grads()
    weight_grads(2)

    tgs, tgl, tgy, tgr = r.tgs, r.tgl, r.tgy, r.tgr

    def rows_of(ref, at):
        return jnp.concatenate([ref[t, at] for t in range(T)], axis=1)

    def half_of(cc):
        return jnp.concatenate(
            [wbuf[t, pl.ds(cc * half, half)].reshape(chans, CW) for t in range(T)], axis=1
        )

    w_sib = half_of(sib)
    for k in (2, 1, 3, 0):
        of = lax.rem(y + k, Y)
        tgs[of] = dot_nt(rows_of(gpb, of), w_sib).astype(BF)
        rc(tgs.at[of], tgl.at[of], r.tgs_s.at[0], r.tgs_r.at[of], s, sib).start()
    weight_sums(0)
    weight_sums(1)
    w_own = half_of(c)
    for k in (2, 1, 3, 0):
        of = lax.rem(y + k, Y)
        own = dot_nt(rows_of(gpb, of), w_own)
        got(tgl.at[of], r.tgs_r.at[of])
        tgy[of] = (own + tgl[of].astype(F32)).astype(BF)
        if k:
            rc(tgy.at[of], tgr.at[y], r.tg_s.at[0], r.tg_r.at[0], dev(g, of), c).start()
    tgr[y] = tgy[y]

    weight_sums(2)

    got(r.kgx.at[pl.ds(0, X - 1)], r.kx_r.at[0])
    kgz, kgz_own = r.kgz, r.kgz_own
    kgz_own[...] = sum4(r.kgx)
    for k in reversed(by_distance(Z)):
        to = lax.rem(z + k, Z)
        rc(kgz_own, kgz.at[z], r.kz_s.at[0], r.kz_r.at[0], dev(to * X + x, y), c).start()
    kgz[z] = kgz_own[...]

    y_got(r.rgl, r.rg_r)
    r.rgc[0] = sum4(r.rgl).astype(BF)
    rc(r.rgc.at[0], r.rgc.at[1], r.fc_s.at[0], r.fc_r.at[0], s, sib).start()
    y_got(r.lgl, r.lg_r)
    r.lgc[0] = sum4(r.lgl).astype(BF)
    rc(r.lgc.at[0], r.lgc.at[1], r.fc_s.at[1], r.fc_r.at[1], s, sib).start()

    for t in range(T):
        got(r.mland.at[t, pl.ds(0, Y - 1)], r.mm_r.at[t])
    for tile in range(Y * T // 2):
        top, bottom = whole(lambda yy, t: r.mland[t, yy], tile)
        r.mixed_out[0:HB, tile * CW : (tile + 1) * CW] = top.astype(BF)
        r.mixed_out[HB:BLK, tile * CW : (tile + 1) * CW] = bottom.astype(BF)

    row = lax.broadcasted_iota(jnp.int32, (Y * 16, RB), 0)
    col = lax.broadcasted_iota(jnp.int32, (Y * 16, RB), 1)
    spread = jnp.zeros((Y * 16, RB), F32)
    for a in range(Y):
        hit = (col >= R * a) & (col < R * (a + 1)) & (row - col == (16 - R) * a)
        spread = jnp.where(hit, 1.0, spread)
    spread = spread.astype(BF)
    for t in range(T):
        got(zland.at[t, pl.ds(0, Z - 1)], r.wz_r.at[t])
        total = zland[t, 0].astype(F32)
        for i in range(1, Z):
            total = total + zland[t, i].astype(F32)
        r.ymsg[:, t] = dot(spread, total.astype(BF)).astype(BF).reshape(Y, 16, CW)
    y_send(lambda to: r.ymsg.at[to], r.yland, r.wb_s, r.wb_r)
    r.yland[y] = r.ymsg[y]

    got(kgz.at[pl.ds(0, Z - 1)], r.kz_r.at[0])
    kgy, kgy_own = r.kgy, r.kgy_own
    total = kgz[0]
    for i in range(1, Z):
        total = total + kgz[i]
    kgy_own[...] = total
    y_send(lambda to: kgy_own, kgy, r.ky_s, r.ky_r)
    kgy[y] = total

    sent(tokbuf.at[0], r.ts_s.at[0])
    y_sent(tokbuf.at[0], r.ty_s)
    y_sent(r.wmsg, r.wy_s)
    for i in range(2):
        sent(r.rbuf.at[pl.ds(0, Y - 1), 0], r.rf_s.at[i])
        sent(r.lbuf.at[pl.ds(0, Y - 1), 0], r.lf_s.at[i])
    y_sent(r.cmsg, r.cy_s)
    for t in range(T):
        sent(wbuf.at[t, pl.ds(0, Z - 1), 0], r.gz_s.at[t])
        for i in range(X - 1):
            sent(wbuf.at[t, :, i], r.gx_s.at[t])
        sent(ext.at[t, pl.ds(0, 8)], r.h_s.at[t])
        sent(extg.at[t, pl.ds(0, 8)], r.h_s.at[T + t])
        sent(r.a1s.at[t, pl.ds(0, NG - 1)], r.a1_s.at[t])
        sent(r.a2s.at[t, pl.ds(0, NG - 1)], r.a2_s.at[t])
        for i in range(X - 1):
            sent(wgs.at[t, :, i], r.wx_s.at[t])
        sent(zland.at[t, pl.ds(0, Z - 1)], r.wz_s.at[t])
    sent(tgs, r.tgs_s.at[0])
    y_sent(tgs, r.tg_s)
    sent(r.kgx.at[pl.ds(0, X - 1)], r.kx_s.at[0])
    sent(kgz.at[pl.ds(0, Z - 1)], r.kz_s.at[0])
    for t in range(T):
        sent(r.mmsg.at[t, pl.ds(0, Y - 1)], r.mm_s.at[t])
    y_sent(r.rgs, r.rg_s)
    y_sent(r.lgs, r.lg_s)

    got(r.rgc.at[1], r.fc_r.at[0])
    r.rg_out[0] = r.rgc[0].astype(F32) + r.rgc[1].astype(F32)
    got(r.lgc.at[1], r.fc_r.at[1])
    r.lg_out[0] = r.lgc[0].astype(F32) + r.lgc[1].astype(F32)
    y_got(tgr, r.tg_r)
    r.tg_out[...] = sum4(tgr).astype(BF)
    y_got(r.yland, r.wb_r)
    for tile in range(Y * T // 2):
        u, v = whole(lambda yy, t: r.yland[yy, t], tile)
        r.pug_out[:, tile * CW : (tile + 1) * CW] = u[0:R]
        r.pvg_out[:, tile * CW : (tile + 1) * CW] = v[0:R]
    y_got(kgy, r.ky_r)
    for tile in range(Y * T // 2):
        u, v = whole(lambda yy, t: kgy[yy, t], tile)
        r.cug_out[:, tile * CW : (tile + 1) * CW] = u[0:3]
        r.cvg_out[:, tile * CW : (tile + 1) * CW] = v[0:3]
    for i in range(2):
        sent(r.rgc.at[0], r.fc_s.at[i])
    y_sent(r.ymsg, r.wb_s)
    y_sent(kgy, r.ky_s)


def layer(Z, X, tokens, cotangent, proj_u, proj_v, right_factor, left_factor, conv_u, conv_v):
    BLK, chans = tokens.shape
    R = proj_u.shape[0]
    NG = Z * X
    CW = 2 * (chans // (Y * T))
    HB = BLK // 2
    N = Y * BLK
    RB = Y * R
    ins = dict(
        tok_in=tokens,
        cot_in=cotangent,
        pu_in=proj_u,
        pv_in=proj_v,
        rf_in=right_factor,
        lf_in=left_factor,
        cu_in=conv_u,
        cv_in=conv_v,
    )
    shape = jax.ShapeDtypeStruct
    outs = dict(
        mixed_out=shape(tokens.shape, BF),
        tg_out=shape(tokens.shape, BF),
        pug_out=shape(proj_u.shape, F32),
        pvg_out=shape(proj_v.shape, F32),
        rg_out=shape(right_factor.shape, F32),
        lg_out=shape(left_factor.shape, F32),
        cug_out=shape(conv_u.shape, F32),
        cvg_out=shape(conv_v.shape, F32),
    )
    scratch = dict(
        pu=(proj_u.shape, BF),
        pv=(proj_v.shape, BF),
        cot=(cotangent.shape, BF),
        cu=(conv_u.shape, F32),
        cv=(conv_v.shape, F32),
        wpad=((2, 16, chans), F32),
        kpad=((2, 8, chans), F32),
        kk=((T, 8, CW), F32),
        wmsg=((Y, T, 16, CW), BF),
        wland=((Y, T, 16, CW), BF),
        cmsg=((Y, T, HB, CW), BF),
        cland=((Y, T, HB, CW), BF),
        tokbuf=((2, Y, BLK, chans), BF),
        rbuf=((Y, 2, HB, BLK), BF),
        lbuf=((Y, 2, HB, BLK), BF),
        rt=((Y, BLK, BLK), BF),
        lt=((Y, BLK, BLK), BF),
        wbuf=((T, Z, X, RB, CW), BF),
        to_msg1=((N, N), BF),
        from_msg1=((N, N), BF),
        to_msg2=((N, N), BF),
        from_msg2=((N, N), BF),
        cot2=((T, N, CW), F32),
        ext=((T, N + 8, CW), F32),
        extg=((T, N + 8, CW), F32),
        cvs=((T, N, CW), F32),
        zs=((T, N, CW), F32),
        ccb=((T, Y, BLK, CW), BF),
        gpb=((T, Y, BLK, CW), BF),
        vb=((N, CW), BF),
        xb=((T, N, CW), BF),
        a1s=((T, NG, 16, CW), BF),
        a1r=((T, NG, 16, CW), BF),
        a2s=((T, NG, 16, CW), BF),
        a2r=((T, NG, 16, CW), BF),
        tokt=((Z, X * RB, N), BF),
        lgs=((Y, BLK, BLK), BF),
        lgl=((Y, BLK, BLK), BF),
        lgc=((2, BLK, BLK), BF),
        rgs=((Y, BLK, BLK), BF),
        rgl=((Y, BLK, BLK), BF),
        rgc=((2, BLK, BLK), BF),
        mmsg=((T, Y, HB, CW), BF),
        mland=((T, Y, HB, CW), BF),
        kgs=((T, 8, CW), F32),
        kgx=((X, T, 8, CW), F32),
        kgz_own=((T, 8, CW), F32),
        kgz=((Z, T, 8, CW), F32),
        kgy_own=((T, 8, CW), F32),
        kgy=((Y, T, 8, CW), F32),
        tgs=((Y, BLK, chans), BF),
        tgl=((Y, BLK, chans), BF),
        tgy=((Y, BLK, chans), BF),
        tgr=((Y, BLK, chans), BF),
        wgs=((T, Z, X, RB, CW), BF),
        wgx=((T, Z, X, RB, CW), BF),
        zsend=((T, Z, RB, CW), BF),
        zland=((T, Z, RB, CW), BF),
        ymsg=((Y, T, 16, CW), BF),
        yland=((Y, T, 16, CW), BF),
    )
    one = (1,)
    sems = dict(
        in_s=(10,),
        ts_s=one,
        ts_r=one,
        ty_s=one,
        ty_r=(Y,),
        gz_s=(T,),
        gz_r=(T, Z),
        gx_s=(T,),
        gx_r=(T, X),
        h_s=(2 * T,),
        h_r=(2 * T,),
        a1_s=(T,),
        a1_r=(T,),
        a2_s=(T,),
        a2_r=(T,),
        wx_s=(T,),
        wx_r=(T, Z),
        wz_s=(T,),
        wz_r=(T,),
        kx_s=one,
        kx_r=one,
        kz_s=one,
        kz_r=one,
        tgs_s=one,
        tgs_r=(Y,),
        fc_s=(2,),
        fc_r=(2,),
        wy_s=one,
        wy_r=one,
        rf_s=(2,),
        rf_r=(2,),
        cy_s=one,
        cy_r=one,
        lf_s=(2,),
        lf_r=(2,),
        lg_s=one,
        lg_r=one,
        rg_s=one,
        rg_r=one,
        mm_s=(T,),
        mm_r=(T,),
        ky_s=one,
        ky_r=one,
        tg_s=one,
        tg_r=one,
        wb_s=one,
        wb_r=one,
    )
    names = list(ins) + list(outs) + list(scratch) + list(sems)

    def body(*refs):
        kernel(Z, X, types.SimpleNamespace(**dict(zip(names, refs))))

    vmem = pl.BlockSpec(memory_space=pltpu.VMEM)
    hbm = pl.BlockSpec(memory_space=pltpu.HBM)
    results = pl.pallas_call(
        body,
        out_shape=list(outs.values()),
        in_specs=[hbm] * len(ins),
        out_specs=[vmem] * len(outs),
        scratch_shapes=[pltpu.VMEM(sh, dt) for sh, dt in scratch.values()]
        + [pltpu.SemaphoreType.DMA(sh) for sh in sems.values()],
        compiler_params=pltpu.CompilerParams(
            collective_id=0, has_side_effects=True, vmem_limit_bytes=63 * 1024 * 1024
        ),
    )(*ins.values())

    count = len(outs)

    def write(*refs):
        froms, tos, held = refs[:count], refs[count : 2 * count], refs[2 * count : 3 * count]
        into, out_of = refs[3 * count :]
        first = [pltpu.make_async_copy(froms[i], held[i], into.at[i]) for i in range(count)]
        second = [pltpu.make_async_copy(held[i], tos[i], out_of.at[i]) for i in range(count)]
        for copy in first:
            copy.start()
        for before, after in zip(first, second):
            before.wait()
            after.start()
        for copy in second:
            copy.wait()

    return pl.pallas_call(
        write,
        out_shape=list(outs.values()),
        in_specs=[hbm] * count,
        out_specs=[hbm] * count,
        scratch_shapes=[pltpu.VMEM(o.shape, o.dtype) for o in outs.values()]
        + [pltpu.SemaphoreType.DMA((count,))] * 2,
    )(*results)


def solution(mesh):
    groups = mesh.shape["seq"] // Y
    specs = (
        P("seq", "ch"),
        P("seq", "ch"),
        P("seq", "ch"),
        P("seq", "ch"),
        P("seq", None, None),
        P("seq", None, None),
        P(None, "ch"),
        P(None, "ch"),
    )
    return jax.shard_map(
        functools.partial(layer, groups // X, X),
        mesh=mesh,
        in_specs=specs,
        out_specs=specs,
        check_vma=False,
    )
```

```python
import functools
import types

import jax
import jax.numpy as jnp
from jax import lax
from jax.experimental import pallas as pl
from jax.experimental.pallas import tpu as pltpu
from jax.sharding import PartitionSpec as P

MESH = pl.DeviceIdType.MESH
BF = jnp.bfloat16
F32 = jnp.float32
Y = 4
X = 4
T = 3


def dot(a, b):
    return jnp.dot(a, b, preferred_element_type=F32)


def dot_nt(a, b):
    return lax.dot_general(a, b, (((1,), (1,)), ((), ())), preferred_element_type=F32)


def transposed(a):
    return a.astype(F32).T.astype(BF)


def by_distance(n):
    return sorted(range(1, n), key=lambda k: (min(k, n - k), k))


def kernel(Z, X, r):
    NG = Z * X
    BLK, chans = r.tok_in.shape
    HC = chans // (Y * T)
    CW = 2 * HC
    HB = BLK // 2
    N = Y * BLK
    R = r.pu_in.shape[0]
    RB = Y * R
    half = Z // 2

    s = lax.axis_index("seq")
    c = lax.axis_index("ch")
    g = s // Y
    y = lax.rem(s, Y)
    z = g // X
    x = lax.rem(g, X)
    sib = 1 - c

    def dev(gg, yy):
        return gg * Y + yy

    def in_u(shape):
        return lax.broadcasted_iota(jnp.int32, shape, len(shape) - 1) < HC

    def pick(u, v):
        return jnp.where(in_u(u.shape), u, v)

    def swap(v):
        return pltpu.roll(v, HC, 1)

    def rc(src, dst, send_sem, recv_sem, seq, ch):
        return pltpu.make_async_remote_copy(
            src_ref=src,
            dst_ref=dst,
            send_sem=send_sem,
            recv_sem=recv_sem,
            device_id=(seq, ch),
            device_id_type=MESH,
        )

    def got(ref, sem):
        rc(ref, ref, sem, sem, s, c).wait_recv()

    def sent(ref, sem):
        rc(ref, ref, sem, sem, s, c).wait_send()

    def part(u, v, yy, t):
        q = yy * T + t
        uq = u[:, q // 2 * CW : (q // 2 + 1) * CW]
        vq = v[:, q // 2 * CW : (q // 2 + 1) * CW]
        return pick(uq, swap(vq)) if q % 2 == 0 else pick(swap(uq), vq)

    def whole(land, tile):
        q = 2 * tile
        a = land(q // T, q % T).astype(F32)
        b = land((q + 1) // T, (q + 1) % T).astype(F32)
        return pick(a, swap(b)), pick(swap(a), b)

    def y_send(src_of, dst, send, recv):
        for k in (2, 1, 3):
            to = lax.rem(y + k, Y)
            rc(src_of(to), dst.at[y], send.at[0], recv.at[0], dev(g, to), c).start()

    def y_got(dst, recv):
        got(dst.at[pl.ds(0, Y - 1)], recv.at[0])

    def y_sent(like, send):
        sent(like.at[pl.ds(0, Y - 1)], send.at[0])

    def load(src, dst, i):
        copy = pltpu.make_async_copy(src, dst, r.in_s.at[i])
        copy.start()
        return copy

    tokbuf = r.tokbuf
    in_pu = load(r.pu_in, r.pu, 0)
    in_pv = load(r.pv_in, r.pv, 1)
    in_tok = load(r.tok_in, tokbuf.at[c, y], 2)
    in_cot = load(r.cot_in, r.cot, 3)
    in_cu = load(r.cu_in, r.cu, 4)
    in_cv = load(r.cv_in, r.cv, 5)
    in_factors = [
        load(a.at[0, pl.ds(h * HB, HB)], b.at[y, h], 6 + 2 * i + h)
        for i, (a, b) in enumerate(((r.rf_in, r.rbuf), (r.lf_in, r.lbuf)))
        for h in range(2)
    ]

    barrier = pltpu.get_barrier_semaphore()

    def greet(k, carry):
        pl.semaphore_signal(
            barrier, inc=1, device_id=(dev(lax.rem(g + k, NG), y), c), device_id_type=MESH
        )
        return carry

    for k in (1, 2, 3):
        pl.semaphore_signal(
            barrier, inc=1, device_id=(dev(g, lax.rem(y + k, Y)), c), device_id_type=MESH
        )
    pl.semaphore_signal(barrier, inc=1, device_id=(s, sib), device_id_type=MESH)
    lax.fori_loop(1, NG, greet, 0)

    wpad = r.wpad
    wpad[...] = jnp.zeros_like(wpad)
    kpad = r.kpad
    kpad[...] = jnp.zeros_like(kpad)
    in_pu.wait()
    in_pv.wait()
    wpad[0, 0:R, :] = r.pu[...].astype(F32)
    wpad[1, 0:R, :] = r.pv[...].astype(F32)
    for yy in range(Y):
        for t in range(T):
            r.wmsg[yy, t] = part(wpad[0], wpad[1], yy, t).astype(BF)
    pl.semaphore_wait(barrier, NG - 1 + Y)

    y_send(lambda to: r.wmsg.at[to], r.wland, r.wy_s, r.wy_r)
    in_tok.wait()
    rc(tokbuf.at[c, y], tokbuf.at[c, y], r.ts_s.at[0], r.ts_r.at[0], s, sib).start()
    for k in (2, 1, 3):
        to = lax.rem(y + k, Y)
        rc(tokbuf.at[c, y], tokbuf.at[c, y], r.ty_s.at[0], r.ty_r.at[y], dev(g, to), c).start()

    def factor_send(buf, send, recv):
        for k in (2, 1, 3):
            to = lax.rem(y + k, Y)
            rc(buf.at[y, c], buf.at[y, c], send.at[0], recv.at[0], dev(g, to), c).start()

    def factor_hand_on(buf, send, recv):
        got(buf.at[pl.ds(0, Y - 1), 0], recv.at[0])
        for k in (1, 3, 2):
            of = lax.rem(y + k, Y)
            rc(buf.at[of, c], buf.at[of, c], send.at[1], recv.at[1], s, sib).start()

    def factor(buf, recv):
        got(buf.at[pl.ds(0, Y - 1), 0], recv.at[1])
        return [buf[j].reshape(BLK, BLK) for j in range(Y)]

    r.wland[y] = r.wmsg[y]
    for copy in in_factors:
        copy.wait()
    factor_send(r.rbuf, r.rf_s, r.rf_r)
    in_cot.wait()
    cot = r.cot[...].astype(F32)
    for yy in range(Y):
        for t in range(T):
            r.cmsg[yy, t] = part(cot[:HB], cot[HB:], yy, t).astype(BF)
    y_send(lambda to: r.cmsg.at[to], r.cland, r.cy_s, r.cy_r)
    r.cland[y] = r.cmsg[y]
    factor_send(r.lbuf, r.lf_s, r.lf_r)

    row = lax.broadcasted_iota(jnp.int32, (RB, Y * 16), 0)
    col = lax.broadcasted_iota(jnp.int32, (RB, Y * 16), 1)
    sel = jnp.zeros((RB, Y * 16), F32)
    for a in range(Y):
        hit = (row >= R * a) & (row < R * (a + 1)) & (col - row == (16 - R) * a)
        sel = jnp.where(hit, 1.0, sel)
    sel = sel.astype(BF)


    wbuf = r.wbuf
    def along_x(t, of):
        for k in (2, 1, 3):
            to = lax.rem(x + k, X)
            block = wbuf.at[t, of, x]
            rc(block, block, r.gx_s.at[t], r.gx_r.at[t, x], dev(z * X + to, y), c).start()

    y_got(r.wland, r.wy_r)
    for t in range(T):
        wbuf[t, z, x] = dot(sel, r.wland[:, t].reshape(Y * 16, CW)).astype(BF)
        block = wbuf.at[t, z, x]
        if t < T - 1:
            for k in reversed(by_distance(Z)):
                to = lax.rem(z + k, Z)
                rc(block, block, r.gz_s.at[t], r.gz_r.at[t, z], dev(to * X + x, y), c).start()
        along_x(t, z)

    out_i = lax.broadcasted_iota(jnp.int32, (N, N), 0)
    in_i = lax.broadcasted_iota(jnp.int32, (N, N), 1)

    def hits(a, b):
        return jnp.where(a == b, 1.0, 0.0).astype(BF)

    def swapped_index(v):
        return lax.rem(v // 4, 4) * BLK + (v // 16) * 4 + lax.rem(v, 4)

    def rotated_index(v):
        return lax.rem(v, 4) * BLK + (v // 16) * 4 + lax.rem(v // 4, 4)

    r.to_msg1[...] = hits(in_i, rotated_index(out_i))
    r.from_msg1[...] = hits(out_i, swapped_index(in_i))
    r.to_msg2[...] = hits(in_i, swapped_index(out_i))
    r.from_msg2[...] = hits(out_i, rotated_index(in_i))

    in_cu.wait()
    in_cv.wait()
    kpad[0, 0:3, :] = r.cu[...]
    kpad[1, 0:3, :] = r.cv[...]
    for t in range(T):
        kt = part(kpad[0], kpad[1], 0, t)
        for yy in range(1, Y):
            kt = jnp.where(y == yy, part(kpad[0], kpad[1], yy, t), kt)
        r.kk[t] = kt

    def conv(t, first, second, third):
        return r.kk[t, 0:1] * first + r.kk[t, 1:2] * second + r.kk[t, 2:3] * third

    def gather_x(t):
        for k in by_distance(Z):
            of = lax.rem(z + k, Z)
            got(wbuf.at[t, of, x], r.gz_r.at[t, of])
            along_x(t, of)

    def gather_z(t):
        for k in (1, 3, 2):
            of = lax.rem(x + k, X)
            got(wbuf.at[t, z, of], r.gx_r.at[t, of])
        for k in reversed(by_distance(Z)):
            to = lax.rem(z + k, Z)
            rc(wbuf.at[t, z], wbuf.at[t, z], r.gz_s.at[t], r.gz_r.at[t, z], dev(to * X + x, y), c).start()

    ext, cvs, ccb, vb, xb = r.ext, r.cvs, r.ccb, r.vb, r.xb
    cot2, extg, zs, gpb = r.cot2, r.extg, r.zs, r.gpb

    def project(t):
        if t == T - 1:
            for k in by_distance(Z):
                of = lax.rem(z + k, Z)
                got(wbuf.at[t, of], r.gz_r.at[t, of])
        else:
            for k in (1, 3, 2):
                of = lax.rem(x + k, X)
                got(wbuf.at[t, :, of], r.gx_r.at[t, of])
        pre = dot(tokbuf[c].reshape(N, chans), wbuf[t, pl.ds(c * half, half)].reshape(chans, CW))
        if t == 0:
            got(tokbuf.at[0], r.ts_r.at[0])
        pre = pre + dot(tokbuf[sib].reshape(N, chans), wbuf[t, pl.ds(sib * half, half)].reshape(chans, CW))
        ext[t, 8 : 8 + N, :] = pre.astype(BF).astype(F32)
        rc(ext.at[t, pl.ds(N, 8)], ext.at[t, pl.ds(0, 8)], r.h_s.at[t], r.h_r.at[t], dev(lax.rem(g + 1, NG), y), c).start()

    zs_to = [lax.rem(z + k, Z) for k in range(Z)]
    xs_to = [lax.rem(x + k, X) for k in range(X)]
    far_first = sorted(
        [(dz, dx) for dz in range(Z) for dx in range(X) if dz or dx],
        key=lambda d: -(min(d[0], Z - d[0]) + min(d[1], X - d[1])),
    )

    def exchange(src, dst, send, recv):
        for dz, dx in far_first:
            to = zs_to[dz] * X + xs_to[dx]
            rc(src.at[to], dst.at[g], send, recv, dev(to, y), c).start()
        dst[g] = src[g]

    def mix_rows(t):
        got(ext.at[t, pl.ds(0, 8)], r.h_r.at[t])

        @pl.when(g == 0)
        def _():
            ext[t, 0:8, :] = jnp.zeros((8, CW), F32)

        for j in range(Y):
            at = j * BLK
            m = r.cland[j, t].astype(F32)
            cot2[t, at : at + HB, :] = swap(m)
            cot2[t, at + HB : at + BLK, :] = m
            cv = conv(
                t,
                ext[t, 8 + at : 8 + at + BLK, :],
                ext[t, 7 + at : 7 + at + BLK, :],
                ext[t, 6 + at : 6 + at + BLK, :],
            )
            cvs[t, at : at + BLK, :] = cv
            cb = cv.astype(BF)
            ccb[t, j] = cb
            vb[at : at + BLK, :] = pick(dot(r.rbuf[j].reshape(BLK, BLK), cb), cot2[t, at : at + BLK, :] * cv).astype(BF)
        r.a1s[t] = dot(r.to_msg1[...], vb[...]).astype(BF).reshape(NG, 16, CW)
        exchange(r.a1s.at[t], r.a1r.at[t], r.a1_s.at[t], r.a1_r.at[t])

    def mix_columns(t):
        got(r.a1r.at[t, pl.ds(0, NG - 1)], r.a1_r.at[t])
        xb[t] = dot(r.from_msg1[...], r.a1r[t].reshape(N, CW)).astype(BF)
        for i in range(Y):
            xi = xb[t, i * BLK : (i + 1) * BLK, :]
            both = dot(r.lt[i], xi)
            vb[i * BLK : (i + 1) * BLK, :] = pick(both[:BLK], both[BLK:]).astype(BF)
        r.a2s[t] = dot(r.to_msg2[...], vb[...]).astype(BF).reshape(NG, 16, CW)
        exchange(r.a2s.at[t], r.a2r.at[t], r.a2_s.at[t], r.a2_r.at[t])

    def back_rows(t):
        got(r.a2r.at[t, pl.ds(0, NG - 1)], r.a2_r.at[t])
        zs[t] = swap(dot(r.from_msg2[...], r.a2r[t].reshape(N, CW)))
        for j in range(Y):
            at = j * BLK
            zj = zs[t, at : at + BLK, :]
            extg[t, at : at + BLK, :] = pick(dot(r.rt[j], zj.astype(BF)), cot2[t, at : at + BLK, :] * zj)
            m = cvs[t, at : at + BLK, :] * zj
            r.mmsg[t, j] = pick(swap(m[:HB]), m[HB:]).astype(BF)
        rc(extg.at[t, pl.ds(0, 8)], extg.at[t, pl.ds(N, 8)], r.h_s.at[T + t], r.h_r.at[T + t], dev(lax.rem(g + NG - 1, NG), y), c).start()
        for k in (2, 1, 3):
            to = lax.rem(y + k, Y)
            rc(r.mmsg.at[t, to], r.mland.at[t, y], r.mm_s.at[t], r.mm_r.at[t], dev(g, to), c).start()
        r.mland[t, y] = r.mmsg[t, y]

    wgs, wgx, zsend, zland = r.wgs, r.wgx, r.zsend, r.zland
    z_order = list(reversed(by_distance(Z))) + [0]

    def weight_grads(t):
        got(extg.at[t, pl.ds(N, 8)], r.h_r.at[T + t])

        @pl.when(g == NG - 1)
        def _():
            extg[t, N : N + 8, :] = jnp.zeros((8, CW), F32)

        for j in range(Y):
            at = j * BLK
            gpb[t, j] = conv(
                t,
                extg[t, at : at + BLK, :],
                extg[t, at + 1 : at + 1 + BLK, :],
                extg[t, at + 2 : at + 2 + BLK, :],
            ).astype(BF)
        gp = gpb[t].reshape(N, CW)
        for k in z_order:
            to = lax.rem(z + k, Z)
            wgs[t, to] = dot(r.tokt[to], gp).astype(BF).reshape(X, RB, CW)
            for kx in (2, 1, 3):
                tox = lax.rem(x + kx, X)
                rc(wgs.at[t, to, tox], wgx.at[t, to, x], r.wx_s.at[t], r.wx_r.at[t, to], dev(z * X + tox, y), c).start()
            wgx[t, to, x] = wgs[t, to, x]

    def sum4(land):
        return (land[0].astype(F32) + land[1].astype(F32)) + (land[2].astype(F32) + land[3].astype(F32))

    def weight_sums(t):
        for k in z_order:
            to = lax.rem(z + k, Z)
            got(wgx.at[t, to, pl.ds(0, X - 1)], r.wx_r.at[t, to])
            zsend[t, to] = sum4(wgx[t, to]).astype(BF)
            if k:
                rc(zsend.at[t, to], zland.at[t, z], r.wz_s.at[t], r.wz_r.at[t], dev(to * X + x, y), c).start()
        zland[t, z] = zsend[t, z]

    def left_grads():
        for i in range(Y):
            grads, cols = [], []
            for t in range(T):
                xi = xb[t, i * BLK : (i + 1) * BLK, :]
                xs = swap(xi.astype(F32))
                grads.append(pick(xs, jnp.zeros_like(xs)).astype(BF))
                cols.append(xi)
            r.lgs[i] = dot_nt(jnp.concatenate(grads, axis=1), jnp.concatenate(cols, axis=1)).astype(BF)
        y_send(lambda to: r.lgs.at[to], r.lgl, r.lg_s, r.lg_r)
        r.lgl[y] = r.lgs[y]

    def right_grads():
        for j in range(Y):
            rows = []
            for t in range(T):
                zj = zs[t, j * BLK : (j + 1) * BLK, :]
                rows.append(pick(zj, jnp.zeros_like(zj)).astype(BF))
            r.rgs[j] = dot_nt(
                jnp.concatenate(rows, axis=1), jnp.concatenate([ccb[t, j] for t in range(T)], axis=1)
            ).astype(BF)
        y_send(lambda to: r.rgs.at[to], r.rgl, r.rg_s, r.rg_r)
        r.rgl[y] = r.rgs[y]

    kgs = r.kgs

    def conv_grads():
        kgs[...] = jnp.zeros_like(kgs)
        for t in range(T):
            for lag in range(3):
                kgs[t, lag : lag + 1, :] = jnp.sum(
                    extg[t, 0:N, :] * ext[t, 8 - lag : 8 - lag + N, :], axis=0, keepdims=True
                )
        for k in (2, 1, 3):
            to = lax.rem(x + k, X)
            rc(kgs, r.kgx.at[x], r.kx_s.at[0], r.kx_r.at[0], dev(z * X + to, y), c).start()
        r.kgx[x] = kgs[...]

    tgs, tgl, tgy, tgr = r.tgs, r.tgl, r.tgy, r.tgr

    def rows_of(at, chunks):
        return jnp.concatenate([gpb[t, at] for t in chunks], axis=1)

    def half_of(cc, chunks):
        return jnp.concatenate(
            [wbuf[t, pl.ds(cc * half, half)].reshape(chans, CW) for t in chunks], axis=1
        )

    early, late = list(range(T - 1)), [T - 1]

    def token_grads(out, cc, chunks):
        w = half_of(cc, chunks)
        for k in (2, 1, 3, 0):
            of = lax.rem(y + k, Y)
            out[of] = dot_nt(rows_of(of, chunks), w)

    gather_z(2)
    gather_x(0)
    for k in (1, 3, 2):
        of = lax.rem(y + k, Y)
        block = tokbuf.at[c, of]
        got(block, r.ty_r.at[of])
        rc(block, block, r.ts_s.at[0], r.ts_r.at[0], s, sib).start()
    gather_x(1)
    factor_hand_on(r.rbuf, r.rf_s, r.rf_r)
    project(0)
    project(1)
    y_got(r.cland, r.cy_r)
    right = factor(r.rbuf, r.rf_r)
    mix_rows(0)
    project(2)
    mix_rows(1)
    factor_hand_on(r.lbuf, r.lf_s, r.lf_r)
    for j in range(Y):
        r.rt[j] = transposed(right[j])
    for i in range(2):
        r.tokt[i * half : (i + 1) * half] = transposed(tokbuf[i].reshape(N, chans)).reshape(half, X * RB, N)
    mix_rows(2)
    left = factor(r.lbuf, r.lf_r)
    for j in range(Y):
        r.lt[j, 0:BLK] = left[j]
        r.lt[j, BLK:] = transposed(left[j])
    mix_columns(0)
    mix_columns(1)
    mix_columns(2)
    back_rows(0)
    left_grads()
    back_rows(1)
    weight_grads(0)
    back_rows(2)
    weight_grads(1)
    right_grads()
    conv_grads()
    token_grads(r.tg_part, sib, early)
    weight_grads(2)

    w_sib = half_of(sib, late)
    for k in (2, 1, 3, 0):
        of = lax.rem(y + k, Y)
        tgs[of] = (r.tg_part[of] + dot_nt(rows_of(of, late), w_sib)).astype(BF)
        rc(tgs.at[of], tgl.at[of], r.tgs_s.at[0], r.tgs_r.at[of], s, sib).start()
    token_grads(r.tg_part, c, early + late)
    weight_sums(0)

    got(r.kgx.at[pl.ds(0, X - 1)], r.kx_r.at[0])
    kgz, kgz_own = r.kgz, r.kgz_own
    kgz_own[...] = sum4(r.kgx)
    for k in reversed(by_distance(Z)):
        to = lax.rem(z + k, Z)
        rc(kgz_own, kgz.at[z], r.kz_s.at[0], r.kz_r.at[0], dev(to * X + x, y), c).start()
    kgz[z] = kgz_own[...]

    for k in (2, 1, 3, 0):
        of = lax.rem(y + k, Y)
        got(tgl.at[of], r.tgs_r.at[of])
        tgy[of] = (r.tg_part[of] + tgl[of].astype(F32)).astype(BF)
        if k:
            rc(tgy.at[of], tgr.at[y], r.tg_s.at[0], r.tg_r.at[0], dev(g, of), c).start()
    weight_sums(1)
    tgr[y] = tgy[y]

    weight_sums(2)

    got(kgz.at[pl.ds(0, Z - 1)], r.kz_r.at[0])
    kgy, kgy_own = r.kgy, r.kgy_own
    total = kgz[0]
    for i in range(1, Z):
        total = total + kgz[i]
    kgy_own[...] = total
    y_send(lambda to: kgy_own, kgy, r.ky_s, r.ky_r)
    kgy[y] = total

    y_got(r.rgl, r.rg_r)
    r.rgc[0] = sum4(r.rgl).astype(BF)
    rc(r.rgc.at[0], r.rgc.at[1], r.fc_s.at[0], r.fc_r.at[0], s, sib).start()
    y_got(r.lgl, r.lg_r)
    r.lgc[0] = sum4(r.lgl).astype(BF)
    rc(r.lgc.at[0], r.lgc.at[1], r.fc_s.at[1], r.fc_r.at[1], s, sib).start()

    for t in range(T):
        got(r.mland.at[t, pl.ds(0, Y - 1)], r.mm_r.at[t])
    for tile in range(Y * T // 2):
        top, bottom = whole(lambda yy, t: r.mland[t, yy], tile)
        r.mixed_v[0:HB, tile * CW : (tile + 1) * CW] = top.astype(BF)
        r.mixed_v[HB:BLK, tile * CW : (tile + 1) * CW] = bottom.astype(BF)

    row = lax.broadcasted_iota(jnp.int32, (Y * 16, RB), 0)
    col = lax.broadcasted_iota(jnp.int32, (Y * 16, RB), 1)
    spread = jnp.zeros((Y * 16, RB), F32)
    for a in range(Y):
        hit = (col >= R * a) & (col < R * (a + 1)) & (row - col == (16 - R) * a)
        spread = jnp.where(hit, 1.0, spread)
    spread = spread.astype(BF)
    for t in range(T):
        got(zland.at[t, pl.ds(0, Z - 1)], r.wz_r.at[t])
        total = zland[t, 0].astype(F32)
        for i in range(1, Z):
            total = total + zland[t, i].astype(F32)
        r.ymsg[:, t] = dot(spread, total.astype(BF)).astype(BF).reshape(Y, 16, CW)
    y_send(lambda to: r.ymsg.at[to], r.yland, r.wb_s, r.wb_r)
    r.yland[y] = r.ymsg[y]

    stores = []

    def store(src, dst):
        copy = pltpu.make_async_copy(src, dst, r.out_s.at[len(stores)])
        copy.start()
        stores.append(copy)

    store(r.mixed_v, r.mixed_out)

    sent(tokbuf.at[0], r.ts_s.at[0])
    y_sent(tokbuf.at[0], r.ty_s)
    y_sent(r.wmsg, r.wy_s)
    for i in range(2):
        sent(r.rbuf.at[pl.ds(0, Y - 1), 0], r.rf_s.at[i])
        sent(r.lbuf.at[pl.ds(0, Y - 1), 0], r.lf_s.at[i])
    y_sent(r.cmsg, r.cy_s)
    for t in range(T):
        if t == T - 1:
            sent(wbuf.at[t, pl.ds(0, Z - 1)], r.gz_s.at[t])
            sent(wbuf.at[t, 0, pl.ds(0, X - 1)], r.gx_s.at[t])
        else:
            sent(wbuf.at[t, pl.ds(0, Z - 1), 0], r.gz_s.at[t])
            for i in range(X - 1):
                sent(wbuf.at[t, :, i], r.gx_s.at[t])
        sent(ext.at[t, pl.ds(0, 8)], r.h_s.at[t])
        sent(extg.at[t, pl.ds(0, 8)], r.h_s.at[T + t])
        sent(r.a1s.at[t, pl.ds(0, NG - 1)], r.a1_s.at[t])
        sent(r.a2s.at[t, pl.ds(0, NG - 1)], r.a2_s.at[t])
        for i in range(X - 1):
            sent(wgs.at[t, :, i], r.wx_s.at[t])
        sent(zland.at[t, pl.ds(0, Z - 1)], r.wz_s.at[t])
    sent(tgs, r.tgs_s.at[0])
    y_sent(tgs, r.tg_s)
    sent(r.kgx.at[pl.ds(0, X - 1)], r.kx_s.at[0])
    sent(kgz.at[pl.ds(0, Z - 1)], r.kz_s.at[0])
    for t in range(T):
        sent(r.mmsg.at[t, pl.ds(0, Y - 1)], r.mm_s.at[t])
    y_sent(r.rgs, r.rg_s)
    y_sent(r.lgs, r.lg_s)

    got(r.rgc.at[1], r.fc_r.at[0])
    r.rg_v[0] = r.rgc[0].astype(F32) + r.rgc[1].astype(F32)
    store(r.rg_v, r.rg_out)
    got(r.lgc.at[1], r.fc_r.at[1])
    r.lg_v[0] = r.lgc[0].astype(F32) + r.lgc[1].astype(F32)
    store(r.lg_v, r.lg_out)
    y_got(kgy, r.ky_r)
    for tile in range(Y * T // 2):
        u, v = whole(lambda yy, t: kgy[yy, t], tile)
        r.cug_v[:, tile * CW : (tile + 1) * CW] = u[0:3]
        r.cvg_v[:, tile * CW : (tile + 1) * CW] = v[0:3]
    store(r.cug_v, r.cug_out)
    store(r.cvg_v, r.cvg_out)
    y_got(tgr, r.tg_r)
    r.tg_v[...] = sum4(tgr).astype(BF)
    store(r.tg_v, r.tg_out)
    y_got(r.yland, r.wb_r)
    for tile in range(Y * T // 2):
        u, v = whole(lambda yy, t: r.yland[yy, t], tile)
        r.pug_v[:, tile * CW : (tile + 1) * CW] = u[0:R]
        r.pvg_v[:, tile * CW : (tile + 1) * CW] = v[0:R]
    store(r.pug_v, r.pug_out)
    store(r.pvg_v, r.pvg_out)
    for i in range(2):
        sent(r.rgc.at[0], r.fc_s.at[i])
    y_sent(r.ymsg, r.wb_s)
    y_sent(kgy, r.ky_s)
    for copy in stores:
        copy.wait()


def layer(Z, X, tokens, cotangent, proj_u, proj_v, right_factor, left_factor, conv_u, conv_v):
    BLK, chans = tokens.shape
    R = proj_u.shape[0]
    NG = Z * X
    CW = 2 * (chans // (Y * T))
    HB = BLK // 2
    N = Y * BLK
    RB = Y * R
    ins = dict(
        tok_in=tokens,
        cot_in=cotangent,
        pu_in=proj_u,
        pv_in=proj_v,
        rf_in=right_factor,
        lf_in=left_factor,
        cu_in=conv_u,
        cv_in=conv_v,
    )
    shape = jax.ShapeDtypeStruct
    outs = dict(
        mixed_out=shape(tokens.shape, BF),
        tg_out=shape(tokens.shape, BF),
        pug_out=shape(proj_u.shape, F32),
        pvg_out=shape(proj_v.shape, F32),
        rg_out=shape(right_factor.shape, F32),
        lg_out=shape(left_factor.shape, F32),
        cug_out=shape(conv_u.shape, F32),
        cvg_out=shape(conv_v.shape, F32),
    )
    scratch = dict(
        mixed_v=(tokens.shape, BF),
        tg_v=(tokens.shape, BF),
        pug_v=(proj_u.shape, F32),
        pvg_v=(proj_v.shape, F32),
        rg_v=(right_factor.shape, F32),
        lg_v=(left_factor.shape, F32),
        cug_v=(conv_u.shape, F32),
        cvg_v=(conv_v.shape, F32),
        pu=(proj_u.shape, BF),
        pv=(proj_v.shape, BF),
        cot=(cotangent.shape, BF),
        cu=(conv_u.shape, F32),
        cv=(conv_v.shape, F32),
        wpad=((2, 16, chans), F32),
        kpad=((2, 8, chans), F32),
        kk=((T, 8, CW), F32),
        wmsg=((Y, T, 16, CW), BF),
        wland=((Y, T, 16, CW), BF),
        cmsg=((Y, T, HB, CW), BF),
        cland=((Y, T, HB, CW), BF),
        tokbuf=((2, Y, BLK, chans), BF),
        rbuf=((Y, 2, HB, BLK), BF),
        lbuf=((Y, 2, HB, BLK), BF),
        rt=((Y, BLK, BLK), BF),
        lt=((Y, 2 * BLK, BLK), BF),
        wbuf=((T, Z, X, RB, CW), BF),
        to_msg1=((N, N), BF),
        from_msg1=((N, N), BF),
        to_msg2=((N, N), BF),
        from_msg2=((N, N), BF),
        cot2=((T, N, CW), F32),
        ext=((T, N + 8, CW), F32),
        extg=((T, N + 8, CW), F32),
        cvs=((T, N, CW), F32),
        zs=((T, N, CW), F32),
        ccb=((T, Y, BLK, CW), BF),
        gpb=((T, Y, BLK, CW), BF),
        vb=((N, CW), BF),
        xb=((T, N, CW), BF),
        a1s=((T, NG, 16, CW), BF),
        a1r=((T, NG, 16, CW), BF),
        a2s=((T, NG, 16, CW), BF),
        a2r=((T, NG, 16, CW), BF),
        tokt=((Z, X * RB, N), BF),
        lgs=((Y, BLK, BLK), BF),
        lgl=((Y, BLK, BLK), BF),
        lgc=((2, BLK, BLK), BF),
        rgs=((Y, BLK, BLK), BF),
        rgl=((Y, BLK, BLK), BF),
        rgc=((2, BLK, BLK), BF),
        mmsg=((T, Y, HB, CW), BF),
        mland=((T, Y, HB, CW), BF),
        kgs=((T, 8, CW), F32),
        kgx=((X, T, 8, CW), F32),
        kgz_own=((T, 8, CW), F32),
        kgz=((Z, T, 8, CW), F32),
        kgy_own=((T, 8, CW), F32),
        kgy=((Y, T, 8, CW), F32),
        tg_part=((Y, BLK, chans), F32),
        tgs=((Y, BLK, chans), BF),
        tgl=((Y, BLK, chans), BF),
        tgy=((Y, BLK, chans), BF),
        tgr=((Y, BLK, chans), BF),
        wgs=((T, Z, X, RB, CW), BF),
        wgx=((T, Z, X, RB, CW), BF),
        zsend=((T, Z, RB, CW), BF),
        zland=((T, Z, RB, CW), BF),
        ymsg=((Y, T, 16, CW), BF),
        yland=((Y, T, 16, CW), BF),
    )
    one = (1,)
    sems = dict(
        in_s=(10,),
        out_s=(8,),
        ts_s=one,
        ts_r=one,
        ty_s=one,
        ty_r=(Y,),
        gz_s=(T,),
        gz_r=(T, Z),
        gx_s=(T,),
        gx_r=(T, X),
        h_s=(2 * T,),
        h_r=(2 * T,),
        a1_s=(T,),
        a1_r=(T,),
        a2_s=(T,),
        a2_r=(T,),
        wx_s=(T,),
        wx_r=(T, Z),
        wz_s=(T,),
        wz_r=(T,),
        kx_s=one,
        kx_r=one,
        kz_s=one,
        kz_r=one,
        tgs_s=one,
        tgs_r=(Y,),
        fc_s=(2,),
        fc_r=(2,),
        wy_s=one,
        wy_r=one,
        rf_s=(2,),
        rf_r=(2,),
        cy_s=one,
        cy_r=one,
        lf_s=(2,),
        lf_r=(2,),
        lg_s=one,
        lg_r=one,
        rg_s=one,
        rg_r=one,
        mm_s=(T,),
        mm_r=(T,),
        ky_s=one,
        ky_r=one,
        tg_s=one,
        tg_r=one,
        wb_s=one,
        wb_r=one,
    )
    names = list(ins) + list(outs) + list(scratch) + list(sems)

    def body(*refs):
        kernel(Z, X, types.SimpleNamespace(**dict(zip(names, refs))))

    hbm = pl.BlockSpec(memory_space=pltpu.HBM)
    results = pl.pallas_call(
        body,
        out_shape=list(outs.values()),
        in_specs=[hbm] * len(ins),
        out_specs=[hbm] * len(outs),
        scratch_shapes=[pltpu.VMEM(sh, dt) for sh, dt in scratch.values()]
        + [pltpu.SemaphoreType.DMA(sh) for sh in sems.values()],
        compiler_params=pltpu.CompilerParams(
            collective_id=0, has_side_effects=True, vmem_limit_bytes=63 * 1024 * 1024
        ),
    )(*ins.values())

    count = len(outs)

    def write(*refs):
        froms, tos, held = refs[:count], refs[count : 2 * count], refs[2 * count : 3 * count]
        into, out_of = refs[3 * count :]
        first = [pltpu.make_async_copy(froms[i], held[i], into.at[i]) for i in range(count)]
        second = [pltpu.make_async_copy(held[i], tos[i], out_of.at[i]) for i in range(count)]
        for copy in first:
            copy.start()
        for before, after in zip(first, second):
            before.wait()
            after.start()
        for copy in second:
            copy.wait()

    return pl.pallas_call(
        write,
        out_shape=list(outs.values()),
        in_specs=[hbm] * count,
        out_specs=[hbm] * count,
        scratch_shapes=[pltpu.VMEM(o.shape, o.dtype) for o in outs.values()]
        + [pltpu.SemaphoreType.DMA((count,))] * 2,
    )(*results)


def solution(mesh):
    groups = mesh.shape["seq"] // Y
    specs = (
        P("seq", "ch"),
        P("seq", "ch"),
        P("seq", "ch"),
        P("seq", "ch"),
        P("seq", None, None),
        P("seq", None, None),
        P(None, "ch"),
        P(None, "ch"),
    )
    return jax.shard_map(
        functools.partial(layer, groups // X, X),
        mesh=mesh,
        in_specs=specs,
        out_specs=specs,
        check_vma=False,
    )
```

```python
import functools
import types

import jax
import jax.numpy as jnp
from jax import lax
from jax.experimental import pallas as pl
from jax.experimental.pallas import tpu as pltpu
from jax.sharding import PartitionSpec as P

MESH = pl.DeviceIdType.MESH
BF = jnp.bfloat16
F32 = jnp.float32
Y = 4
X = 4
T = 3


def dot(a, b):
    return jnp.dot(a, b, preferred_element_type=F32)


def dot_nt(a, b):
    return lax.dot_general(a, b, (((1,), (1,)), ((), ())), preferred_element_type=F32)


def transposed(a):
    return a.astype(F32).T.astype(BF)


def by_distance(n):
    return sorted(range(1, n), key=lambda k: (min(k, n - k), k))


def kernel(Z, X, r):
    NG = Z * X
    BLK, chans = r.tok_in.shape
    HC = chans // (Y * T)
    CW = 2 * HC
    HB = BLK // 2
    N = Y * BLK
    R = r.pu_in.shape[0]
    RB = Y * R
    half = Z // 2

    s = lax.axis_index("seq")
    c = lax.axis_index("ch")
    g = s // Y
    y = lax.rem(s, Y)
    z = g // X
    x = lax.rem(g, X)
    sib = 1 - c

    def dev(gg, yy):
        return gg * Y + yy

    def in_u(shape):
        return lax.broadcasted_iota(jnp.int32, shape, len(shape) - 1) < HC

    def pick(u, v):
        return jnp.where(in_u(u.shape), u, v)

    def swap(v):
        return pltpu.roll(v, HC, 1)

    def rc(src, dst, send_sem, recv_sem, seq, ch):
        return pltpu.make_async_remote_copy(
            src_ref=src,
            dst_ref=dst,
            send_sem=send_sem,
            recv_sem=recv_sem,
            device_id=(seq, ch),
            device_id_type=MESH,
        )

    def got(ref, sem):
        rc(ref, ref, sem, sem, s, c).wait_recv()

    def sent(ref, sem):
        rc(ref, ref, sem, sem, s, c).wait_send()

    def part(u, v, yy, t):
        q = yy * T + t
        uq = u[:, q // 2 * CW : (q // 2 + 1) * CW]
        vq = v[:, q // 2 * CW : (q // 2 + 1) * CW]
        return pick(uq, swap(vq)) if q % 2 == 0 else pick(swap(uq), vq)

    def whole(land, tile):
        q = 2 * tile
        a = land(q // T, q % T).astype(F32)
        b = land((q + 1) // T, (q + 1) % T).astype(F32)
        return pick(a, swap(b)), pick(swap(a), b)

    def y_send(src_of, dst, send, recv):
        for k in (2, 1, 3):
            to = lax.rem(y + k, Y)
            rc(src_of(to), dst.at[y], send, recv.at[0], dev(g, to), c).start()

    def y_got(dst, recv):
        got(dst.at[pl.ds(0, Y - 1)], recv.at[0])

    def y_sent(like, send):
        sent(like.at[pl.ds(0, Y - 1)], send)

    def load(src, dst, i):
        copy = pltpu.make_async_copy(src, dst, r.in_s.at[i])
        copy.start()
        return copy

    tokbuf = r.tokbuf
    in_pu = load(r.pu_in, r.pu, 0)
    in_pv = load(r.pv_in, r.pv, 1)
    in_tok = load(r.tok_in, tokbuf.at[c, y], 2)
    in_cot = load(r.cot_in, r.cot, 3)
    in_cu = load(r.cu_in, r.cu, 4)
    in_cv = load(r.cv_in, r.cv, 5)
    in_factors = [
        load(a.at[0, pl.ds(h * HB, HB)], b.at[y, h], 6 + 2 * i + h)
        for i, (a, b) in enumerate(((r.rf_in, r.rbuf), (r.lf_in, r.lbuf)))
        for h in range(2)
    ]

    barrier = pltpu.get_barrier_semaphore()

    def greet(k, carry):
        pl.semaphore_signal(
            barrier, inc=1, device_id=(dev(lax.rem(g + k, NG), y), c), device_id_type=MESH
        )
        return carry

    for k in (1, 2, 3):
        pl.semaphore_signal(
            barrier, inc=1, device_id=(dev(g, lax.rem(y + k, Y)), c), device_id_type=MESH
        )
    pl.semaphore_signal(barrier, inc=1, device_id=(s, sib), device_id_type=MESH)
    lax.fori_loop(1, NG, greet, 0)

    wpad = r.wpad
    wpad[...] = jnp.zeros_like(wpad)
    kpad = r.kpad
    kpad[...] = jnp.zeros_like(kpad)
    in_pu.wait()
    in_pv.wait()
    wpad[0, 0:R, :] = r.pu[...].astype(F32)
    wpad[1, 0:R, :] = r.pv[...].astype(F32)
    for yy in range(Y):
        for t in range(T):
            r.wmsg[yy, t] = part(wpad[0], wpad[1], yy, t).astype(BF)
    pl.semaphore_wait(barrier, NG - 1 + Y)

    y_send(lambda to: r.wmsg.at[to], r.wland, r.few_s.at[0], r.wy_r)
    in_tok.wait()
    rc(tokbuf.at[c, y], tokbuf.at[c, y], r.ts_s.at[0], r.ts_r.at[0], s, sib).start()
    for k in (2, 1, 3):
        to = lax.rem(y + k, Y)
        rc(tokbuf.at[c, y], tokbuf.at[c, y], r.ty_s.at[0], r.ty_r.at[y], dev(g, to), c).start()

    def factor_send(buf, send, recv):
        for k in (2, 1, 3):
            to = lax.rem(y + k, Y)
            rc(buf.at[y, c], buf.at[y, c], send, recv.at[0], dev(g, to), c).start()

    def factor_hand_on(buf, send, recv):
        got(buf.at[pl.ds(0, Y - 1), 0], recv.at[0])
        for k in (1, 3, 2):
            of = lax.rem(y + k, Y)
            rc(buf.at[of, c], buf.at[of, c], send, recv.at[1], s, sib).start()

    def factor(buf, recv):
        got(buf.at[pl.ds(0, Y - 1), 0], recv.at[1])
        return [buf[j].reshape(BLK, BLK) for j in range(Y)]

    r.wland[y] = r.wmsg[y]
    for copy in in_factors:
        copy.wait()
    factor_send(r.rbuf, r.few_s.at[0], r.rf_r)
    in_cot.wait()
    cot = r.cot[...].astype(F32)
    for yy in range(Y):
        for t in range(T):
            r.cmsg[yy, t] = part(cot[:HB], cot[HB:], yy, t).astype(BF)
    y_send(lambda to: r.cmsg.at[to], r.cland, r.few_s.at[0], r.cy_r)
    r.cland[y] = r.cmsg[y]
    factor_send(r.lbuf, r.few_s.at[0], r.lf_r)

    row = lax.broadcasted_iota(jnp.int32, (RB, Y * 16), 0)
    col = lax.broadcasted_iota(jnp.int32, (RB, Y * 16), 1)
    sel = jnp.zeros((RB, Y * 16), F32)
    for a in range(Y):
        hit = (row >= R * a) & (row < R * (a + 1)) & (col - row == (16 - R) * a)
        sel = jnp.where(hit, 1.0, sel)
    sel = sel.astype(BF)


    wbuf = r.wbuf
    def along_x(t, of):
        for k in (2, 1, 3):
            to = lax.rem(x + k, X)
            block = wbuf.at[t, of, x]
            rc(block, block, r.gx_s.at[0], r.gx_r.at[t], dev(z * X + to, y), c).start()

    y_got(r.wland, r.wy_r)
    for t in range(T):
        wbuf[t, z, x] = dot(sel, r.wland[:, t].reshape(Y * 16, CW)).astype(BF)
        block = wbuf.at[t, z, x]
        if t < T - 1:
            for k in reversed(by_distance(Z)):
                to = lax.rem(z + k, Z)
                rc(block, block, r.gz_s.at[0], r.gz_r.at[t, z], dev(to * X + x, y), c).start()
        along_x(t, z)

    out_i = lax.broadcasted_iota(jnp.int32, (N, N), 0)
    in_i = lax.broadcasted_iota(jnp.int32, (N, N), 1)

    def hits(a, b):
        return jnp.where(a == b, 1.0, 0.0).astype(BF)

    def swapped_index(v):
        return lax.rem(v // 4, 4) * BLK + (v // 16) * 4 + lax.rem(v, 4)

    def rotated_index(v):
        return lax.rem(v, 4) * BLK + (v // 16) * 4 + lax.rem(v // 4, 4)

    r.to_msg1[...] = hits(in_i, rotated_index(out_i))
    r.from_msg1[...] = hits(out_i, swapped_index(in_i))
    r.to_msg2[...] = hits(in_i, swapped_index(out_i))
    r.from_msg2[...] = hits(out_i, rotated_index(in_i))

    in_cu.wait()
    in_cv.wait()
    kpad[0, 0:3, :] = r.cu[...]
    kpad[1, 0:3, :] = r.cv[...]
    for t in range(T):
        kt = part(kpad[0], kpad[1], 0, t)
        for yy in range(1, Y):
            kt = jnp.where(y == yy, part(kpad[0], kpad[1], yy, t), kt)
        r.kk[t] = kt

    def conv(t, first, second, third):
        return r.kk[t, 0:1] * first + r.kk[t, 1:2] * second + r.kk[t, 2:3] * third

    def gather_x(t):
        for k in by_distance(Z):
            of = lax.rem(z + k, Z)
            got(wbuf.at[t, of, x], r.gz_r.at[t, of])
            along_x(t, of)

    def gather_z(t):
        got(wbuf.at[t, z, pl.ds(0, X - 1)], r.gx_r.at[t])
        for k in reversed(by_distance(Z)):
            to = lax.rem(z + k, Z)
            rc(wbuf.at[t, z], wbuf.at[t, z], r.gz_s.at[0], r.gz_r.at[t, z], dev(to * X + x, y), c).start()

    ext, cvs, ccb, vb, xb = r.ext, r.cvs, r.ccb, r.vb, r.xb
    cot2, extg, zs, gpb = r.cot2, r.extg, r.zs, r.gpb

    def project(t):
        if t == T - 1:
            for k in by_distance(Z):
                of = lax.rem(z + k, Z)
                got(wbuf.at[t, of], r.gz_r.at[t, of])
        else:
            got(wbuf.at[t, :, pl.ds(0, X - 1)], r.gx_r.at[t])
        pre = dot(tokbuf[c].reshape(N, chans), wbuf[t, pl.ds(c * half, half)].reshape(chans, CW))
        if t == 0:
            got(tokbuf.at[0], r.ts_r.at[0])
        pre = pre + dot(tokbuf[sib].reshape(N, chans), wbuf[t, pl.ds(sib * half, half)].reshape(chans, CW))
        ext[t, 8 : 8 + N, :] = pre.astype(BF).astype(F32)
        rc(ext.at[t, pl.ds(N, 8)], ext.at[t, pl.ds(0, 8)], r.few_s.at[0], r.h_r.at[t], dev(lax.rem(g + 1, NG), y), c).start()

    zs_to = [lax.rem(z + k, Z) for k in range(Z)]
    xs_to = [lax.rem(x + k, X) for k in range(X)]
    far_first = sorted(
        [(dz, dx) for dz in range(Z) for dx in range(X) if dz or dx],
        key=lambda d: -(min(d[0], Z - d[0]) + min(d[1], X - d[1])),
    )

    def exchange(src, dst, send, recv):
        for dz, dx in far_first:
            to = zs_to[dz] * X + xs_to[dx]
            rc(src.at[to], dst.at[g], send, recv, dev(to, y), c).start()
        dst[g] = src[g]

    def mix_rows(t):
        got(ext.at[t, pl.ds(0, 8)], r.h_r.at[t])

        @pl.when(g == 0)
        def _():
            ext[t, 0:8, :] = jnp.zeros((8, CW), F32)

        for j in range(Y):
            at = j * BLK
            m = r.cland[j, t].astype(F32)
            cot2[t, at : at + HB, :] = swap(m)
            cot2[t, at + HB : at + BLK, :] = m
            cv = conv(
                t,
                ext[t, 8 + at : 8 + at + BLK, :],
                ext[t, 7 + at : 7 + at + BLK, :],
                ext[t, 6 + at : 6 + at + BLK, :],
            )
            cvs[t, at : at + BLK, :] = cv
            cb = cv.astype(BF)
            ccb[t, j] = cb
            vb[at : at + BLK, :] = pick(dot(r.rbuf[j].reshape(BLK, BLK), cb), cot2[t, at : at + BLK, :] * cv).astype(BF)
        r.a1s[t] = dot(r.to_msg1[...], vb[...]).astype(BF).reshape(NG, 16, CW)
        exchange(r.a1s.at[t], r.a1r.at[t], r.a_s.at[0], r.a1_r.at[t])

    def mix_columns(t):
        got(r.a1r.at[t, pl.ds(0, NG - 1)], r.a1_r.at[t])
        xb[t] = dot(r.from_msg1[...], r.a1r[t].reshape(N, CW)).astype(BF)
        for i in range(Y):
            xi = xb[t, i * BLK : (i + 1) * BLK, :]
            both = dot(r.lt[i], xi)
            vb[i * BLK : (i + 1) * BLK, :] = pick(both[:BLK], both[BLK:]).astype(BF)
        r.a2s[t] = dot(r.to_msg2[...], vb[...]).astype(BF).reshape(NG, 16, CW)
        exchange(r.a2s.at[t], r.a2r.at[t], r.a_s.at[0], r.a2_r.at[t])

    def back_rows(t):
        got(r.a2r.at[t, pl.ds(0, NG - 1)], r.a2_r.at[t])
        zs[t] = swap(dot(r.from_msg2[...], r.a2r[t].reshape(N, CW)))
        for j in range(Y):
            at = j * BLK
            zj = zs[t, at : at + BLK, :]
            extg[t, at : at + BLK, :] = pick(dot(r.rt[j], zj.astype(BF)), cot2[t, at : at + BLK, :] * zj)
            m = cvs[t, at : at + BLK, :] * zj
            r.mmsg[t, j] = pick(swap(m[:HB]), m[HB:]).astype(BF)
        rc(extg.at[t, pl.ds(0, 8)], extg.at[t, pl.ds(N, 8)], r.few_s.at[0], r.h_r.at[t], dev(lax.rem(g + NG - 1, NG), y), c).start()
        for k in (2, 1, 3):
            to = lax.rem(y + k, Y)
            rc(r.mmsg.at[t, to], r.mland.at[t, y], r.few_s.at[1], r.mm_r.at[0], dev(g, to), c).start()
        r.mland[t, y] = r.mmsg[t, y]

    wgs, wgq, wgx, zsend, zland = r.wgs, r.wgq, r.wgx, r.zsend, r.zland
    z_order = list(reversed(by_distance(Z))) + [0]

    def gate_back(t):
        got(extg.at[t, pl.ds(N, 8)], r.h_r.at[t])

        @pl.when(g == NG - 1)
        def _():
            extg[t, N : N + 8, :] = jnp.zeros((8, CW), F32)

        for j in range(Y):
            at = j * BLK
            gpb[t, j] = conv(
                t,
                extg[t, at : at + BLK, :],
                extg[t, at + 1 : at + 1 + BLK, :],
                extg[t, at + 2 : at + 2 + BLK, :],
            ).astype(BF)

    far_z = [k for k in z_order if min(k, Z - k) > 2]
    near_z = [k for k in z_order if k not in far_z]
    near_count = X * len(near_z) - 1

    def weight_grads(t):
        gp = gpb[t].reshape(N, CW)
        for i, k in enumerate(z_order):
            to = lax.rem(z + k, Z)
            wgs[t, to] = dot(r.tokt[to], gp).astype(BF).reshape(X, RB, CW)
            if t == T - 1 and k not in far_z:
                for kx in (2, 1, 3, 0):
                    if k or kx:
                        at = to * X + xs_to[kx]
                        rc(wgs.at[t, to, xs_to[kx]], r.wga.at[g], r.wx_s.at[t], r.wa_r.at[0], dev(at, y), c).start()
            elif t == 0:
                ahead, behind, across = x_ways(i)
                rc(wgs.at[t, to, across], wgq.at[to], r.wx_s.at[t], r.wq_r.at[to], dev(z * X + ahead, y), c).start()
                rc(wgs.at[t, to, behind], wgx.at[t, to, 0], r.wx_s.at[t], r.gz_r.at[t, to], dev(z * X + behind, y), c).start()
            else:
                for kx in (2, 1, 3):
                    rc(wgs.at[t, to, xs_to[kx]], wgx.at[t, to, x], r.wx_s.at[t], r.gz_r.at[t, to], dev(z * X + xs_to[kx], y), c).start()
                wgx[t, to, x] = wgs[t, to, x]
        if t == T - 1:
            r.wga[g] = wgs[t, z, x]

    def x_ways(i):
        d = 1 if i % 2 == 0 else X - 1
        return lax.rem(x + d, X), lax.rem(x + X - d, X), lax.rem(x + 2, X)

    def weight_relay():
        t = 0
        for i, k in enumerate(z_order):
            to = lax.rem(z + k, Z)
            ahead = x_ways(i)[0]
            got(wgq.at[to], r.wq_r.at[to])
            wgs[t, to, ahead] = (wgs[t, to, ahead].astype(F32) + wgq[to].astype(F32)).astype(BF)
            rc(wgs.at[t, to, ahead], wgx.at[t, to, 1], r.wx_s.at[t], r.gz_r.at[t, to], dev(z * X + ahead, y), c).start()

    def sum4(land):
        return (land[0].astype(F32) + land[1].astype(F32)) + (land[2].astype(F32) + land[3].astype(F32))

    def weight_sums(t):
        for k in z_order if t < T - 1 else far_z:
            to = lax.rem(z + k, Z)
            if t:
                got(wgx.at[t, to, pl.ds(0, X - 1)], r.gz_r.at[t, to])
                zsend[t, to] = sum4(wgx[t, to]).astype(BF)
            else:
                got(wgx.at[t, to, pl.ds(0, 2)], r.gz_r.at[t, to])
                zsend[t, to] = (
                    wgs[t, to, x].astype(F32) + wgx[t, to, 0].astype(F32) + wgx[t, to, 1].astype(F32)
                ).astype(BF)
            if k:
                rc(zsend.at[t, to], zland.at[t, z], r.wz_s.at[0], r.wz_r.at[t], dev(to * X + x, y), c).start()
        if t < T - 1:
            zland[t, z] = zsend[t, z]

    def left_grads():
        for i in range(Y):
            grads, cols = [], []
            for t in range(T):
                xi = xb[t, i * BLK : (i + 1) * BLK, :]
                xs = swap(xi.astype(F32))
                grads.append(pick(xs, jnp.zeros_like(xs)).astype(BF))
                cols.append(xi)
            r.lgs[i] = dot_nt(jnp.concatenate(grads, axis=1), jnp.concatenate(cols, axis=1)).astype(BF)
        y_send(lambda to: r.lgs.at[to], r.lgl, r.few_s.at[1], r.lg_r)
        r.lgl[y] = r.lgs[y]

    def right_grads():
        for j in range(Y):
            rows = []
            for t in range(T):
                zj = zs[t, j * BLK : (j + 1) * BLK, :]
                rows.append(pick(zj, jnp.zeros_like(zj)).astype(BF))
            r.rgs[j] = dot_nt(
                jnp.concatenate(rows, axis=1), jnp.concatenate([ccb[t, j] for t in range(T)], axis=1)
            ).astype(BF)
        y_send(lambda to: r.rgs.at[to], r.rgl, r.few_s.at[1], r.rg_r)
        r.rgl[y] = r.rgs[y]

    kgs = r.kgs

    def conv_grads():
        kgs[...] = jnp.zeros_like(kgs)
        for t in range(T):
            for lag in range(3):
                kgs[t, lag : lag + 1, :] = jnp.sum(
                    extg[t, 0:N, :] * ext[t, 8 - lag : 8 - lag + N, :], axis=0, keepdims=True
                )
        for k in (2, 1, 3):
            to = lax.rem(x + k, X)
            rc(kgs, r.kgx.at[x], r.few_s.at[1], r.kx_r.at[0], dev(z * X + to, y), c).start()
        r.kgx[x] = kgs[...]

    tgs, tgl, tgy, tgr = r.tgs, r.tgl, r.tgy, r.tgr

    def rows_of(at, chunks):
        return jnp.concatenate([gpb[t, at] for t in chunks], axis=1)

    def half_of(cc, chunks):
        return jnp.concatenate(
            [wbuf[t, pl.ds(cc * half, half)].reshape(chans, CW) for t in chunks], axis=1
        )

    early, late = list(range(T - 1)), [T - 1]

    def token_grads(out, cc, chunks):
        w = half_of(cc, chunks)
        for k in (2, 1, 3, 0):
            of = lax.rem(y + k, Y)
            out[of] = dot_nt(rows_of(of, chunks), w)

    gather_x(0)
    gather_z(2)
    for k in (1, 3, 2):
        of = lax.rem(y + k, Y)
        block = tokbuf.at[c, of]
        got(block, r.ty_r.at[of])
        rc(block, block, r.ts_s.at[0], r.ts_r.at[0], s, sib).start()
    gather_x(1)
    factor_hand_on(r.rbuf, r.few_s.at[0], r.rf_r)
    project(0)
    project(1)
    y_got(r.cland, r.cy_r)
    right = factor(r.rbuf, r.rf_r)
    mix_rows(0)
    project(2)
    mix_rows(1)
    factor_hand_on(r.lbuf, r.few_s.at[0], r.lf_r)
    for j in range(Y):
        r.rt[j] = transposed(right[j])
    for i in range(2):
        r.tokt[i * half : (i + 1) * half] = transposed(tokbuf[i].reshape(N, chans)).reshape(half, X * RB, N)
    mix_rows(2)
    left = factor(r.lbuf, r.lf_r)
    for j in range(Y):
        r.lt[j, 0:BLK] = left[j]
        r.lt[j, BLK:] = transposed(left[j])
    mix_columns(0)
    mix_columns(1)
    mix_columns(2)
    back_rows(0)
    left_grads()
    back_rows(1)
    gate_back(0)
    weight_grads(0)
    y_got(r.lgl, r.lg_r)
    r.lgc[0] = sum4(r.lgl).astype(BF)
    rc(r.lgc.at[0], r.lgc.at[1], r.few_s.at[1], r.fc_r.at[1], s, sib).start()
    back_rows(2)
    conv_grads()
    gate_back(1)
    weight_grads(1)
    token_grads(r.tg_part, sib, early)
    weight_relay()
    gate_back(2)

    w_sib = half_of(sib, late)
    for k in (2, 1, 3, 0):
        of = lax.rem(y + k, Y)
        tgs[of] = (r.tg_part[of] + dot_nt(rows_of(of, late), w_sib)).astype(BF)
        rc(tgs.at[of], tgl.at[of], r.tgs_s.at[0], r.tgs_r.at[of], s, sib).start()
    got(r.kgx.at[pl.ds(0, X - 1)], r.kx_r.at[0])
    kgz, kgz_own = r.kgz, r.kgz_own
    kgz_own[...] = sum4(r.kgx)
    for k in reversed(by_distance(Z)):
        to = lax.rem(z + k, Z)
        rc(kgz_own, kgz.at[z], r.few_s.at[1], r.kz_r.at[0], dev(to * X + x, y), c).start()
    kgz[z] = kgz_own[...]

    weight_grads(2)
    right_grads()
    token_grads(r.tg_part, c, early + late)
    weight_sums(0)
    ahead, across, behind = (lax.rem(y + k, Y) for k in (1, 2, 3))

    def y_copy(src, dst, recv, to):
        rc(src, dst, r.tg_s.at[0], recv, dev(g, to), c).start()

    for of in (across, ahead, behind, y):
        got(tgl.at[of], r.tgs_r.at[of])
        total = r.tg_part[of] + tgl[of].astype(F32)
        r.tg_part[of] = total
        tgy[of] = total.astype(BF).reshape(2, HB, chans)
        if of is across:
            y_copy(tgy.at[of, 0], r.tgq.at[0], r.tq_r.at[0], ahead)
            y_copy(tgy.at[of, 1], r.tgq.at[1], r.tq_r.at[1], behind)
        if of is ahead:
            y_copy(tgy.at[of, 1], tgr.at[0, 1], r.tg_r.at[0], ahead)
        if of is behind:
            y_copy(tgy.at[of, 0], tgr.at[1, 0], r.tg_r.at[0], behind)
    weight_sums(2)
    weight_sums(1)
    y_got(r.rgl, r.rg_r)
    r.rgc[0] = sum4(r.rgl).astype(BF)
    rc(r.rgc.at[0], r.rgc.at[1], r.few_s.at[1], r.fc_r.at[0], s, sib).start()
    got(kgz.at[pl.ds(0, Z - 1)], r.kz_r.at[0])
    kgy, kgy_own = r.kgy, r.kgy_own
    total = kgz[0]
    for i in range(1, Z):
        total = total + kgz[i]
    kgy_own[...] = total
    y_send(lambda to: kgy_own, kgy, r.few_s.at[1], r.ky_r)
    kgy[y] = total
    got(r.tgq.at[0], r.tq_r.at[0])
    tgy[ahead, 0] = (r.tg_part[ahead, 0:HB] + r.tgq[0].astype(F32)).astype(BF)
    y_copy(tgy.at[ahead, 0], tgr.at[0, 0], r.tg_r.at[0], ahead)
    got(r.tgq.at[1], r.tq_r.at[1])
    tgy[behind, 1] = (r.tg_part[behind, HB:] + r.tgq[1].astype(F32)).astype(BF)
    y_copy(tgy.at[behind, 1], tgr.at[1, 1], r.tg_r.at[0], behind)


    got(r.mland.at[:, pl.ds(0, Y - 1)], r.mm_r.at[0])
    for tile in range(Y * T // 2):
        top, bottom = whole(lambda yy, t: r.mland[t, yy], tile)
        r.mixed_v[0:HB, tile * CW : (tile + 1) * CW] = top.astype(BF)
        r.mixed_v[HB:BLK, tile * CW : (tile + 1) * CW] = bottom.astype(BF)

    row = lax.broadcasted_iota(jnp.int32, (Y * 16, RB), 0)
    col = lax.broadcasted_iota(jnp.int32, (Y * 16, RB), 1)
    spread = jnp.zeros((Y * 16, RB), F32)
    for a in range(Y):
        hit = (col >= R * a) & (col < R * (a + 1)) & (row - col == (16 - R) * a)
        spread = jnp.where(hit, 1.0, spread)
    spread = spread.astype(BF)
    for t in range(T):
        if t < T - 1:
            got(zland.at[t, pl.ds(0, Z - 1)], r.wz_r.at[t])
            parts = [zland[t, i] for i in range(Z)]
        else:
            got(r.wga.at[pl.ds(0, near_count)], r.wa_r.at[0])
            parts = [r.wga[zs_to[k] * X + i] for k in near_z for i in range(X)]
            if far_z:
                got(zland.at[t, pl.ds(0, len(far_z))], r.wz_r.at[t])
                parts += [zland[t, zs_to[k]] for k in far_z]
        total = parts[0].astype(F32)
        for block in parts[1:]:
            total = total + block.astype(F32)
        r.ymsg[:, t] = dot(spread, total.astype(BF)).astype(BF).reshape(Y, 16, CW)
    y_send(lambda to: r.ymsg.at[to], r.yland, r.few_s.at[1], r.wb_r)
    r.yland[y] = r.ymsg[y]

    stores = []

    def store(src, dst):
        copy = pltpu.make_async_copy(src, dst, r.in_s.at[len(stores)])
        copy.start()
        stores.append(copy)

    store(r.mixed_v, r.mixed_out)

    sent(tokbuf.at[0], r.ts_s.at[0])
    y_sent(tokbuf.at[0], r.ty_s.at[0])
    y_sent(r.wmsg, r.few_s.at[0])
    for i in range(2):
        sent(r.rbuf.at[pl.ds(0, Y - 1), 0], r.few_s.at[0])
        sent(r.lbuf.at[pl.ds(0, Y - 1), 0], r.few_s.at[0])
    y_sent(r.cmsg, r.few_s.at[0])
    for t in range(T):
        if t == T - 1:
            sent(wbuf.at[t, pl.ds(0, Z - 1)], r.gz_s.at[0])
            sent(wbuf.at[t, 0, pl.ds(0, X - 1)], r.gx_s.at[0])
        else:
            sent(wbuf.at[t, pl.ds(0, Z - 1), 0], r.gz_s.at[0])
            for i in range(X - 1):
                sent(wbuf.at[t, :, i], r.gx_s.at[0])
        sent(ext.at[t, pl.ds(0, 8)], r.few_s.at[0])
        sent(extg.at[t, pl.ds(0, 8)], r.few_s.at[0])
        sent(r.a1s.at[t, pl.ds(0, NG - 1)], r.a_s.at[0])
        sent(r.a2s.at[t, pl.ds(0, NG - 1)], r.a_s.at[0])
        if t < T - 1:
            for i in range(X - 1):
                sent(wgs.at[t, :, i], r.wx_s.at[t])
            sent(zland.at[t, pl.ds(0, Z - 1)], r.wz_s.at[0])
        else:
            sent(r.wga.at[pl.ds(0, near_count)], r.wx_s.at[t])
            if far_z:
                sent(r.wga.at[pl.ds(0, (X - 1) * len(far_z))], r.wx_s.at[t])
                sent(zland.at[t, pl.ds(0, len(far_z))], r.wz_s.at[0])
    sent(tgs, r.tgs_s.at[0])
    y_sent(tgs, r.tg_s.at[0])
    sent(r.kgx.at[pl.ds(0, X - 1)], r.few_s.at[1])
    sent(kgz.at[pl.ds(0, Z - 1)], r.few_s.at[1])
    for t in range(T):
        sent(r.mmsg.at[t, pl.ds(0, Y - 1)], r.few_s.at[1])
    y_sent(r.rgs, r.few_s.at[1])
    y_sent(r.lgs, r.few_s.at[1])

    got(r.rgc.at[1], r.fc_r.at[0])
    r.rg_v[0] = r.rgc[0].astype(F32) + r.rgc[1].astype(F32)
    store(r.rg_v, r.rg_out)
    got(r.lgc.at[1], r.fc_r.at[1])
    r.lg_v[0] = r.lgc[0].astype(F32) + r.lgc[1].astype(F32)
    store(r.lg_v, r.lg_out)
    y_got(kgy, r.ky_r)
    for tile in range(Y * T // 2):
        u, v = whole(lambda yy, t: kgy[yy, t], tile)
        r.cug_v[:, tile * CW : (tile + 1) * CW] = u[0:3]
        r.cvg_v[:, tile * CW : (tile + 1) * CW] = v[0:3]
    store(r.cug_v, r.cug_out)
    store(r.cvg_v, r.cvg_out)
    got(tgr, r.tg_r.at[0])
    for h in range(2):
        total = r.tg_part[y, h * HB : (h + 1) * HB] + tgr[0, h].astype(F32) + tgr[1, h].astype(F32)
        r.tg_v[h * HB : (h + 1) * HB, :] = total.astype(BF)
    store(r.tg_v, r.tg_out)
    y_got(r.yland, r.wb_r)
    for tile in range(Y * T // 2):
        u, v = whole(lambda yy, t: r.yland[yy, t], tile)
        r.pug_v[:, tile * CW : (tile + 1) * CW] = u[0:R]
        r.pvg_v[:, tile * CW : (tile + 1) * CW] = v[0:R]
    store(r.pug_v, r.pug_out)
    store(r.pvg_v, r.pvg_out)
    for i in range(2):
        sent(r.rgc.at[0], r.few_s.at[1])
    y_sent(r.ymsg, r.few_s.at[1])
    y_sent(kgy, r.few_s.at[1])
    for copy in stores:
        copy.wait()


def layer(Z, X, tokens, cotangent, proj_u, proj_v, right_factor, left_factor, conv_u, conv_v):
    BLK, chans = tokens.shape
    R = proj_u.shape[0]
    NG = Z * X
    CW = 2 * (chans // (Y * T))
    HB = BLK // 2
    N = Y * BLK
    RB = Y * R
    ins = dict(
        tok_in=tokens,
        cot_in=cotangent,
        pu_in=proj_u,
        pv_in=proj_v,
        rf_in=right_factor,
        lf_in=left_factor,
        cu_in=conv_u,
        cv_in=conv_v,
    )
    shape = jax.ShapeDtypeStruct
    outs = dict(
        mixed_out=shape(tokens.shape, BF),
        tg_out=shape(tokens.shape, BF),
        pug_out=shape(proj_u.shape, F32),
        pvg_out=shape(proj_v.shape, F32),
        rg_out=shape(right_factor.shape, F32),
        lg_out=shape(left_factor.shape, F32),
        cug_out=shape(conv_u.shape, F32),
        cvg_out=shape(conv_v.shape, F32),
    )
    scratch = dict(
        mixed_v=(tokens.shape, BF),
        tg_v=(tokens.shape, BF),
        pug_v=(proj_u.shape, F32),
        pvg_v=(proj_v.shape, F32),
        rg_v=(right_factor.shape, F32),
        lg_v=(left_factor.shape, F32),
        cug_v=(conv_u.shape, F32),
        cvg_v=(conv_v.shape, F32),
        pu=(proj_u.shape, BF),
        pv=(proj_v.shape, BF),
        cot=(cotangent.shape, BF),
        cu=(conv_u.shape, F32),
        cv=(conv_v.shape, F32),
        wpad=((2, 16, chans), F32),
        kpad=((2, 8, chans), F32),
        kk=((T, 8, CW), F32),
        wmsg=((Y, T, 16, CW), BF),
        wland=((Y, T, 16, CW), BF),
        cmsg=((Y, T, HB, CW), BF),
        cland=((Y, T, HB, CW), BF),
        tokbuf=((2, Y, BLK, chans), BF),
        rbuf=((Y, 2, HB, BLK), BF),
        lbuf=((Y, 2, HB, BLK), BF),
        rt=((Y, BLK, BLK), BF),
        lt=((Y, 2 * BLK, BLK), BF),
        wbuf=((T, Z, X, RB, CW), BF),
        to_msg1=((N, N), BF),
        from_msg1=((N, N), BF),
        to_msg2=((N, N), BF),
        from_msg2=((N, N), BF),
        cot2=((T, N, CW), F32),
        ext=((T, N + 8, CW), F32),
        extg=((T, N + 8, CW), F32),
        cvs=((T, N, CW), F32),
        zs=((T, N, CW), F32),
        ccb=((T, Y, BLK, CW), BF),
        gpb=((T, Y, BLK, CW), BF),
        vb=((N, CW), BF),
        xb=((T, N, CW), BF),
        a1s=((T, NG, 16, CW), BF),
        a1r=((T, NG, 16, CW), BF),
        a2s=((T, NG, 16, CW), BF),
        a2r=((T, NG, 16, CW), BF),
        tokt=((Z, X * RB, N), BF),
        lgs=((Y, BLK, BLK), BF),
        lgl=((Y, BLK, BLK), BF),
        lgc=((2, BLK, BLK), BF),
        rgs=((Y, BLK, BLK), BF),
        rgl=((Y, BLK, BLK), BF),
        rgc=((2, BLK, BLK), BF),
        mmsg=((T, Y, HB, CW), BF),
        mland=((T, Y, HB, CW), BF),
        kgs=((T, 8, CW), F32),
        kgx=((X, T, 8, CW), F32),
        kgz_own=((T, 8, CW), F32),
        kgz=((Z, T, 8, CW), F32),
        kgy_own=((T, 8, CW), F32),
        kgy=((Y, T, 8, CW), F32),
        tg_part=((Y, BLK, chans), F32),
        tgs=((Y, BLK, chans), BF),
        tgl=((Y, BLK, chans), BF),
        tgy=((Y, 2, HB, chans), BF),
        tgq=((2, HB, chans), BF),
        tgr=((2, 2, HB, chans), BF),
        wgs=((T, Z, X, RB, CW), BF),
        wgx=((T, Z, X, RB, CW), BF),
        wgq=((Z, RB, CW), BF),
        wga=((NG, RB, CW), BF),
        zsend=((T, Z, RB, CW), BF),
        zland=((T, Z, RB, CW), BF),
        ymsg=((Y, T, 16, CW), BF),
        yland=((Y, T, 16, CW), BF),
    )
    one = (1,)
    sems = dict(
        in_s=(10,),
        ts_s=one,
        ts_r=one,
        ty_s=one,
        ty_r=(Y,),
        gz_s=one,
        gz_r=(T, Z),
        gx_s=one,
        a_s=one,
        few_s=(2,),
        gx_r=(T,),
        h_r=(T,),
        a1_r=(T,),
        a2_r=(T,),
        wx_s=(T,),
        wq_r=(Z,),
        wz_s=one,
        wz_r=(T,),
        wa_r=one,
        kx_r=one,
        kz_r=one,
        tgs_s=one,
        tgs_r=(Y,),
        fc_r=(2,),
        wy_r=one,
        rf_r=(2,),
        cy_r=one,
        lf_r=(2,),
        lg_r=one,
        rg_r=one,
        mm_r=one,
        ky_r=one,
        tg_s=one,
        tg_r=one,
        tq_r=(2,),
        wb_r=one,
    )
    names = list(ins) + list(outs) + list(scratch) + list(sems)

    def body(*refs):
        kernel(Z, X, types.SimpleNamespace(**dict(zip(names, refs))))

    hbm = pl.BlockSpec(memory_space=pltpu.HBM)
    results = pl.pallas_call(
        body,
        out_shape=list(outs.values()),
        in_specs=[hbm] * len(ins),
        out_specs=[hbm] * len(outs),
        scratch_shapes=[pltpu.VMEM(sh, dt) for sh, dt in scratch.values()]
        + [pltpu.SemaphoreType.DMA(sh) for sh in sems.values()],
        compiler_params=pltpu.CompilerParams(
            collective_id=0, has_side_effects=True, vmem_limit_bytes=63 * 1024 * 1024
        ),
    )(*ins.values())

    count = len(outs)

    def write(*refs):
        froms, tos, held = refs[:count], refs[count : 2 * count], refs[2 * count : 3 * count]
        into, out_of = refs[3 * count :]
        first = [pltpu.make_async_copy(froms[i], held[i], into.at[i]) for i in range(count)]
        second = [pltpu.make_async_copy(held[i], tos[i], out_of.at[i]) for i in range(count)]
        for copy in first:
            copy.start()
        for before, after in zip(first, second):
            before.wait()
            after.start()
        for copy in second:
            copy.wait()

    return pl.pallas_call(
        write,
        out_shape=list(outs.values()),
        in_specs=[hbm] * count,
        out_specs=[hbm] * count,
        scratch_shapes=[pltpu.VMEM(o.shape, o.dtype) for o in outs.values()]
        + [pltpu.SemaphoreType.DMA((count,))] * 2,
    )(*results)


def solution(mesh):
    groups = mesh.shape["seq"] // Y
    specs = (
        P("seq", "ch"),
        P("seq", "ch"),
        P("seq", "ch"),
        P("seq", "ch"),
        P("seq", None, None),
        P("seq", None, None),
        P(None, "ch"),
        P(None, "ch"),
    )
    return jax.shard_map(
        functools.partial(layer, groups // X, X),
        mesh=mesh,
        in_specs=specs,
        out_specs=specs,
        check_vma=False,
    )
```

```python
import functools
import types

import jax
import jax.numpy as jnp
from jax import lax
from jax.experimental import pallas as pl
from jax.experimental.pallas import tpu as pltpu
from jax.sharding import PartitionSpec as P

MESH = pl.DeviceIdType.MESH
BF = jnp.bfloat16
F32 = jnp.float32
Y = 4
X = 4
T = 3


def dot(a, b):
    return jnp.dot(a, b, preferred_element_type=F32)


def dot_nt(a, b):
    return lax.dot_general(a, b, (((1,), (1,)), ((), ())), preferred_element_type=F32)


def transposed(a):
    return a.astype(F32).T.astype(BF)


def by_distance(n):
    return sorted(range(1, n), key=lambda k: (min(k, n - k), k))


def kernel(Z, X, r):
    NG = Z * X
    BLK, chans = r.tok_in.shape
    HC = chans // (Y * T)
    CW = 2 * HC
    HB = BLK // 2
    N = Y * BLK
    R = r.pu_in.shape[0]
    RB = Y * R
    half = Z // 2

    s = lax.axis_index("seq")
    c = lax.axis_index("ch")
    g = s // Y
    y = lax.rem(s, Y)
    z = g // X
    x = lax.rem(g, X)
    sib = 1 - c

    def dev(gg, yy):
        return gg * Y + yy

    def in_u(shape):
        return lax.broadcasted_iota(jnp.int32, shape, len(shape) - 1) < HC

    def pick(u, v):
        return jnp.where(in_u(u.shape), u, v)

    def swap(v):
        return pltpu.roll(v, HC, 1)

    def rc(src, dst, send_sem, recv_sem, seq, ch):
        return pltpu.make_async_remote_copy(
            src_ref=src,
            dst_ref=dst,
            send_sem=send_sem,
            recv_sem=recv_sem,
            device_id=(seq, ch),
            device_id_type=MESH,
        )

    def got(ref, sem):
        rc(ref, ref, sem, sem, s, c).wait_recv()

    def sent(ref, sem):
        rc(ref, ref, sem, sem, s, c).wait_send()

    def part(u, v, yy, t):
        q = yy * T + t
        uq = u[:, q // 2 * CW : (q // 2 + 1) * CW]
        vq = v[:, q // 2 * CW : (q // 2 + 1) * CW]
        return pick(uq, swap(vq)) if q % 2 == 0 else pick(swap(uq), vq)

    def whole(land, tile):
        q = 2 * tile
        a = land(q // T, q % T).astype(F32)
        b = land((q + 1) // T, (q + 1) % T).astype(F32)
        return pick(a, swap(b)), pick(swap(a), b)

    def y_send(src_of, dst, send, recv):
        for k in (2, 1, 3):
            to = lax.rem(y + k, Y)
            rc(src_of(to), dst.at[y], send, recv.at[0], dev(g, to), c).start()

    def y_got(dst, recv):
        got(dst.at[pl.ds(0, Y - 1)], recv.at[0])

    def y_sent(like, send):
        sent(like.at[pl.ds(0, Y - 1)], send)

    def load(src, dst, i):
        copy = pltpu.make_async_copy(src, dst, r.in_s.at[i])
        copy.start()
        return copy

    tokbuf = r.tokbuf
    in_pu = load(r.pu_in, r.pu, 0)
    in_pv = load(r.pv_in, r.pv, 1)
    in_tok = [load(r.tok_in.at[pl.ds(h * HB, HB)], tokbuf.at[c, y, h], 2 + 8 * h) for h in range(2)]
    in_cot = load(r.cot_in, r.cot, 3)
    in_cu = load(r.cu_in, r.cu, 4)
    in_cv = load(r.cv_in, r.cv, 5)
    in_factors = [
        load(a.at[0, pl.ds(h * HB, HB)], b.at[y, h], 6 + 2 * i + h)
        for i, (a, b) in enumerate(((r.rf_in, r.rbuf), (r.lf_in, r.lbuf)))
        for h in range(2)
    ]

    barrier = pltpu.get_barrier_semaphore()

    def greet(k, carry):
        pl.semaphore_signal(
            barrier, inc=1, device_id=(dev(lax.rem(g + k, NG), y), c), device_id_type=MESH
        )
        return carry

    for k in (1, 2, 3):
        pl.semaphore_signal(
            barrier, inc=1, device_id=(dev(g, lax.rem(y + k, Y)), c), device_id_type=MESH
        )
    pl.semaphore_signal(barrier, inc=1, device_id=(s, sib), device_id_type=MESH)
    lax.fori_loop(1, NG, greet, 0)

    wpad = r.wpad
    wpad[...] = jnp.zeros_like(wpad)
    kpad = r.kpad
    kpad[...] = jnp.zeros_like(kpad)
    in_pu.wait()
    in_pv.wait()
    wpad[0, 0:R, :] = r.pu[...].astype(F32)
    wpad[1, 0:R, :] = r.pv[...].astype(F32)
    for yy in range(Y):
        for t in range(T):
            r.wmsg[yy, t] = part(wpad[0], wpad[1], yy, t).astype(BF)
    pl.semaphore_wait(barrier, NG - 1 + Y)

    y_send(lambda to: r.wmsg.at[to], r.wland, r.few_s.at[0], r.wy_r)
    for copy in in_tok:
        copy.wait()
    rc(tokbuf.at[c, y], tokbuf.at[c, y], r.ts_s.at[0], r.ts_r.at[0], s, sib).start()

    def factor_send(buf, send, recv):
        for k in (2, 1, 3):
            to = lax.rem(y + k, Y)
            rc(buf.at[y, c], buf.at[y, c], send, recv.at[0], dev(g, to), c).start()

    def factor_hand_on(buf, send, recv):
        got(buf.at[pl.ds(0, Y - 1), 0], recv.at[0])
        for k in (1, 3, 2):
            of = lax.rem(y + k, Y)
            rc(buf.at[of, c], buf.at[of, c], send, recv.at[1], s, sib).start()

    def factor(buf, recv):
        got(buf.at[pl.ds(0, Y - 1), 0], recv.at[1])
        return [buf[j].reshape(BLK, BLK) for j in range(Y)]

    r.wland[y] = r.wmsg[y]
    for copy in in_factors:
        copy.wait()
    in_cot.wait()
    cot = r.cot[...].astype(F32)
    for yy in range(Y):
        for t in range(T):
            r.cmsg[yy, t] = part(cot[:HB], cot[HB:], yy, t).astype(BF)
    r.cland[y] = r.cmsg[y]

    row = lax.broadcasted_iota(jnp.int32, (RB, Y * 16), 0)
    col = lax.broadcasted_iota(jnp.int32, (RB, Y * 16), 1)
    sel = jnp.zeros((RB, Y * 16), F32)
    for a in range(Y):
        hit = (row >= R * a) & (row < R * (a + 1)) & (col - row == (16 - R) * a)
        sel = jnp.where(hit, 1.0, sel)
    sel = sel.astype(BF)


    wbuf = r.wbuf
    def along_x(t, of):
        for k in (2, 1, 3):
            to = lax.rem(x + k, X)
            block = wbuf.at[t, of, x]
            rc(block, block, r.gx_s.at[0], r.gx_r.at[t], dev(z * X + to, y), c).start()

    y_got(r.wland, r.wy_r)
    for t in range(T):
        wbuf[t, z, x] = dot(sel, r.wland[:, t].reshape(Y * 16, CW)).astype(BF)
        block = wbuf.at[t, z, x]
        if t < T - 1:
            for k in reversed(by_distance(Z)):
                to = lax.rem(z + k, Z)
                rc(block, block, r.gz_s.at[0], r.gz_r.at[t, z], dev(to * X + x, y), c).start()
        along_x(t, z)

    ahead, across, behind = (lax.rem(y + k, Y) for k in (1, 2, 3))

    def token_copy(of, h, to):
        block = tokbuf.at[c, of, h]
        rc(block, block, r.ty_s.at[0], r.ty_r.at[of, h], dev(g, to), c).start()

    def token_hand_on(of, h):
        block = tokbuf.at[c, of, h]
        got(block, r.ty_r.at[of, h])
        rc(block, block, r.ts_s.at[0], r.ts_r.at[0], s, sib).start()

    token_copy(y, 0, ahead)
    token_copy(y, 1, behind)
    token_copy(y, 1, ahead)
    token_copy(y, 0, behind)
    factor_send(r.rbuf, r.few_s.at[0], r.rf_r)
    y_send(lambda to: r.cmsg.at[to], r.cland, r.few_s.at[0], r.cy_r)
    factor_send(r.lbuf, r.few_s.at[0], r.lf_r)

    out_i = lax.broadcasted_iota(jnp.int32, (N, N), 0)
    in_i = lax.broadcasted_iota(jnp.int32, (N, N), 1)

    def hits(a, b):
        return jnp.where(a == b, 1.0, 0.0).astype(BF)

    def swapped_index(v):
        return lax.rem(v // 4, 4) * BLK + (v // 16) * 4 + lax.rem(v, 4)

    def rotated_index(v):
        return lax.rem(v, 4) * BLK + (v // 16) * 4 + lax.rem(v // 4, 4)

    r.to_msg1[...] = hits(in_i, rotated_index(out_i))
    r.from_msg1[...] = hits(out_i, swapped_index(in_i))
    r.to_msg2[...] = hits(in_i, swapped_index(out_i))
    r.from_msg2[...] = hits(out_i, rotated_index(in_i))

    in_cu.wait()
    in_cv.wait()
    kpad[0, 0:3, :] = r.cu[...]
    kpad[1, 0:3, :] = r.cv[...]
    for t in range(T):
        kt = part(kpad[0], kpad[1], 0, t)
        for yy in range(1, Y):
            kt = jnp.where(y == yy, part(kpad[0], kpad[1], yy, t), kt)
        r.kk[t] = kt

    def conv(t, first, second, third):
        return r.kk[t, 0:1] * first + r.kk[t, 1:2] * second + r.kk[t, 2:3] * third

    def gather_x(t):
        for k in by_distance(Z):
            of = lax.rem(z + k, Z)
            got(wbuf.at[t, of, x], r.gz_r.at[t, of])
            along_x(t, of)

    def gather_z(t):
        got(wbuf.at[t, z, pl.ds(0, X - 1)], r.gx_r.at[t])
        for k in reversed(by_distance(Z)):
            to = lax.rem(z + k, Z)
            rc(wbuf.at[t, z], wbuf.at[t, z], r.gz_s.at[0], r.gz_r.at[t, z], dev(to * X + x, y), c).start()

    ext, cvs, ccb, vb, xb = r.ext, r.cvs, r.ccb, r.vb, r.xb
    cot2, extg, zs, gpb = r.cot2, r.extg, r.zs, r.gpb

    def project(t):
        if t == T - 1:
            for k in by_distance(Z):
                of = lax.rem(z + k, Z)
                got(wbuf.at[t, of], r.gz_r.at[t, of])
        else:
            got(wbuf.at[t, :, pl.ds(0, X - 1)], r.gx_r.at[t])
        pre = dot(tokbuf[c].reshape(N, chans), wbuf[t, pl.ds(c * half, half)].reshape(chans, CW))
        if t == 0:
            got(tokbuf.at[0], r.ts_r.at[0])
        pre = pre + dot(tokbuf[sib].reshape(N, chans), wbuf[t, pl.ds(sib * half, half)].reshape(chans, CW))
        ext[t, 8 : 8 + N, :] = pre.astype(BF).astype(F32)
        rc(ext.at[t, pl.ds(N, 8)], ext.at[t, pl.ds(0, 8)], r.few_s.at[0], r.h_r.at[t], dev(lax.rem(g + 1, NG), y), c).start()

    zs_to = [lax.rem(z + k, Z) for k in range(Z)]
    xs_to = [lax.rem(x + k, X) for k in range(X)]
    far_first = sorted(
        [(dz, dx) for dz in range(Z) for dx in range(X) if dz or dx],
        key=lambda d: -(min(d[0], Z - d[0]) + min(d[1], X - d[1])),
    )

    def exchange(src, dst, send, recv):
        for dz, dx in far_first:
            to = zs_to[dz] * X + xs_to[dx]
            rc(src.at[to], dst.at[g], send, recv, dev(to, y), c).start()
        dst[g] = src[g]

    def mix_rows(t):
        got(ext.at[t, pl.ds(0, 8)], r.h_r.at[t])

        @pl.when(g == 0)
        def _():
            ext[t, 0:8, :] = jnp.zeros((8, CW), F32)

        for j in range(Y):
            at = j * BLK
            m = r.cland[j, t].astype(F32)
            cot2[t, at : at + HB, :] = swap(m)
            cot2[t, at + HB : at + BLK, :] = m
            cv = conv(
                t,
                ext[t, 8 + at : 8 + at + BLK, :],
                ext[t, 7 + at : 7 + at + BLK, :],
                ext[t, 6 + at : 6 + at + BLK, :],
            )
            cvs[t, at : at + BLK, :] = cv
            cb = cv.astype(BF)
            ccb[t, j] = cb
            vb[at : at + BLK, :] = pick(dot(r.rbuf[j].reshape(BLK, BLK), cb), cot2[t, at : at + BLK, :] * cv).astype(BF)
        r.a1s[t] = dot(r.to_msg1[...], vb[...]).astype(BF).reshape(NG, 16, CW)
        exchange(r.a1s.at[t], r.a1r.at[t], r.a_s.at[0], r.a1_r.at[t])

    def mix_columns(t):
        got(r.a1r.at[t, pl.ds(0, NG - 1)], r.a1_r.at[t])
        xb[t] = dot(r.from_msg1[...], r.a1r[t].reshape(N, CW)).astype(BF)
        for i in range(Y):
            xi = xb[t, i * BLK : (i + 1) * BLK, :]
            both = dot(r.lt[i], xi)
            vb[i * BLK : (i + 1) * BLK, :] = pick(both[:BLK], both[BLK:]).astype(BF)
        r.a2s[t] = dot(r.to_msg2[...], vb[...]).astype(BF).reshape(NG, 16, CW)
        exchange(r.a2s.at[t], r.a2r.at[t], r.a_s.at[0], r.a2_r.at[t])

    def back_rows(t):
        got(r.a2r.at[t, pl.ds(0, NG - 1)], r.a2_r.at[t])
        zs[t] = swap(dot(r.from_msg2[...], r.a2r[t].reshape(N, CW)))
        for j in range(Y):
            at = j * BLK
            zj = zs[t, at : at + BLK, :]
            extg[t, at : at + BLK, :] = pick(dot(r.rt[j], zj.astype(BF)), cot2[t, at : at + BLK, :] * zj)
            m = cvs[t, at : at + BLK, :] * zj
            r.mmsg[t, j] = pick(swap(m[:HB]), m[HB:]).astype(BF)
        rc(extg.at[t, pl.ds(0, 8)], extg.at[t, pl.ds(N, 8)], r.few_s.at[0], r.h_r.at[t], dev(lax.rem(g + NG - 1, NG), y), c).start()
        for k in (2, 1, 3):
            to = lax.rem(y + k, Y)
            rc(r.mmsg.at[t, to], r.mland.at[t, y], r.few_s.at[1], r.mm_r.at[0], dev(g, to), c).start()
        r.mland[t, y] = r.mmsg[t, y]

    wgs, wgq, wgx, zsend, zland = r.wgs, r.wgq, r.wgx, r.zsend, r.zland
    z_order = list(reversed(by_distance(Z))) + [0]

    def gate_back(t):
        got(extg.at[t, pl.ds(N, 8)], r.h_r.at[t])

        @pl.when(g == NG - 1)
        def _():
            extg[t, N : N + 8, :] = jnp.zeros((8, CW), F32)

        for j in range(Y):
            at = j * BLK
            gpb[t, j] = conv(
                t,
                extg[t, at : at + BLK, :],
                extg[t, at + 1 : at + 1 + BLK, :],
                extg[t, at + 2 : at + 2 + BLK, :],
            ).astype(BF)

    far_z = [k for k in z_order if min(k, Z - k) > 2]
    near_z = [k for k in z_order if k not in far_z]
    near_count = X * len(near_z) - 1

    def weight_grads(t):
        gp = gpb[t].reshape(N, CW)
        for i, k in enumerate(z_order):
            to = lax.rem(z + k, Z)
            wgs[t, to] = dot(r.tokt[to], gp).astype(BF).reshape(X, RB, CW)
            if t == T - 1 and k not in far_z:
                for kx in (2, 1, 3, 0):
                    if k or kx:
                        at = to * X + xs_to[kx]
                        rc(wgs.at[t, to, xs_to[kx]], r.wga.at[g], r.wx_s.at[t], r.wa_r.at[0], dev(at, y), c).start()
            elif t == 0:
                ahead, behind, across = x_ways(i)
                rc(wgs.at[t, to, across], wgq.at[to], r.wx_s.at[t], r.wq_r.at[to], dev(z * X + ahead, y), c).start()
                rc(wgs.at[t, to, behind], wgx.at[t, to, 0], r.wx_s.at[t], r.gz_r.at[t, to], dev(z * X + behind, y), c).start()
            else:
                for kx in (2, 1, 3):
                    rc(wgs.at[t, to, xs_to[kx]], wgx.at[t, to, x], r.wx_s.at[t], r.gz_r.at[t, to], dev(z * X + xs_to[kx], y), c).start()
                wgx[t, to, x] = wgs[t, to, x]
        if t == T - 1:
            r.wga[g] = wgs[t, z, x]

    def x_ways(i):
        d = 1 if i % 2 == 0 else X - 1
        return lax.rem(x + d, X), lax.rem(x + X - d, X), lax.rem(x + 2, X)

    def weight_relay():
        t = 0
        for i, k in enumerate(z_order):
            to = lax.rem(z + k, Z)
            ahead = x_ways(i)[0]
            got(wgq.at[to], r.wq_r.at[to])
            wgs[t, to, ahead] = (wgs[t, to, ahead].astype(F32) + wgq[to].astype(F32)).astype(BF)
            rc(wgs.at[t, to, ahead], wgx.at[t, to, 1], r.wx_s.at[t], r.gz_r.at[t, to], dev(z * X + ahead, y), c).start()

    def sum4(land):
        return (land[0].astype(F32) + land[1].astype(F32)) + (land[2].astype(F32) + land[3].astype(F32))

    def weight_sums(t):
        for k in z_order if t < T - 1 else far_z:
            to = lax.rem(z + k, Z)
            if t:
                got(wgx.at[t, to, pl.ds(0, X - 1)], r.gz_r.at[t, to])
                zsend[t, to] = sum4(wgx[t, to]).astype(BF)
            else:
                got(wgx.at[t, to, pl.ds(0, 2)], r.gz_r.at[t, to])
                zsend[t, to] = (
                    wgs[t, to, x].astype(F32) + wgx[t, to, 0].astype(F32) + wgx[t, to, 1].astype(F32)
                ).astype(BF)
            if k:
                rc(zsend.at[t, to], zland.at[t, z], r.wz_s.at[0], r.wz_r.at[t], dev(to * X + x, y), c).start()
        if t < T - 1:
            zland[t, z] = zsend[t, z]

    def left_grads():
        for i in range(Y):
            grads, cols = [], []
            for t in range(T):
                xi = xb[t, i * BLK : (i + 1) * BLK, :]
                xs = swap(xi.astype(F32))
                grads.append(pick(xs, jnp.zeros_like(xs)).astype(BF))
                cols.append(xi)
            r.lgs[i] = dot_nt(jnp.concatenate(grads, axis=1), jnp.concatenate(cols, axis=1)).astype(BF)
        y_send(lambda to: r.lgs.at[to], r.lgl, r.few_s.at[1], r.lg_r)
        r.lgl[y] = r.lgs[y]

    def right_grads():
        for j in range(Y):
            rows = []
            for t in range(T):
                zj = zs[t, j * BLK : (j + 1) * BLK, :]
                rows.append(pick(zj, jnp.zeros_like(zj)).astype(BF))
            r.rgs[j] = dot_nt(
                jnp.concatenate(rows, axis=1), jnp.concatenate([ccb[t, j] for t in range(T)], axis=1)
            ).astype(BF)
        y_send(lambda to: r.rgs.at[to], r.rgl, r.few_s.at[1], r.rg_r)
        r.rgl[y] = r.rgs[y]

    kgs = r.kgs

    def conv_grads():
        kgs[...] = jnp.zeros_like(kgs)
        for t in range(T):
            for lag in range(3):
                kgs[t, lag : lag + 1, :] = jnp.sum(
                    extg[t, 0:N, :] * ext[t, 8 - lag : 8 - lag + N, :], axis=0, keepdims=True
                )
        for k in (2, 1, 3):
            to = lax.rem(x + k, X)
            rc(kgs, r.kgx.at[x], r.few_s.at[1], r.kx_r.at[0], dev(z * X + to, y), c).start()
        r.kgx[x] = kgs[...]

    tgs, tgl, tgy, tgr = r.tgs, r.tgl, r.tgy, r.tgr

    def rows_of(at, chunks):
        return jnp.concatenate([gpb[t, at] for t in chunks], axis=1)

    def half_of(cc, chunks):
        return jnp.concatenate(
            [wbuf[t, pl.ds(cc * half, half)].reshape(chans, CW) for t in chunks], axis=1
        )

    early, late = list(range(T - 1)), [T - 1]

    def token_grads(out, cc, chunks):
        w = half_of(cc, chunks)
        for k in (2, 1, 3, 0):
            of = lax.rem(y + k, Y)
            out[of] = dot_nt(rows_of(of, chunks), w)

    gather_x(0)
    token_hand_on(behind, 0)
    token_copy(behind, 0, ahead)
    token_hand_on(ahead, 1)
    token_copy(ahead, 1, behind)
    gather_z(2)
    gather_x(1)
    token_hand_on(behind, 1)
    token_hand_on(ahead, 0)
    token_hand_on(across, 0)
    token_hand_on(across, 1)
    factor_hand_on(r.rbuf, r.few_s.at[0], r.rf_r)
    project(0)
    project(1)
    y_got(r.cland, r.cy_r)
    right = factor(r.rbuf, r.rf_r)
    mix_rows(0)
    project(2)
    mix_rows(1)
    factor_hand_on(r.lbuf, r.few_s.at[0], r.lf_r)
    for j in range(Y):
        r.rt[j] = transposed(right[j])
    for i in range(2):
        r.tokt[i * half : (i + 1) * half] = transposed(tokbuf[i].reshape(N, chans)).reshape(half, X * RB, N)
    mix_rows(2)
    left = factor(r.lbuf, r.lf_r)
    for j in range(Y):
        r.lt[j, 0:BLK] = left[j]
        r.lt[j, BLK:] = transposed(left[j])
    mix_columns(0)
    mix_columns(1)
    mix_columns(2)
    back_rows(0)
    left_grads()
    back_rows(1)
    gate_back(0)
    weight_grads(0)
    y_got(r.lgl, r.lg_r)
    r.lgc[0] = sum4(r.lgl).astype(BF)
    rc(r.lgc.at[0], r.lgc.at[1], r.few_s.at[1], r.fc_r.at[1], s, sib).start()
    back_rows(2)
    conv_grads()
    gate_back(1)
    weight_grads(1)
    token_grads(r.tg_part, sib, early)
    weight_relay()
    gate_back(2)

    w_sib = half_of(sib, late)
    for k in (2, 1, 3, 0):
        of = lax.rem(y + k, Y)
        tgs[of] = (r.tg_part[of] + dot_nt(rows_of(of, late), w_sib)).astype(BF)
        rc(tgs.at[of], tgl.at[of], r.tgs_s.at[0], r.tgs_r.at[of], s, sib).start()
    got(r.kgx.at[pl.ds(0, X - 1)], r.kx_r.at[0])
    kgz, kgz_own = r.kgz, r.kgz_own
    kgz_own[...] = sum4(r.kgx)
    for k in reversed(by_distance(Z)):
        to = lax.rem(z + k, Z)
        rc(kgz_own, kgz.at[z], r.few_s.at[1], r.kz_r.at[0], dev(to * X + x, y), c).start()
    kgz[z] = kgz_own[...]

    weight_grads(2)
    right_grads()
    token_grads(r.tg_part, c, early + late)
    weight_sums(0)

    def y_copy(src, dst, recv, to):
        rc(src, dst, r.tg_s.at[0], recv, dev(g, to), c).start()

    for of in (across, ahead, behind, y):
        got(tgl.at[of], r.tgs_r.at[of])
        total = r.tg_part[of] + tgl[of].astype(F32)
        r.tg_part[of] = total
        tgy[of] = total.astype(BF).reshape(2, HB, chans)
        if of is across:
            y_copy(tgy.at[of, 0], r.tgq.at[0], r.tq_r.at[0], ahead)
            y_copy(tgy.at[of, 1], r.tgq.at[1], r.tq_r.at[1], behind)
        if of is ahead:
            y_copy(tgy.at[of, 1], tgr.at[0, 1], r.tg_r.at[0], ahead)
        if of is behind:
            y_copy(tgy.at[of, 0], tgr.at[1, 0], r.tg_r.at[0], behind)
    weight_sums(2)
    weight_sums(1)
    y_got(r.rgl, r.rg_r)
    r.rgc[0] = sum4(r.rgl).astype(BF)
    rc(r.rgc.at[0], r.rgc.at[1], r.few_s.at[1], r.fc_r.at[0], s, sib).start()
    got(kgz.at[pl.ds(0, Z - 1)], r.kz_r.at[0])
    kgy, kgy_own = r.kgy, r.kgy_own
    total = kgz[0]
    for i in range(1, Z):
        total = total + kgz[i]
    kgy_own[...] = total
    y_send(lambda to: kgy_own, kgy, r.few_s.at[1], r.ky_r)
    kgy[y] = total
    got(r.tgq.at[0], r.tq_r.at[0])
    tgy[ahead, 0] = (r.tg_part[ahead, 0:HB] + r.tgq[0].astype(F32)).astype(BF)
    y_copy(tgy.at[ahead, 0], tgr.at[0, 0], r.tg_r.at[0], ahead)
    got(r.tgq.at[1], r.tq_r.at[1])
    tgy[behind, 1] = (r.tg_part[behind, HB:] + r.tgq[1].astype(F32)).astype(BF)
    y_copy(tgy.at[behind, 1], tgr.at[1, 1], r.tg_r.at[0], behind)


    got(r.mland.at[:, pl.ds(0, Y - 1)], r.mm_r.at[0])
    for tile in range(Y * T // 2):
        top, bottom = whole(lambda yy, t: r.mland[t, yy], tile)
        r.mixed_v[0:HB, tile * CW : (tile + 1) * CW] = top.astype(BF)
        r.mixed_v[HB:BLK, tile * CW : (tile + 1) * CW] = bottom.astype(BF)

    row = lax.broadcasted_iota(jnp.int32, (Y * 16, RB), 0)
    col = lax.broadcasted_iota(jnp.int32, (Y * 16, RB), 1)
    spread = jnp.zeros((Y * 16, RB), F32)
    for a in range(Y):
        hit = (col >= R * a) & (col < R * (a + 1)) & (row - col == (16 - R) * a)
        spread = jnp.where(hit, 1.0, spread)
    spread = spread.astype(BF)
    for t in range(T):
        if t < T - 1:
            got(zland.at[t, pl.ds(0, Z - 1)], r.wz_r.at[t])
            parts = [zland[t, i] for i in range(Z)]
        else:
            got(r.wga.at[pl.ds(0, near_count)], r.wa_r.at[0])
            parts = [r.wga[zs_to[k] * X + i] for k in near_z for i in range(X)]
            if far_z:
                got(zland.at[t, pl.ds(0, len(far_z))], r.wz_r.at[t])
                parts += [zland[t, zs_to[k]] for k in far_z]
        total = parts[0].astype(F32)
        for block in parts[1:]:
            total = total + block.astype(F32)
        r.ymsg[:, t] = dot(spread, total.astype(BF)).astype(BF).reshape(Y, 16, CW)
    y_send(lambda to: r.ymsg.at[to], r.yland, r.few_s.at[1], r.wb_r)
    r.yland[y] = r.ymsg[y]

    stores = []

    def store(src, dst):
        copy = pltpu.make_async_copy(src, dst, r.in_s.at[len(stores)])
        copy.start()
        stores.append(copy)

    store(r.mixed_v, r.mixed_out)

    sent(tokbuf.at[0], r.ts_s.at[0])
    y_sent(tokbuf.at[0], r.ty_s.at[0])
    y_sent(r.wmsg, r.few_s.at[0])
    for i in range(2):
        sent(r.rbuf.at[pl.ds(0, Y - 1), 0], r.few_s.at[0])
        sent(r.lbuf.at[pl.ds(0, Y - 1), 0], r.few_s.at[0])
    y_sent(r.cmsg, r.few_s.at[0])
    for t in range(T):
        if t == T - 1:
            sent(wbuf.at[t, pl.ds(0, Z - 1)], r.gz_s.at[0])
            sent(wbuf.at[t, 0, pl.ds(0, X - 1)], r.gx_s.at[0])
        else:
            sent(wbuf.at[t, pl.ds(0, Z - 1), 0], r.gz_s.at[0])
            for i in range(X - 1):
                sent(wbuf.at[t, :, i], r.gx_s.at[0])
        sent(ext.at[t, pl.ds(0, 8)], r.few_s.at[0])
        sent(extg.at[t, pl.ds(0, 8)], r.few_s.at[0])
        sent(r.a1s.at[t, pl.ds(0, NG - 1)], r.a_s.at[0])
        sent(r.a2s.at[t, pl.ds(0, NG - 1)], r.a_s.at[0])
        if t < T - 1:
            for i in range(X - 1):
                sent(wgs.at[t, :, i], r.wx_s.at[t])
            sent(zland.at[t, pl.ds(0, Z - 1)], r.wz_s.at[0])
        else:
            sent(r.wga.at[pl.ds(0, near_count)], r.wx_s.at[t])
            if far_z:
                sent(r.wga.at[pl.ds(0, (X - 1) * len(far_z))], r.wx_s.at[t])
                sent(zland.at[t, pl.ds(0, len(far_z))], r.wz_s.at[0])
    sent(tgs, r.tgs_s.at[0])
    y_sent(tgs, r.tg_s.at[0])
    sent(r.kgx.at[pl.ds(0, X - 1)], r.few_s.at[1])
    sent(kgz.at[pl.ds(0, Z - 1)], r.few_s.at[1])
    for t in range(T):
        sent(r.mmsg.at[t, pl.ds(0, Y - 1)], r.few_s.at[1])
    y_sent(r.rgs, r.few_s.at[1])
    y_sent(r.lgs, r.few_s.at[1])

    got(r.rgc.at[1], r.fc_r.at[0])
    r.rg_v[0] = r.rgc[0].astype(F32) + r.rgc[1].astype(F32)
    store(r.rg_v, r.rg_out)
    got(r.lgc.at[1], r.fc_r.at[1])
    r.lg_v[0] = r.lgc[0].astype(F32) + r.lgc[1].astype(F32)
    store(r.lg_v, r.lg_out)
    y_got(kgy, r.ky_r)
    for tile in range(Y * T // 2):
        u, v = whole(lambda yy, t: kgy[yy, t], tile)
        r.cug_v[:, tile * CW : (tile + 1) * CW] = u[0:3]
        r.cvg_v[:, tile * CW : (tile + 1) * CW] = v[0:3]
    store(r.cug_v, r.cug_out)
    store(r.cvg_v, r.cvg_out)
    got(tgr, r.tg_r.at[0])
    for h in range(2):
        total = r.tg_part[y, h * HB : (h + 1) * HB] + tgr[0, h].astype(F32) + tgr[1, h].astype(F32)
        r.tg_v[h * HB : (h + 1) * HB, :] = total.astype(BF)
    store(r.tg_v, r.tg_out)
    y_got(r.yland, r.wb_r)
    for tile in range(Y * T // 2):
        u, v = whole(lambda yy, t: r.yland[yy, t], tile)
        r.pug_v[:, tile * CW : (tile + 1) * CW] = u[0:R]
        r.pvg_v[:, tile * CW : (tile + 1) * CW] = v[0:R]
    store(r.pug_v, r.pug_out)
    store(r.pvg_v, r.pvg_out)
    for i in range(2):
        sent(r.rgc.at[0], r.few_s.at[1])
    y_sent(r.ymsg, r.few_s.at[1])
    y_sent(kgy, r.few_s.at[1])
    for copy in stores:
        copy.wait()


def layer(Z, X, tokens, cotangent, proj_u, proj_v, right_factor, left_factor, conv_u, conv_v):
    BLK, chans = tokens.shape
    R = proj_u.shape[0]
    NG = Z * X
    CW = 2 * (chans // (Y * T))
    HB = BLK // 2
    N = Y * BLK
    RB = Y * R
    ins = dict(
        tok_in=tokens,
        cot_in=cotangent,
        pu_in=proj_u,
        pv_in=proj_v,
        rf_in=right_factor,
        lf_in=left_factor,
        cu_in=conv_u,
        cv_in=conv_v,
    )
    shape = jax.ShapeDtypeStruct
    outs = dict(
        mixed_out=shape(tokens.shape, BF),
        tg_out=shape(tokens.shape, BF),
        pug_out=shape(proj_u.shape, F32),
        pvg_out=shape(proj_v.shape, F32),
        rg_out=shape(right_factor.shape, F32),
        lg_out=shape(left_factor.shape, F32),
        cug_out=shape(conv_u.shape, F32),
        cvg_out=shape(conv_v.shape, F32),
    )
    scratch = dict(
        mixed_v=(tokens.shape, BF),
        tg_v=(tokens.shape, BF),
        pug_v=(proj_u.shape, F32),
        pvg_v=(proj_v.shape, F32),
        rg_v=(right_factor.shape, F32),
        lg_v=(left_factor.shape, F32),
        cug_v=(conv_u.shape, F32),
        cvg_v=(conv_v.shape, F32),
        pu=(proj_u.shape, BF),
        pv=(proj_v.shape, BF),
        cot=(cotangent.shape, BF),
        cu=(conv_u.shape, F32),
        cv=(conv_v.shape, F32),
        wpad=((2, 16, chans), F32),
        kpad=((2, 8, chans), F32),
        kk=((T, 8, CW), F32),
        wmsg=((Y, T, 16, CW), BF),
        wland=((Y, T, 16, CW), BF),
        cmsg=((Y, T, HB, CW), BF),
        cland=((Y, T, HB, CW), BF),
        tokbuf=((2, Y, 2, HB, chans), BF),
        rbuf=((Y, 2, HB, BLK), BF),
        lbuf=((Y, 2, HB, BLK), BF),
        rt=((Y, BLK, BLK), BF),
        lt=((Y, 2 * BLK, BLK), BF),
        wbuf=((T, Z, X, RB, CW), BF),
        to_msg1=((N, N), BF),
        from_msg1=((N, N), BF),
        to_msg2=((N, N), BF),
        from_msg2=((N, N), BF),
        cot2=((T, N, CW), F32),
        ext=((T, N + 8, CW), F32),
        extg=((T, N + 8, CW), F32),
        cvs=((T, N, CW), F32),
        zs=((T, N, CW), F32),
        ccb=((T, Y, BLK, CW), BF),
        gpb=((T, Y, BLK, CW), BF),
        vb=((N, CW), BF),
        xb=((T, N, CW), BF),
        a1s=((T, NG, 16, CW), BF),
        a1r=((T, NG, 16, CW), BF),
        a2s=((T, NG, 16, CW), BF),
        a2r=((T, NG, 16, CW), BF),
        tokt=((Z, X * RB, N), BF),
        lgs=((Y, BLK, BLK), BF),
        lgl=((Y, BLK, BLK), BF),
        lgc=((2, BLK, BLK), BF),
        rgs=((Y, BLK, BLK), BF),
        rgl=((Y, BLK, BLK), BF),
        rgc=((2, BLK, BLK), BF),
        mmsg=((T, Y, HB, CW), BF),
        mland=((T, Y, HB, CW), BF),
        kgs=((T, 8, CW), F32),
        kgx=((X, T, 8, CW), F32),
        kgz_own=((T, 8, CW), F32),
        kgz=((Z, T, 8, CW), F32),
        kgy_own=((T, 8, CW), F32),
        kgy=((Y, T, 8, CW), F32),
        tg_part=((Y, BLK, chans), F32),
        tgs=((Y, BLK, chans), BF),
        tgl=((Y, BLK, chans), BF),
        tgy=((Y, 2, HB, chans), BF),
        tgq=((2, HB, chans), BF),
        tgr=((2, 2, HB, chans), BF),
        wgs=((T, Z, X, RB, CW), BF),
        wgx=((T, Z, X, RB, CW), BF),
        wgq=((Z, RB, CW), BF),
        wga=((NG, RB, CW), BF),
        zsend=((T, Z, RB, CW), BF),
        zland=((T, Z, RB, CW), BF),
        ymsg=((Y, T, 16, CW), BF),
        yland=((Y, T, 16, CW), BF),
    )
    one = (1,)
    sems = dict(
        in_s=(11,),
        ts_s=one,
        ts_r=one,
        ty_s=one,
        ty_r=(Y, 2),
        gz_s=one,
        gz_r=(T, Z),
        gx_s=one,
        a_s=one,
        few_s=(2,),
        gx_r=(T,),
        h_r=(T,),
        a1_r=(T,),
        a2_r=(T,),
        wx_s=(T,),
        wq_r=(Z,),
        wz_s=one,
        wz_r=(T,),
        wa_r=one,
        kx_r=one,
        kz_r=one,
        tgs_s=one,
        tgs_r=(Y,),
        fc_r=(2,),
        wy_r=one,
        rf_r=(2,),
        cy_r=one,
        lf_r=(2,),
        lg_r=one,
        rg_r=one,
        mm_r=one,
        ky_r=one,
        tg_s=one,
        tg_r=one,
        tq_r=(2,),
        wb_r=one,
    )
    names = list(ins) + list(outs) + list(scratch) + list(sems)

    def body(*refs):
        kernel(Z, X, types.SimpleNamespace(**dict(zip(names, refs))))

    hbm = pl.BlockSpec(memory_space=pltpu.HBM)
    results = pl.pallas_call(
        body,
        out_shape=list(outs.values()),
        in_specs=[hbm] * len(ins),
        out_specs=[hbm] * len(outs),
        scratch_shapes=[pltpu.VMEM(sh, dt) for sh, dt in scratch.values()]
        + [pltpu.SemaphoreType.DMA(sh) for sh in sems.values()],
        compiler_params=pltpu.CompilerParams(
            collective_id=0, has_side_effects=True, vmem_limit_bytes=63 * 1024 * 1024
        ),
    )(*ins.values())

    count = len(outs)

    def write(*refs):
        froms, tos, held = refs[:count], refs[count : 2 * count], refs[2 * count : 3 * count]
        into, out_of = refs[3 * count :]
        first = [pltpu.make_async_copy(froms[i], held[i], into.at[i]) for i in range(count)]
        second = [pltpu.make_async_copy(held[i], tos[i], out_of.at[i]) for i in range(count)]
        for copy in first:
            copy.start()
        for before, after in zip(first, second):
            before.wait()
            after.start()
        for copy in second:
            copy.wait()

    return pl.pallas_call(
        write,
        out_shape=list(outs.values()),
        in_specs=[hbm] * count,
        out_specs=[hbm] * count,
        scratch_shapes=[pltpu.VMEM(o.shape, o.dtype) for o in outs.values()]
        + [pltpu.SemaphoreType.DMA((count,))] * 2,
    )(*results)


def solution(mesh):
    groups = mesh.shape["seq"] // Y
    specs = (
        P("seq", "ch"),
        P("seq", "ch"),
        P("seq", "ch"),
        P("seq", "ch"),
        P("seq", None, None),
        P("seq", None, None),
        P(None, "ch"),
        P(None, "ch"),
    )
    return jax.shard_map(
        functools.partial(layer, groups // X, X),
        mesh=mesh,
        in_specs=specs,
        out_specs=specs,
        check_vma=False,
    )
```

```python
import functools
import types

import jax
import jax.numpy as jnp
from jax import lax
from jax.experimental import pallas as pl
from jax.experimental.pallas import tpu as pltpu
from jax.sharding import PartitionSpec as P

MESH = pl.DeviceIdType.MESH
BF = jnp.bfloat16
F32 = jnp.float32
Y = 4
X = 4
T = 3


def dot(a, b):
    return jnp.dot(a, b, preferred_element_type=F32)


def dot_nt(a, b):
    return lax.dot_general(a, b, (((1,), (1,)), ((), ())), preferred_element_type=F32)


def transposed(a):
    return a.astype(F32).T.astype(BF)


def by_distance(n):
    return sorted(range(1, n), key=lambda k: (min(k, n - k), k))


def kernel(Z, X, r):
    NG = Z * X
    BLK, chans = r.tok_in.shape
    HC = chans // (Y * T)
    CW = 2 * HC
    HB = BLK // 2
    N = Y * BLK
    R = r.pu_in.shape[0]
    RB = Y * R
    half = Z // 2

    s = lax.axis_index("seq")
    c = lax.axis_index("ch")
    g = s // Y
    y = lax.rem(s, Y)
    z = g // X
    x = lax.rem(g, X)
    sib = 1 - c

    def dev(gg, yy):
        return gg * Y + yy

    def in_u(shape):
        return lax.broadcasted_iota(jnp.int32, shape, len(shape) - 1) < HC

    def pick(u, v):
        return jnp.where(in_u(u.shape), u, v)

    def swap(v):
        return pltpu.roll(v, HC, 1)

    def rc(src, dst, send_sem, recv_sem, seq, ch):
        return pltpu.make_async_remote_copy(
            src_ref=src,
            dst_ref=dst,
            send_sem=send_sem,
            recv_sem=recv_sem,
            device_id=(seq, ch),
            device_id_type=MESH,
        )

    def got(ref, sem):
        rc(ref, ref, sem, sem, s, c).wait_recv()

    def sent(ref, sem):
        rc(ref, ref, sem, sem, s, c).wait_send()

    def part(u, v, yy, t):
        q = yy * T + t
        uq = u[:, q // 2 * CW : (q // 2 + 1) * CW]
        vq = v[:, q // 2 * CW : (q // 2 + 1) * CW]
        return pick(uq, swap(vq)) if q % 2 == 0 else pick(swap(uq), vq)

    def whole(land, tile):
        q = 2 * tile
        a = land(q // T, q % T).astype(F32)
        b = land((q + 1) // T, (q + 1) % T).astype(F32)
        return pick(a, swap(b)), pick(swap(a), b)

    def y_send(src_of, dst, send, recv):
        for k in (2, 1, 3):
            to = lax.rem(y + k, Y)
            rc(src_of(to), dst.at[y], send, recv.at[0], dev(g, to), c).start()

    def y_got(dst, recv):
        got(dst.at[pl.ds(0, Y - 1)], recv.at[0])

    def y_sent(like, send):
        sent(like.at[pl.ds(0, Y - 1)], send)

    def load(src, dst, i):
        copy = pltpu.make_async_copy(src, dst, r.in_s.at[i])
        copy.start()
        return copy

    tokbuf = r.tokbuf
    in_pu = load(r.pu_in, r.pu, 0)
    in_pv = load(r.pv_in, r.pv, 1)
    in_tok = [load(r.tok_in.at[pl.ds(h * HB, HB)], tokbuf.at[c, y, h], 2 + 8 * h) for h in range(2)]
    in_cot = load(r.cot_in, r.cot, 3)
    in_cu = load(r.cu_in, r.cu, 4)
    in_cv = load(r.cv_in, r.cv, 5)
    in_factors = [
        load(a.at[0, pl.ds(h * HB, HB)], b.at[y, h], 6 + 2 * i + h)
        for i, (a, b) in enumerate(((r.rf_in, r.rbuf), (r.lf_in, r.lbuf)))
        for h in range(2)
    ]

    barrier = pltpu.get_barrier_semaphore()

    for k in (1, 2, 3):
        pl.semaphore_signal(
            barrier, inc=1, device_id=(dev(g, lax.rem(y + k, Y)), c), device_id_type=MESH
        )
    pl.semaphore_signal(barrier, inc=1, device_id=(s, sib), device_id_type=MESH)
    for dz in range(Z):
        for dx in range(X):
            if dz or dx:
                to = lax.rem(z + dz, Z) * X + lax.rem(x + dx, X)
                pl.semaphore_signal(barrier, inc=1, device_id=(dev(to, y), c), device_id_type=MESH)

    wpad = r.wpad
    wpad[...] = jnp.zeros_like(wpad)
    kpad = r.kpad
    kpad[...] = jnp.zeros_like(kpad)
    in_pu.wait()
    in_pv.wait()
    wpad[0, 0:R, :] = r.pu[...].astype(F32)
    wpad[1, 0:R, :] = r.pv[...].astype(F32)
    for yy in range(Y):
        for t in range(T):
            r.wmsg[yy, t] = part(wpad[0], wpad[1], yy, t).astype(BF)
    pl.semaphore_wait(barrier, NG - 1 + Y)

    y_send(lambda to: r.wmsg.at[to], r.wland, r.few_s.at[0], r.wy_r)
    for copy in in_tok:
        copy.wait()
    rc(tokbuf.at[c, y], tokbuf.at[c, y], r.ts_s.at[0], r.ts_r.at[0], s, sib).start()

    def factor_send(buf, send, recv):
        for k in (2, 1, 3):
            to = lax.rem(y + k, Y)
            rc(buf.at[y, c], buf.at[y, c], send, recv.at[0], dev(g, to), c).start()

    def factor_hand_on(buf, send, recv):
        got(buf.at[pl.ds(0, Y - 1), 0], recv.at[0])
        for k in (1, 3, 2):
            of = lax.rem(y + k, Y)
            rc(buf.at[of, c], buf.at[of, c], send, recv.at[1], s, sib).start()

    def factor(buf, recv):
        got(buf.at[pl.ds(0, Y - 1), 0], recv.at[1])
        return [buf[j].reshape(BLK, BLK) for j in range(Y)]

    r.wland[y] = r.wmsg[y]
    for copy in in_factors:
        copy.wait()
    in_cot.wait()
    cot = r.cot[...].astype(F32)
    for yy in range(Y):
        for t in range(T):
            r.cmsg[yy, t] = part(cot[:HB], cot[HB:], yy, t).astype(BF)
    r.cland[y] = r.cmsg[y]

    row = lax.broadcasted_iota(jnp.int32, (RB, Y * 16), 0)
    col = lax.broadcasted_iota(jnp.int32, (RB, Y * 16), 1)
    sel = jnp.zeros((RB, Y * 16), F32)
    for a in range(Y):
        hit = (row >= R * a) & (row < R * (a + 1)) & (col - row == (16 - R) * a)
        sel = jnp.where(hit, 1.0, sel)
    sel = sel.astype(BF)


    wbuf = r.wbuf
    def along_x(t, of):
        for k in (2, 1, 3):
            to = lax.rem(x + k, X)
            block = wbuf.at[t, of, x]
            rc(block, block, r.gx_s.at[0], r.gx_r.at[t], dev(z * X + to, y), c).start()

    y_got(r.wland, r.wy_r)

    ahead, across, behind = (lax.rem(y + k, Y) for k in (1, 2, 3))

    def token_copy(of, h, to):
        block = tokbuf.at[c, of, h]
        rc(block, block, r.ty_s.at[0], r.ty_r.at[of, h], dev(g, to), c).start()

    def token_hand_on(of, h):
        block = tokbuf.at[c, of, h]
        got(block, r.ty_r.at[of, h])
        rc(block, block, r.ts_s.at[0], r.ts_r.at[0], s, sib).start()

    token_copy(y, 0, ahead)
    token_copy(y, 1, behind)
    token_copy(y, 1, ahead)
    token_copy(y, 0, behind)

    for t in range(T):
        wbuf[t, z, x] = dot(sel, r.wland[:, t].reshape(Y * 16, CW)).astype(BF)
        block = wbuf.at[t, z, x]
        if t < T - 1:
            for k in reversed(by_distance(Z)):
                to = lax.rem(z + k, Z)
                rc(block, block, r.gz_s.at[0], r.gz_r.at[t, z], dev(to * X + x, y), c).start()
        along_x(t, z)


    out_i = lax.broadcasted_iota(jnp.int32, (N, N), 0)
    in_i = lax.broadcasted_iota(jnp.int32, (N, N), 1)

    def hits(a, b):
        return jnp.where(a == b, 1.0, 0.0).astype(BF)

    def swapped_index(v):
        return lax.rem(v // 4, 4) * BLK + (v // 16) * 4 + lax.rem(v, 4)

    def rotated_index(v):
        return lax.rem(v, 4) * BLK + (v // 16) * 4 + lax.rem(v // 4, 4)

    r.to_msg1[...] = hits(in_i, rotated_index(out_i))
    r.from_msg1[...] = hits(out_i, swapped_index(in_i))
    r.to_msg2[...] = hits(in_i, swapped_index(out_i))
    r.from_msg2[...] = hits(out_i, rotated_index(in_i))

    in_cu.wait()
    in_cv.wait()
    kpad[0, 0:3, :] = r.cu[...]
    kpad[1, 0:3, :] = r.cv[...]
    for t in range(T):
        kt = part(kpad[0], kpad[1], 0, t)
        for yy in range(1, Y):
            kt = jnp.where(y == yy, part(kpad[0], kpad[1], yy, t), kt)
        r.kk[t] = kt

    def conv(t, first, second, third):
        return r.kk[t, 0:1] * first + r.kk[t, 1:2] * second + r.kk[t, 2:3] * third

    def gather_x(t):
        for k in by_distance(Z):
            of = lax.rem(z + k, Z)
            got(wbuf.at[t, of, x], r.gz_r.at[t, of])
            along_x(t, of)

    def gather_z(t):
        got(wbuf.at[t, z, pl.ds(0, X - 1)], r.gx_r.at[t])
        for k in reversed(by_distance(Z)):
            to = lax.rem(z + k, Z)
            rc(wbuf.at[t, z], wbuf.at[t, z], r.gz_s.at[0], r.gz_r.at[t, z], dev(to * X + x, y), c).start()

    ext, cvs, ccb, vb, xb = r.ext, r.cvs, r.ccb, r.vb, r.xb
    cot2, extg, zs, gpb = r.cot2, r.extg, r.zs, r.gpb

    def project(t):
        if t == T - 1:
            for k in by_distance(Z):
                of = lax.rem(z + k, Z)
                got(wbuf.at[t, of], r.gz_r.at[t, of])
        else:
            got(wbuf.at[t, :, pl.ds(0, X - 1)], r.gx_r.at[t])
        w_own = wbuf[t, pl.ds(c * half, half)].reshape(chans, CW)
        w_sib = wbuf[t, pl.ds(sib * half, half)].reshape(chans, CW)
        if t == 0:
            extg[t, 0:N, :] = dot(tokbuf[c].reshape(N, chans), w_own)
            got(tokbuf.at[0], r.ts_r.at[0])

        def rows(first, count):
            at = slice(first * BLK, (first + count) * BLK)
            other = dot(tokbuf[sib, first : first + count].reshape(count * BLK, chans), w_sib)
            if t == 0:
                pre = extg[t, at, :] + other
            else:
                pre = dot(tokbuf[c, first : first + count].reshape(count * BLK, chans), w_own) + other
            ext[t, 8 + first * BLK : 8 + (first + count) * BLK, :] = pre.astype(BF).astype(F32)

        rows(Y - 1, 1)
        rc(ext.at[t, pl.ds(N, 8)], ext.at[t, pl.ds(0, 8)], r.few_s.at[0], r.h_r.at[t], dev(lax.rem(g + 1, NG), y), c).start()
        rows(0, Y - 1)

    zs_to = [lax.rem(z + k, Z) for k in range(Z)]
    xs_to = [lax.rem(x + k, X) for k in range(X)]
    far_first = sorted(
        [(dz, dx) for dz in range(Z) for dx in range(X) if dz or dx],
        key=lambda d: -(min(d[0], Z - d[0]) + min(d[1], X - d[1])),
    )

    def exchange(src, dst, send, recv):
        for dz, dx in far_first:
            to = zs_to[dz] * X + xs_to[dx]
            rc(src.at[to], dst.at[g], send, recv, dev(to, y), c).start()
        dst[g] = src[g]

    def mix_rows(t):
        got(ext.at[t, pl.ds(0, 8)], r.h_r.at[t])

        @pl.when(g == 0)
        def _():
            ext[t, 0:8, :] = jnp.zeros((8, CW), F32)

        for j in range(Y):
            at = j * BLK
            m = r.cland[j, t].astype(F32)
            cot2[t, at : at + HB, :] = swap(m)
            cot2[t, at + HB : at + BLK, :] = m
            cv = conv(
                t,
                ext[t, 8 + at : 8 + at + BLK, :],
                ext[t, 7 + at : 7 + at + BLK, :],
                ext[t, 6 + at : 6 + at + BLK, :],
            )
            cvs[t, at : at + BLK, :] = cv
            cb = cv.astype(BF)
            ccb[t, j] = cb
            vb[at : at + BLK, :] = pick(dot(r.rbuf[j].reshape(BLK, BLK), cb), cot2[t, at : at + BLK, :] * cv).astype(BF)
        r.a1s[t] = dot(r.to_msg1[...], vb[...]).astype(BF).reshape(NG, 16, CW)
        exchange(r.a1s.at[t], r.a1r.at[t], r.a_s.at[0], r.a1_r.at[t])

    def mix_columns(t):
        got(r.a1r.at[t, pl.ds(0, NG - 1)], r.a1_r.at[t])
        xb[t] = dot(r.from_msg1[...], r.a1r[t].reshape(N, CW)).astype(BF)
        for i in range(Y):
            xi = xb[t, i * BLK : (i + 1) * BLK, :]
            both = dot(r.lt[i], xi)
            vb[i * BLK : (i + 1) * BLK, :] = pick(both[:BLK], both[BLK:]).astype(BF)
        r.a2s[t] = dot(r.to_msg2[...], vb[...]).astype(BF).reshape(NG, 16, CW)
        exchange(r.a2s.at[t], r.a2r.at[t], r.a_s.at[0], r.a2_r.at[t])

    def back_rows(t):
        got(r.a2r.at[t, pl.ds(0, NG - 1)], r.a2_r.at[t])
        zs[t] = swap(dot(r.from_msg2[...], r.a2r[t].reshape(N, CW)))
        for j in range(Y):
            at = j * BLK
            zj = zs[t, at : at + BLK, :]
            extg[t, at : at + BLK, :] = pick(dot(r.rt[j], zj.astype(BF)), cot2[t, at : at + BLK, :] * zj)
            m = cvs[t, at : at + BLK, :] * zj
            r.mmsg[t, j] = pick(swap(m[:HB]), m[HB:]).astype(BF)
        rc(extg.at[t, pl.ds(0, 8)], extg.at[t, pl.ds(N, 8)], r.few_s.at[0], r.h_r.at[t], dev(lax.rem(g + NG - 1, NG), y), c).start()
        for k in (2, 1, 3):
            to = lax.rem(y + k, Y)
            rc(r.mmsg.at[t, to], r.mland.at[t, y], r.few_s.at[1], r.mm_r.at[0], dev(g, to), c).start()
        r.mland[t, y] = r.mmsg[t, y]

    wgs, wgq, wgx, zsend, zland = r.wgs, r.wgq, r.wgx, r.zsend, r.zland
    z_order = list(reversed(by_distance(Z))) + [0]

    def gate_back(t):
        got(extg.at[t, pl.ds(N, 8)], r.h_r.at[t])

        @pl.when(g == NG - 1)
        def _():
            extg[t, N : N + 8, :] = jnp.zeros((8, CW), F32)

        for j in range(Y):
            at = j * BLK
            gpb[t, j] = conv(
                t,
                extg[t, at : at + BLK, :],
                extg[t, at + 1 : at + 1 + BLK, :],
                extg[t, at + 2 : at + 2 + BLK, :],
            ).astype(BF)

    far_z = [k for k in z_order if min(k, Z - k) > 2]
    near_z = [k for k in z_order if k not in far_z]
    near_count = X * len(near_z) - 1

    def weight_grads(t):
        gp = gpb[t].reshape(N, CW)
        for i, k in enumerate(z_order):
            to = lax.rem(z + k, Z)
            wgs[t, to] = dot(r.tokt[to], gp).astype(BF).reshape(X, RB, CW)
            if t == T - 1 and k not in far_z:
                for kx in (2, 1, 3, 0):
                    if k or kx:
                        at = to * X + xs_to[kx]
                        rc(wgs.at[t, to, xs_to[kx]], r.wga.at[g], r.wx_s.at[t], r.wa_r.at[0], dev(at, y), c).start()
            elif t == 0:
                ahead, behind, across = x_ways(i)
                rc(wgs.at[t, to, across], wgq.at[to], r.wx_s.at[t], r.wq_r.at[to], dev(z * X + ahead, y), c).start()
                rc(wgs.at[t, to, behind], wgx.at[t, to, 0], r.wx_s.at[t], r.gz_r.at[t, to], dev(z * X + behind, y), c).start()
            else:
                for kx in (2, 1, 3):
                    rc(wgs.at[t, to, xs_to[kx]], wgx.at[t, to, x], r.wx_s.at[t], r.gz_r.at[t, to], dev(z * X + xs_to[kx], y), c).start()
                wgx[t, to, x] = wgs[t, to, x]
        if t == T - 1:
            r.wga[g] = wgs[t, z, x]

    def x_ways(i):
        d = 1 if i % 2 == 0 else X - 1
        return lax.rem(x + d, X), lax.rem(x + X - d, X), lax.rem(x + 2, X)

    def weight_relay():
        t = 0
        for i, k in enumerate(z_order):
            to = lax.rem(z + k, Z)
            ahead = x_ways(i)[0]
            got(wgq.at[to], r.wq_r.at[to])
            wgs[t, to, ahead] = (wgs[t, to, ahead].astype(F32) + wgq[to].astype(F32)).astype(BF)
            rc(wgs.at[t, to, ahead], wgx.at[t, to, 1], r.wx_s.at[t], r.gz_r.at[t, to], dev(z * X + ahead, y), c).start()

    def sum4(land):
        return (land[0].astype(F32) + land[1].astype(F32)) + (land[2].astype(F32) + land[3].astype(F32))

    def weight_sums(t):
        for k in z_order if t < T - 1 else far_z:
            to = lax.rem(z + k, Z)
            if t:
                got(wgx.at[t, to, pl.ds(0, X - 1)], r.gz_r.at[t, to])
                zsend[t, to] = sum4(wgx[t, to]).astype(BF)
            else:
                got(wgx.at[t, to, pl.ds(0, 2)], r.gz_r.at[t, to])
                zsend[t, to] = (
                    wgs[t, to, x].astype(F32) + wgx[t, to, 0].astype(F32) + wgx[t, to, 1].astype(F32)
                ).astype(BF)
            if k:
                rc(zsend.at[t, to], zland.at[t, z], r.wz_s.at[0], r.wz_r.at[t], dev(to * X + x, y), c).start()
        if t < T - 1:
            zland[t, z] = zsend[t, z]

    def left_grads():
        for i in range(Y):
            grads, cols = [], []
            for t in range(T):
                xi = xb[t, i * BLK : (i + 1) * BLK, :]
                xs = swap(xi.astype(F32))
                grads.append(pick(xs, jnp.zeros_like(xs)).astype(BF))
                cols.append(xi)
            r.lgs[i] = dot_nt(jnp.concatenate(grads, axis=1), jnp.concatenate(cols, axis=1)).astype(BF)
        y_send(lambda to: r.lgs.at[to], r.lgl, r.few_s.at[1], r.lg_r)
        r.lgl[y] = r.lgs[y]

    def right_grads():
        for j in range(Y):
            rows = []
            for t in range(T):
                zj = zs[t, j * BLK : (j + 1) * BLK, :]
                rows.append(pick(zj, jnp.zeros_like(zj)).astype(BF))
            r.rgs[j] = dot_nt(
                jnp.concatenate(rows, axis=1), jnp.concatenate([ccb[t, j] for t in range(T)], axis=1)
            ).astype(BF)
        y_send(lambda to: r.rgs.at[to], r.rgl, r.few_s.at[1], r.rg_r)
        r.rgl[y] = r.rgs[y]

    kgs = r.kgs

    def conv_grads():
        kgs[...] = jnp.zeros_like(kgs)
        for t in range(T):
            for lag in range(3):
                kgs[t, lag : lag + 1, :] = jnp.sum(
                    extg[t, 0:N, :] * ext[t, 8 - lag : 8 - lag + N, :], axis=0, keepdims=True
                )
        for k in (2, 1, 3):
            to = lax.rem(x + k, X)
            rc(kgs, r.kgx.at[x], r.few_s.at[1], r.kx_r.at[0], dev(z * X + to, y), c).start()
        r.kgx[x] = kgs[...]

    tgs, tgl, tgy, tgr = r.tgs, r.tgl, r.tgy, r.tgr

    def rows_of(at, chunks):
        return jnp.concatenate([gpb[t, at] for t in chunks], axis=1)

    def half_of(cc, chunks):
        return jnp.concatenate(
            [wbuf[t, pl.ds(cc * half, half)].reshape(chans, CW) for t in chunks], axis=1
        )

    early, late = list(range(T - 1)), [T - 1]

    def token_grads(out, cc, chunks):
        w = half_of(cc, chunks)
        for k in (2, 1, 3, 0):
            of = lax.rem(y + k, Y)
            out[of] = dot_nt(rows_of(of, chunks), w)

    gather_x(0)
    token_hand_on(behind, 0)
    token_copy(behind, 0, ahead)
    token_hand_on(ahead, 1)
    token_copy(ahead, 1, behind)
    factor_send(r.rbuf, r.few_s.at[0], r.rf_r)
    y_send(lambda to: r.cmsg.at[to], r.cland, r.few_s.at[0], r.cy_r)
    factor_send(r.lbuf, r.few_s.at[0], r.lf_r)
    gather_z(2)
    gather_x(1)
    token_hand_on(behind, 1)
    token_hand_on(ahead, 0)
    token_hand_on(across, 0)
    token_hand_on(across, 1)
    factor_hand_on(r.rbuf, r.few_s.at[0], r.rf_r)
    project(0)
    project(1)
    y_got(r.cland, r.cy_r)
    right = factor(r.rbuf, r.rf_r)
    mix_rows(0)
    project(2)
    mix_rows(1)
    factor_hand_on(r.lbuf, r.few_s.at[0], r.lf_r)
    for j in range(Y):
        r.rt[j] = transposed(right[j])
    for i in range(2):
        r.tokt[i * half : (i + 1) * half] = transposed(tokbuf[i].reshape(N, chans)).reshape(half, X * RB, N)
    mix_rows(2)
    left = factor(r.lbuf, r.lf_r)
    for j in range(Y):
        r.lt[j, 0:BLK] = left[j]
        r.lt[j, BLK:] = transposed(left[j])
    mix_columns(0)
    mix_columns(1)
    mix_columns(2)
    back_rows(0)
    left_grads()
    back_rows(1)
    gate_back(0)
    weight_grads(0)
    y_got(r.lgl, r.lg_r)
    r.lgc[0] = sum4(r.lgl).astype(BF)
    rc(r.lgc.at[0], r.lgc.at[1], r.few_s.at[1], r.fc_r.at[1], s, sib).start()
    back_rows(2)
    conv_grads()
    gate_back(1)
    weight_grads(1)
    token_grads(r.tg_part, sib, early)
    weight_relay()
    gate_back(2)

    w_sib = half_of(sib, late)
    for k in (2, 1, 3, 0):
        of = lax.rem(y + k, Y)
        tgs[of] = (r.tg_part[of] + dot_nt(rows_of(of, late), w_sib)).astype(BF)
        rc(tgs.at[of], tgl.at[of], r.tgs_s.at[0], r.tgs_r.at[of], s, sib).start()
    got(r.kgx.at[pl.ds(0, X - 1)], r.kx_r.at[0])
    kgz, kgz_own = r.kgz, r.kgz_own
    kgz_own[...] = sum4(r.kgx)
    for k in reversed(by_distance(Z)):
        to = lax.rem(z + k, Z)
        rc(kgz_own, kgz.at[z], r.few_s.at[1], r.kz_r.at[0], dev(to * X + x, y), c).start()
    kgz[z] = kgz_own[...]

    weight_grads(2)
    right_grads()
    token_grads(r.tg_part, c, early + late)
    weight_sums(0)

    def y_copy(src, dst, recv, to):
        rc(src, dst, r.tg_s.at[0], recv, dev(g, to), c).start()

    for of in (across, ahead, behind, y):
        got(tgl.at[of], r.tgs_r.at[of])
        total = r.tg_part[of] + tgl[of].astype(F32)
        r.tg_part[of] = total
        tgy[of] = total.astype(BF).reshape(2, HB, chans)
        if of is across:
            y_copy(tgy.at[of, 0], r.tgq.at[0], r.tq_r.at[0], ahead)
            y_copy(tgy.at[of, 1], r.tgq.at[1], r.tq_r.at[1], behind)
        if of is ahead:
            y_copy(tgy.at[of, 1], tgr.at[0, 1], r.tg_r.at[0], ahead)
        if of is behind:
            y_copy(tgy.at[of, 0], tgr.at[1, 0], r.tg_r.at[0], behind)
    weight_sums(2)
    weight_sums(1)
    y_got(r.rgl, r.rg_r)
    r.rgc[0] = sum4(r.rgl).astype(BF)
    rc(r.rgc.at[0], r.rgc.at[1], r.few_s.at[1], r.fc_r.at[0], s, sib).start()
    got(kgz.at[pl.ds(0, Z - 1)], r.kz_r.at[0])
    kgy, kgy_own = r.kgy, r.kgy_own
    total = kgz[0]
    for i in range(1, Z):
        total = total + kgz[i]
    kgy_own[...] = total
    y_send(lambda to: kgy_own, kgy, r.few_s.at[1], r.ky_r)
    kgy[y] = total
    got(r.tgq.at[0], r.tq_r.at[0])
    tgy[ahead, 0] = (r.tg_part[ahead, 0:HB] + r.tgq[0].astype(F32)).astype(BF)
    y_copy(tgy.at[ahead, 0], tgr.at[0, 0], r.tg_r.at[0], ahead)
    got(r.tgq.at[1], r.tq_r.at[1])
    tgy[behind, 1] = (r.tg_part[behind, HB:] + r.tgq[1].astype(F32)).astype(BF)
    y_copy(tgy.at[behind, 1], tgr.at[1, 1], r.tg_r.at[0], behind)


    got(r.mland.at[:, pl.ds(0, Y - 1)], r.mm_r.at[0])
    for tile in range(Y * T // 2):
        top, bottom = whole(lambda yy, t: r.mland[t, yy], tile)
        r.mixed_v[0:HB, tile * CW : (tile + 1) * CW] = top.astype(BF)
        r.mixed_v[HB:BLK, tile * CW : (tile + 1) * CW] = bottom.astype(BF)

    row = lax.broadcasted_iota(jnp.int32, (Y * 16, RB), 0)
    col = lax.broadcasted_iota(jnp.int32, (Y * 16, RB), 1)
    spread = jnp.zeros((Y * 16, RB), F32)
    for a in range(Y):
        hit = (col >= R * a) & (col < R * (a + 1)) & (row - col == (16 - R) * a)
        spread = jnp.where(hit, 1.0, spread)
    spread = spread.astype(BF)
    for t in range(T):
        if t < T - 1:
            got(zland.at[t, pl.ds(0, Z - 1)], r.wz_r.at[t])
            parts = [zland[t, i] for i in range(Z)]
        else:
            got(r.wga.at[pl.ds(0, near_count)], r.wa_r.at[0])
            parts = [r.wga[zs_to[k] * X + i] for k in near_z for i in range(X)]
            if far_z:
                got(zland.at[t, pl.ds(0, len(far_z))], r.wz_r.at[t])
                parts += [zland[t, zs_to[k]] for k in far_z]
        total = parts[0].astype(F32)
        for block in parts[1:]:
            total = total + block.astype(F32)
        r.ymsg[:, t] = dot(spread, total.astype(BF)).astype(BF).reshape(Y, 16, CW)
    y_send(lambda to: r.ymsg.at[to], r.yland, r.few_s.at[1], r.wb_r)
    r.yland[y] = r.ymsg[y]

    stores = []

    def store(src, dst):
        copy = pltpu.make_async_copy(src, dst, r.in_s.at[len(stores)])
        copy.start()
        stores.append(copy)

    store(r.mixed_v, r.mixed_out)

    sent(tokbuf.at[0], r.ts_s.at[0])
    y_sent(tokbuf.at[0], r.ty_s.at[0])
    y_sent(r.wmsg, r.few_s.at[0])
    for i in range(2):
        sent(r.rbuf.at[pl.ds(0, Y - 1), 0], r.few_s.at[0])
        sent(r.lbuf.at[pl.ds(0, Y - 1), 0], r.few_s.at[0])
    y_sent(r.cmsg, r.few_s.at[0])
    for t in range(T):
        if t == T - 1:
            sent(wbuf.at[t, pl.ds(0, Z - 1)], r.gz_s.at[0])
            sent(wbuf.at[t, 0, pl.ds(0, X - 1)], r.gx_s.at[0])
        else:
            sent(wbuf.at[t, pl.ds(0, Z - 1), 0], r.gz_s.at[0])
            for i in range(X - 1):
                sent(wbuf.at[t, :, i], r.gx_s.at[0])
        sent(ext.at[t, pl.ds(0, 8)], r.few_s.at[0])
        sent(extg.at[t, pl.ds(0, 8)], r.few_s.at[0])
        sent(r.a1s.at[t, pl.ds(0, NG - 1)], r.a_s.at[0])
        sent(r.a2s.at[t, pl.ds(0, NG - 1)], r.a_s.at[0])
        if t < T - 1:
            for i in range(X - 1):
                sent(wgs.at[t, :, i], r.wx_s.at[t])
            sent(zland.at[t, pl.ds(0, Z - 1)], r.wz_s.at[0])
        else:
            sent(r.wga.at[pl.ds(0, near_count)], r.wx_s.at[t])
            if far_z:
                sent(r.wga.at[pl.ds(0, (X - 1) * len(far_z))], r.wx_s.at[t])
                sent(zland.at[t, pl.ds(0, len(far_z))], r.wz_s.at[0])
    sent(tgs, r.tgs_s.at[0])
    y_sent(tgs, r.tg_s.at[0])
    sent(r.kgx.at[pl.ds(0, X - 1)], r.few_s.at[1])
    sent(kgz.at[pl.ds(0, Z - 1)], r.few_s.at[1])
    for t in range(T):
        sent(r.mmsg.at[t, pl.ds(0, Y - 1)], r.few_s.at[1])
    y_sent(r.rgs, r.few_s.at[1])
    y_sent(r.lgs, r.few_s.at[1])

    got(r.rgc.at[1], r.fc_r.at[0])
    r.rg_v[0] = r.rgc[0].astype(F32) + r.rgc[1].astype(F32)
    store(r.rg_v, r.rg_out)
    got(r.lgc.at[1], r.fc_r.at[1])
    r.lg_v[0] = r.lgc[0].astype(F32) + r.lgc[1].astype(F32)
    store(r.lg_v, r.lg_out)
    y_got(kgy, r.ky_r)
    for tile in range(Y * T // 2):
        u, v = whole(lambda yy, t: kgy[yy, t], tile)
        r.cug_v[:, tile * CW : (tile + 1) * CW] = u[0:3]
        r.cvg_v[:, tile * CW : (tile + 1) * CW] = v[0:3]
    store(r.cug_v, r.cug_out)
    store(r.cvg_v, r.cvg_out)
    got(tgr, r.tg_r.at[0])
    for h in range(2):
        total = r.tg_part[y, h * HB : (h + 1) * HB] + tgr[0, h].astype(F32) + tgr[1, h].astype(F32)
        r.tg_v[h * HB : (h + 1) * HB, :] = total.astype(BF)
    store(r.tg_v, r.tg_out)
    y_got(r.yland, r.wb_r)
    for tile in range(Y * T // 2):
        u, v = whole(lambda yy, t: r.yland[yy, t], tile)
        r.pug_v[:, tile * CW : (tile + 1) * CW] = u[0:R]
        r.pvg_v[:, tile * CW : (tile + 1) * CW] = v[0:R]
    store(r.pug_v, r.pug_out)
    store(r.pvg_v, r.pvg_out)
    for i in range(2):
        sent(r.rgc.at[0], r.few_s.at[1])
    y_sent(r.ymsg, r.few_s.at[1])
    y_sent(kgy, r.few_s.at[1])
    for copy in stores:
        copy.wait()


def layer(Z, X, tokens, cotangent, proj_u, proj_v, right_factor, left_factor, conv_u, conv_v):
    BLK, chans = tokens.shape
    R = proj_u.shape[0]
    NG = Z * X
    CW = 2 * (chans // (Y * T))
    HB = BLK // 2
    N = Y * BLK
    RB = Y * R
    ins = dict(
        tok_in=tokens,
        cot_in=cotangent,
        pu_in=proj_u,
        pv_in=proj_v,
        rf_in=right_factor,
        lf_in=left_factor,
        cu_in=conv_u,
        cv_in=conv_v,
    )
    shape = jax.ShapeDtypeStruct
    outs = dict(
        mixed_out=shape(tokens.shape, BF),
        tg_out=shape(tokens.shape, BF),
        pug_out=shape(proj_u.shape, F32),
        pvg_out=shape(proj_v.shape, F32),
        rg_out=shape(right_factor.shape, F32),
        lg_out=shape(left_factor.shape, F32),
        cug_out=shape(conv_u.shape, F32),
        cvg_out=shape(conv_v.shape, F32),
    )
    scratch = dict(
        mixed_v=(tokens.shape, BF),
        tg_v=(tokens.shape, BF),
        pug_v=(proj_u.shape, F32),
        pvg_v=(proj_v.shape, F32),
        rg_v=(right_factor.shape, F32),
        lg_v=(left_factor.shape, F32),
        cug_v=(conv_u.shape, F32),
        cvg_v=(conv_v.shape, F32),
        pu=(proj_u.shape, BF),
        pv=(proj_v.shape, BF),
        cot=(cotangent.shape, BF),
        cu=(conv_u.shape, F32),
        cv=(conv_v.shape, F32),
        wpad=((2, 16, chans), F32),
        kpad=((2, 8, chans), F32),
        kk=((T, 8, CW), F32),
        wmsg=((Y, T, 16, CW), BF),
        wland=((Y, T, 16, CW), BF),
        cmsg=((Y, T, HB, CW), BF),
        cland=((Y, T, HB, CW), BF),
        tokbuf=((2, Y, 2, HB, chans), BF),
        rbuf=((Y, 2, HB, BLK), BF),
        lbuf=((Y, 2, HB, BLK), BF),
        rt=((Y, BLK, BLK), BF),
        lt=((Y, 2 * BLK, BLK), BF),
        wbuf=((T, Z, X, RB, CW), BF),
        to_msg1=((N, N), BF),
        from_msg1=((N, N), BF),
        to_msg2=((N, N), BF),
        from_msg2=((N, N), BF),
        cot2=((T, N, CW), F32),
        ext=((T, N + 8, CW), F32),
        extg=((T, N + 8, CW), F32),
        cvs=((T, N, CW), F32),
        zs=((T, N, CW), F32),
        ccb=((T, Y, BLK, CW), BF),
        gpb=((T, Y, BLK, CW), BF),
        vb=((N, CW), BF),
        xb=((T, N, CW), BF),
        a1s=((T, NG, 16, CW), BF),
        a1r=((T, NG, 16, CW), BF),
        a2s=((T, NG, 16, CW), BF),
        a2r=((T, NG, 16, CW), BF),
        tokt=((Z, X * RB, N), BF),
        lgs=((Y, BLK, BLK), BF),
        lgl=((Y, BLK, BLK), BF),
        lgc=((2, BLK, BLK), BF),
        rgs=((Y, BLK, BLK), BF),
        rgl=((Y, BLK, BLK), BF),
        rgc=((2, BLK, BLK), BF),
        mmsg=((T, Y, HB, CW), BF),
        mland=((T, Y, HB, CW), BF),
        kgs=((T, 8, CW), F32),
        kgx=((X, T, 8, CW), F32),
        kgz_own=((T, 8, CW), F32),
        kgz=((Z, T, 8, CW), F32),
        kgy_own=((T, 8, CW), F32),
        kgy=((Y, T, 8, CW), F32),
        tg_part=((Y, BLK, chans), F32),
        tgs=((Y, BLK, chans), BF),
        tgl=((Y, BLK, chans), BF),
        tgy=((Y, 2, HB, chans), BF),
        tgq=((2, HB, chans), BF),
        tgr=((2, 2, HB, chans), BF),
        wgs=((T, Z, X, RB, CW), BF),
        wgx=((T, Z, X, RB, CW), BF),
        wgq=((Z, RB, CW), BF),
        wga=((NG, RB, CW), BF),
        zsend=((T, Z, RB, CW), BF),
        zland=((T, Z, RB, CW), BF),
        ymsg=((Y, T, 16, CW), BF),
        yland=((Y, T, 16, CW), BF),
    )
    one = (1,)
    sems = dict(
        in_s=(11,),
        ts_s=one,
        ts_r=one,
        ty_s=one,
        ty_r=(Y, 2),
        gz_s=one,
        gz_r=(T, Z),
        gx_s=one,
        a_s=one,
        few_s=(2,),
        gx_r=(T,),
        h_r=(T,),
        a1_r=(T,),
        a2_r=(T,),
        wx_s=(T,),
        wq_r=(Z,),
        wz_s=one,
        wz_r=(T,),
        wa_r=one,
        kx_r=one,
        kz_r=one,
        tgs_s=one,
        tgs_r=(Y,),
        fc_r=(2,),
        wy_r=one,
        rf_r=(2,),
        cy_r=one,
        lf_r=(2,),
        lg_r=one,
        rg_r=one,
        mm_r=one,
        ky_r=one,
        tg_s=one,
        tg_r=one,
        tq_r=(2,),
        wb_r=one,
    )
    names = list(ins) + list(outs) + list(scratch) + list(sems)

    def body(*refs):
        kernel(Z, X, types.SimpleNamespace(**dict(zip(names, refs))))

    hbm = pl.BlockSpec(memory_space=pltpu.HBM)
    results = pl.pallas_call(
        body,
        out_shape=list(outs.values()),
        in_specs=[hbm] * len(ins),
        out_specs=[hbm] * len(outs),
        scratch_shapes=[pltpu.VMEM(sh, dt) for sh, dt in scratch.values()]
        + [pltpu.SemaphoreType.DMA(sh) for sh in sems.values()],
        compiler_params=pltpu.CompilerParams(
            collective_id=0, has_side_effects=True, vmem_limit_bytes=63 * 1024 * 1024
        ),
    )(*ins.values())

    count = len(outs)

    def write(*refs):
        froms, tos, held = refs[:count], refs[count : 2 * count], refs[2 * count : 3 * count]
        into, out_of = refs[3 * count :]
        first = [pltpu.make_async_copy(froms[i], held[i], into.at[i]) for i in range(count)]
        second = [pltpu.make_async_copy(held[i], tos[i], out_of.at[i]) for i in range(count)]
        for copy in first:
            copy.start()
        for before, after in zip(first, second):
            before.wait()
            after.start()
        for copy in second:
            copy.wait()

    return pl.pallas_call(
        write,
        out_shape=list(outs.values()),
        in_specs=[hbm] * count,
        out_specs=[hbm] * count,
        scratch_shapes=[pltpu.VMEM(o.shape, o.dtype) for o in outs.values()]
        + [pltpu.SemaphoreType.DMA((count,))] * 2,
    )(*results)


def solution(mesh):
    groups = mesh.shape["seq"] // Y
    specs = (
        P("seq", "ch"),
        P("seq", "ch"),
        P("seq", "ch"),
        P("seq", "ch"),
        P("seq", None, None),
        P("seq", None, None),
        P(None, "ch"),
        P(None, "ch"),
    )
    return jax.shard_map(
        functools.partial(layer, groups // X, X),
        mesh=mesh,
        in_specs=specs,
        out_specs=specs,
        check_vma=False,
    )
```

```python
import functools
import types

import jax
import jax.numpy as jnp
from jax import lax
from jax.experimental import pallas as pl
from jax.experimental.pallas import tpu as pltpu
from jax.sharding import PartitionSpec as P

MESH = pl.DeviceIdType.MESH
BF = jnp.bfloat16
F32 = jnp.float32
Y = 4
X = 4
T = 3


def dot(a, b):
    return jnp.dot(a, b, preferred_element_type=F32)


def dot_nt(a, b):
    return lax.dot_general(a, b, (((1,), (1,)), ((), ())), preferred_element_type=F32)


def transposed(a):
    return a.astype(F32).T.astype(BF)


def by_distance(n):
    return sorted(range(1, n), key=lambda k: (min(k, n - k), k))


def kernel(Z, X, r):
    NG = Z * X
    BLK, chans = r.tok_in.shape
    HC = chans // (Y * T)
    CW = 2 * HC
    HB = BLK // 2
    N = Y * BLK
    R = r.pu_in.shape[0]
    RB = Y * R
    half = Z // 2

    s = lax.axis_index("seq")
    c = lax.axis_index("ch")
    g = s // Y
    y = lax.rem(s, Y)
    z = g // X
    x = lax.rem(g, X)
    sib = 1 - c

    def dev(gg, yy):
        return gg * Y + yy

    def in_u(shape):
        return lax.broadcasted_iota(jnp.int32, shape, len(shape) - 1) < HC

    def pick(u, v):
        return jnp.where(in_u(u.shape), u, v)

    def swap(v):
        return pltpu.roll(v, HC, 1)

    def rc(src, dst, send_sem, recv_sem, seq, ch):
        return pltpu.make_async_remote_copy(
            src_ref=src,
            dst_ref=dst,
            send_sem=send_sem,
            recv_sem=recv_sem,
            device_id=(seq, ch),
            device_id_type=MESH,
        )

    def got(ref, sem):
        rc(ref, ref, sem, sem, s, c).wait_recv()

    def sent(ref, sem):
        rc(ref, ref, sem, sem, s, c).wait_send()

    def part(u, v, yy, t):
        q = yy * T + t
        uq = u[:, q // 2 * CW : (q // 2 + 1) * CW]
        vq = v[:, q // 2 * CW : (q // 2 + 1) * CW]
        return pick(uq, swap(vq)) if q % 2 == 0 else pick(swap(uq), vq)

    def whole(land, tile):
        q = 2 * tile
        a = land(q // T, q % T).astype(F32)
        b = land((q + 1) // T, (q + 1) % T).astype(F32)
        return pick(a, swap(b)), pick(swap(a), b)

    def y_send(src_of, dst, send, recv):
        for k in (2, 1, 3):
            to = lax.rem(y + k, Y)
            rc(src_of(to), dst.at[y], send, recv.at[0], dev(g, to), c).start()

    def y_got(dst, recv):
        got(dst.at[pl.ds(0, Y - 1)], recv.at[0])

    def y_sent(like, send):
        sent(like.at[pl.ds(0, Y - 1)], send)

    def load(src, dst, i):
        copy = pltpu.make_async_copy(src, dst, r.in_s.at[i])
        copy.start()
        return copy

    tokbuf = r.tokbuf
    in_pu = load(r.pu_in, r.pu, 0)
    in_pv = load(r.pv_in, r.pv, 1)
    in_tok = [load(r.tok_in.at[pl.ds(h * HB, HB)], tokbuf.at[c, y, h], 2 + 8 * h) for h in range(2)]
    in_cot = load(r.cot_in, r.cot, 3)
    in_cu = load(r.cu_in, r.cu, 4)
    in_cv = load(r.cv_in, r.cv, 5)
    in_factors = [
        load(a.at[0, pl.ds(h * HB, HB)], b.at[y, h], 6 + 2 * i + h)
        for i, (a, b) in enumerate(((r.rf_in, r.rbuf), (r.lf_in, r.lbuf)))
        for h in range(2)
    ]

    barrier = pltpu.get_barrier_semaphore()

    for k in (1, 2, 3):
        pl.semaphore_signal(
            barrier, inc=1, device_id=(dev(g, lax.rem(y + k, Y)), c), device_id_type=MESH
        )
    pl.semaphore_signal(barrier, inc=1, device_id=(s, sib), device_id_type=MESH)
    for dz in range(Z):
        for dx in range(X):
            if dz or dx:
                to = lax.rem(z + dz, Z) * X + lax.rem(x + dx, X)
                pl.semaphore_signal(barrier, inc=1, device_id=(dev(to, y), c), device_id_type=MESH)

    wpad = r.wpad
    wpad[...] = jnp.zeros_like(wpad)
    kpad = r.kpad
    kpad[...] = jnp.zeros_like(kpad)
    in_pu.wait()
    in_pv.wait()
    wpad[0, 0:R, :] = r.pu[...].astype(F32)
    wpad[1, 0:R, :] = r.pv[...].astype(F32)
    for yy in range(Y):
        for t in range(T):
            r.wmsg[yy, t] = part(wpad[0], wpad[1], yy, t).astype(BF)
    pl.semaphore_wait(barrier, NG - 1 + Y)

    y_send(lambda to: r.wmsg.at[to], r.wland, r.few_s.at[0], r.wy_r)
    for copy in in_tok:
        copy.wait()
    rc(tokbuf.at[c, y], tokbuf.at[c, y], r.ts_s.at[0], r.ts_r.at[0], s, sib).start()

    def factor_send(buf, send, recv):
        for k in (2, 1, 3):
            to = lax.rem(y + k, Y)
            rc(buf.at[y, c], buf.at[y, c], send, recv.at[0], dev(g, to), c).start()

    def factor_hand_on(buf, send, recv):
        got(buf.at[pl.ds(0, Y - 1), 0], recv.at[0])
        for k in (1, 3, 2):
            of = lax.rem(y + k, Y)
            rc(buf.at[of, c], buf.at[of, c], send, recv.at[1], s, sib).start()

    def factor(buf, recv):
        got(buf.at[pl.ds(0, Y - 1), 0], recv.at[1])
        return [buf[j].reshape(BLK, BLK) for j in range(Y)]

    r.wland[y] = r.wmsg[y]
    for copy in in_factors:
        copy.wait()
    in_cot.wait()
    cot = r.cot[...].astype(F32)
    for yy in range(Y):
        for t in range(T):
            r.cmsg[yy, t] = part(cot[:HB], cot[HB:], yy, t).astype(BF)
    r.cland[y] = r.cmsg[y]

    row = lax.broadcasted_iota(jnp.int32, (RB, Y * 16), 0)
    col = lax.broadcasted_iota(jnp.int32, (RB, Y * 16), 1)
    sel = jnp.zeros((RB, Y * 16), F32)
    for a in range(Y):
        hit = (row >= R * a) & (row < R * (a + 1)) & (col - row == (16 - R) * a)
        sel = jnp.where(hit, 1.0, sel)
    sel = sel.astype(BF)


    wbuf = r.wbuf
    def along_x(t, of):
        for k in (2, 1, 3):
            to = lax.rem(x + k, X)
            block = wbuf.at[t, of, x]
            rc(block, block, r.gx_s.at[0], r.gx_r.at[t], dev(z * X + to, y), c).start()

    y_got(r.wland, r.wy_r)

    ahead, across, behind = (lax.rem(y + k, Y) for k in (1, 2, 3))

    def token_copy(of, h, to):
        block = tokbuf.at[c, of, h]
        rc(block, block, r.ty_s.at[0], r.ty_r.at[of, h], dev(g, to), c).start()

    def token_hand_on(of, h):
        block = tokbuf.at[c, of, h]
        got(block, r.ty_r.at[of, h])
        rc(block, block, r.ts_s.at[0], r.ts_r.at[0], s, sib).start()

    token_copy(y, 0, ahead)
    token_copy(y, 1, behind)
    token_copy(y, 1, ahead)
    token_copy(y, 0, behind)

    for t in range(T):
        wbuf[t, z, x] = dot(sel, r.wland[:, t].reshape(Y * 16, CW)).astype(BF)
        block = wbuf.at[t, z, x]
        if t < T - 1:
            for k in reversed(by_distance(Z)):
                to = lax.rem(z + k, Z)
                rc(block, block, r.gz_s.at[0], r.gz_r.at[t, z], dev(to * X + x, y), c).start()
        along_x(t, z)


    out_i = lax.broadcasted_iota(jnp.int32, (N, N), 0)
    in_i = lax.broadcasted_iota(jnp.int32, (N, N), 1)

    def hits(a, b):
        return jnp.where(a == b, 1.0, 0.0).astype(BF)

    def swapped_index(v):
        return lax.rem(v // 4, 4) * BLK + (v // 16) * 4 + lax.rem(v, 4)

    def rotated_index(v):
        return lax.rem(v, 4) * BLK + (v // 16) * 4 + lax.rem(v // 4, 4)

    r.to_msg1[...] = hits(in_i, rotated_index(out_i))
    r.from_msg1[...] = hits(out_i, swapped_index(in_i))
    r.to_msg2[...] = hits(in_i, swapped_index(out_i))
    r.from_msg2[...] = hits(out_i, rotated_index(in_i))

    in_cu.wait()
    in_cv.wait()
    kpad[0, 0:3, :] = r.cu[...]
    kpad[1, 0:3, :] = r.cv[...]
    for t in range(T):
        kt = part(kpad[0], kpad[1], 0, t)
        for yy in range(1, Y):
            kt = jnp.where(y == yy, part(kpad[0], kpad[1], yy, t), kt)
        r.kk[t] = kt

    def conv(t, first, second, third):
        return r.kk[t, 0:1] * first + r.kk[t, 1:2] * second + r.kk[t, 2:3] * third

    def gather_x(t, ks):
        for k in ks:
            of = lax.rem(z + k, Z)
            got(wbuf.at[t, of, x], r.gz_r.at[t, of])
            along_x(t, of)

    def gather_z(t):
        got(wbuf.at[t, z, pl.ds(0, X - 1)], r.gx_r.at[t])
        for k in reversed(by_distance(Z)):
            to = lax.rem(z + k, Z)
            rc(wbuf.at[t, z], wbuf.at[t, z], r.gz_s.at[0], r.gz_r.at[t, z], dev(to * X + x, y), c).start()

    ext, cvs, ccb, vb, xb = r.ext, r.cvs, r.ccb, r.vb, r.xb
    cot2, extg, zs, gpb = r.cot2, r.extg, r.zs, r.gpb

    def project(t):
        if t == T - 1:
            for k in by_distance(Z):
                of = lax.rem(z + k, Z)
                got(wbuf.at[t, of], r.gz_r.at[t, of])
        else:
            got(wbuf.at[t, :, pl.ds(0, X - 1)], r.gx_r.at[t])
        w_own = wbuf[t, pl.ds(c * half, half)].reshape(chans, CW)
        w_sib = wbuf[t, pl.ds(sib * half, half)].reshape(chans, CW)
        if t == 0:
            extg[t, 0:N, :] = dot(tokbuf[c].reshape(N, chans), w_own)
            got(tokbuf.at[0], r.ts_r.at[0])

        def rows(first, count):
            at = slice(first * BLK, (first + count) * BLK)
            other = dot(tokbuf[sib, first : first + count].reshape(count * BLK, chans), w_sib)
            if t == 0:
                pre = extg[t, at, :] + other
            else:
                pre = dot(tokbuf[c, first : first + count].reshape(count * BLK, chans), w_own) + other
            ext[t, 8 + first * BLK : 8 + (first + count) * BLK, :] = pre.astype(BF).astype(F32)

        rows(Y - 1, 1)
        rc(ext.at[t, pl.ds(N, 8)], ext.at[t, pl.ds(0, 8)], r.few_s.at[0], r.h_r.at[t], dev(lax.rem(g + 1, NG), y), c).start()
        rows(0, Y - 1)

    zs_to = [lax.rem(z + k, Z) for k in range(Z)]
    xs_to = [lax.rem(x + k, X) for k in range(X)]
    far_first = sorted(
        [(dz, dx) for dz in range(Z) for dx in range(X) if dz or dx],
        key=lambda d: -(min(d[0], Z - d[0]) + min(d[1], X - d[1])),
    )

    def exchange(src, dst, send, recv):
        for dz, dx in far_first:
            to = zs_to[dz] * X + xs_to[dx]
            rc(src.at[to], dst.at[g], send, recv, dev(to, y), c).start()
        dst[g] = src[g]

    def mix_rows(t):
        got(ext.at[t, pl.ds(0, 8)], r.h_r.at[t])

        @pl.when(g == 0)
        def _():
            ext[t, 0:8, :] = jnp.zeros((8, CW), F32)

        for j in range(Y):
            at = j * BLK
            m = r.cland[j, t].astype(F32)
            cot2[t, at : at + HB, :] = swap(m)
            cot2[t, at + HB : at + BLK, :] = m
            cv = conv(
                t,
                ext[t, 8 + at : 8 + at + BLK, :],
                ext[t, 7 + at : 7 + at + BLK, :],
                ext[t, 6 + at : 6 + at + BLK, :],
            )
            cvs[t, at : at + BLK, :] = cv
            cb = cv.astype(BF)
            ccb[t, j] = cb
            vb[at : at + BLK, :] = pick(dot(r.rbuf[j].reshape(BLK, BLK), cb), cot2[t, at : at + BLK, :] * cv).astype(BF)
        r.a1s[t] = dot(r.to_msg1[...], vb[...]).astype(BF).reshape(NG, 16, CW)
        exchange(r.a1s.at[t], r.a1r.at[t], r.a_s.at[0], r.a1_r.at[t])

    def mix_columns(t):
        got(r.a1r.at[t, pl.ds(0, NG - 1)], r.a1_r.at[t])
        xb[t] = dot(r.from_msg1[...], r.a1r[t].reshape(N, CW)).astype(BF)
        for i in range(Y):
            xi = xb[t, i * BLK : (i + 1) * BLK, :]
            both = dot(r.lt[i], xi)
            vb[i * BLK : (i + 1) * BLK, :] = pick(both[:BLK], both[BLK:]).astype(BF)
        r.a2s[t] = dot(r.to_msg2[...], vb[...]).astype(BF).reshape(NG, 16, CW)
        exchange(r.a2s.at[t], r.a2r.at[t], r.a_s.at[0], r.a2_r.at[t])

    def back_rows(t):
        got(r.a2r.at[t, pl.ds(0, NG - 1)], r.a2_r.at[t])
        zs[t] = swap(dot(r.from_msg2[...], r.a2r[t].reshape(N, CW)))
        for j in range(Y):
            at = j * BLK
            zj = zs[t, at : at + BLK, :]
            extg[t, at : at + BLK, :] = pick(dot(r.rt[j], zj.astype(BF)), cot2[t, at : at + BLK, :] * zj)
            m = cvs[t, at : at + BLK, :] * zj
            r.mmsg[t, j] = pick(swap(m[:HB]), m[HB:]).astype(BF)
        rc(extg.at[t, pl.ds(0, 8)], extg.at[t, pl.ds(N, 8)], r.few_s.at[0], r.h_r.at[t], dev(lax.rem(g + NG - 1, NG), y), c).start()
        for k in (2, 1, 3):
            to = lax.rem(y + k, Y)
            rc(r.mmsg.at[t, to], r.mland.at[t, y], r.few_s.at[1], r.mm_r.at[0], dev(g, to), c).start()
        r.mland[t, y] = r.mmsg[t, y]

    wgs, wgq, wgx, zsend, zland = r.wgs, r.wgq, r.wgx, r.zsend, r.zland
    z_order = list(reversed(by_distance(Z))) + [0]

    def gate_back(t):
        got(extg.at[t, pl.ds(N, 8)], r.h_r.at[t])

        @pl.when(g == NG - 1)
        def _():
            extg[t, N : N + 8, :] = jnp.zeros((8, CW), F32)

        for j in range(Y):
            at = j * BLK
            gpb[t, j] = conv(
                t,
                extg[t, at : at + BLK, :],
                extg[t, at + 1 : at + 1 + BLK, :],
                extg[t, at + 2 : at + 2 + BLK, :],
            ).astype(BF)

    far_z = [k for k in z_order if min(k, Z - k) > 2]
    near_z = [k for k in z_order if k not in far_z]
    near_count = X * len(near_z) - 1

    def weight_grads(t):
        gp = gpb[t].reshape(N, CW)
        for i, k in enumerate(z_order):
            to = lax.rem(z + k, Z)
            wgs[t, to] = dot(r.tokt[to], gp).astype(BF).reshape(X, RB, CW)
            if t == T - 1 and k not in far_z:
                for kx in (2, 1, 3, 0):
                    if k or kx:
                        at = to * X + xs_to[kx]
                        rc(wgs.at[t, to, xs_to[kx]], r.wga.at[g], r.wx_s.at[t], r.wa_r.at[0], dev(at, y), c).start()
            elif t == 0:
                ahead, behind, across = x_ways(i)
                rc(wgs.at[t, to, across], wgq.at[to], r.wx_s.at[t], r.wq_r.at[to], dev(z * X + ahead, y), c).start()
                rc(wgs.at[t, to, behind], wgx.at[t, to, 0], r.wx_s.at[t], r.gz_r.at[t, to], dev(z * X + behind, y), c).start()
            else:
                for kx in (2, 1, 3):
                    rc(wgs.at[t, to, xs_to[kx]], wgx.at[t, to, x], r.wx_s.at[t], r.gz_r.at[t, to], dev(z * X + xs_to[kx], y), c).start()
                wgx[t, to, x] = wgs[t, to, x]
        if t == T - 1:
            r.wga[g] = wgs[t, z, x]

    def x_ways(i):
        d = 1 if i % 2 == 0 else X - 1
        return lax.rem(x + d, X), lax.rem(x + X - d, X), lax.rem(x + 2, X)

    def weight_relay():
        t = 0
        for i, k in enumerate(z_order):
            to = lax.rem(z + k, Z)
            ahead = x_ways(i)[0]
            got(wgq.at[to], r.wq_r.at[to])
            wgs[t, to, ahead] = (wgs[t, to, ahead].astype(F32) + wgq[to].astype(F32)).astype(BF)
            rc(wgs.at[t, to, ahead], wgx.at[t, to, 1], r.wx_s.at[t], r.gz_r.at[t, to], dev(z * X + ahead, y), c).start()

    def sum4(land):
        return (land[0].astype(F32) + land[1].astype(F32)) + (land[2].astype(F32) + land[3].astype(F32))

    def weight_sums(t):
        for k in z_order if t < T - 1 else far_z:
            to = lax.rem(z + k, Z)
            if t:
                got(wgx.at[t, to, pl.ds(0, X - 1)], r.gz_r.at[t, to])
                zsend[t, to] = sum4(wgx[t, to]).astype(BF)
            else:
                got(wgx.at[t, to, pl.ds(0, 2)], r.gz_r.at[t, to])
                zsend[t, to] = (
                    wgs[t, to, x].astype(F32) + wgx[t, to, 0].astype(F32) + wgx[t, to, 1].astype(F32)
                ).astype(BF)
            if k:
                rc(zsend.at[t, to], zland.at[t, z], r.wz_s.at[0], r.wz_r.at[t], dev(to * X + x, y), c).start()
        if t < T - 1:
            zland[t, z] = zsend[t, z]

    def left_grads():
        for i in range(Y):
            grads, cols = [], []
            for t in range(T):
                xi = xb[t, i * BLK : (i + 1) * BLK, :]
                xs = swap(xi.astype(F32))
                grads.append(pick(xs, jnp.zeros_like(xs)).astype(BF))
                cols.append(xi)
            r.lgs[i] = dot_nt(jnp.concatenate(grads, axis=1), jnp.concatenate(cols, axis=1)).astype(BF)
        y_send(lambda to: r.lgs.at[to], r.lgl, r.few_s.at[1], r.lg_r)
        r.lgl[y] = r.lgs[y]

    def right_grads():
        for j in range(Y):
            rows = []
            for t in range(T):
                zj = zs[t, j * BLK : (j + 1) * BLK, :]
                rows.append(pick(zj, jnp.zeros_like(zj)).astype(BF))
            r.rgs[j] = dot_nt(
                jnp.concatenate(rows, axis=1), jnp.concatenate([ccb[t, j] for t in range(T)], axis=1)
            ).astype(BF)
        y_send(lambda to: r.rgs.at[to], r.rgl, r.few_s.at[1], r.rg_r)
        r.rgl[y] = r.rgs[y]

    kgs = r.kgs

    def conv_grads():
        kgs[...] = jnp.zeros_like(kgs)
        for t in range(T):
            for lag in range(3):
                kgs[t, lag : lag + 1, :] = jnp.sum(
                    extg[t, 0:N, :] * ext[t, 8 - lag : 8 - lag + N, :], axis=0, keepdims=True
                )
        for k in (2, 1, 3):
            to = lax.rem(x + k, X)
            rc(kgs, r.kgx.at[x], r.few_s.at[1], r.kx_r.at[0], dev(z * X + to, y), c).start()
        r.kgx[x] = kgs[...]

    tgs, tgl, tgy, tgr = r.tgs, r.tgl, r.tgy, r.tgr

    def rows_of(at, chunks):
        return jnp.concatenate([gpb[t, at] for t in chunks], axis=1)

    def half_of(cc, chunks):
        return jnp.concatenate(
            [wbuf[t, pl.ds(cc * half, half)].reshape(chans, CW) for t in chunks], axis=1
        )

    early, late = list(range(T - 1)), [T - 1]

    def token_grads(out, cc, chunks):
        w = half_of(cc, chunks)
        for k in (2, 1, 3, 0):
            of = lax.rem(y + k, Y)
            out[of] = dot_nt(rows_of(of, chunks), w)

    gather_x(0, by_distance(Z)[: Z // 2])
    for of, h, to in ((behind, 0, ahead), (ahead, 1, behind)):
        got(tokbuf.at[c, of, h], r.ty_r.at[of, h])
        token_copy(of, h, to)
        rc(tokbuf.at[c, of, h], tokbuf.at[c, of, h], r.ts_s.at[0], r.ts_r.at[0], s, sib).start()
    gather_x(0, by_distance(Z)[Z // 2 :])
    factor_send(r.rbuf, r.few_s.at[0], r.rf_r)
    y_send(lambda to: r.cmsg.at[to], r.cland, r.few_s.at[0], r.cy_r)
    factor_send(r.lbuf, r.few_s.at[0], r.lf_r)
    gather_z(2)
    gather_x(1, by_distance(Z))
    token_hand_on(behind, 1)
    token_hand_on(ahead, 0)
    token_hand_on(across, 0)
    token_hand_on(across, 1)
    factor_hand_on(r.rbuf, r.few_s.at[0], r.rf_r)
    project(0)
    project(1)
    y_got(r.cland, r.cy_r)
    right = factor(r.rbuf, r.rf_r)
    mix_rows(0)
    project(2)
    mix_rows(1)
    factor_hand_on(r.lbuf, r.few_s.at[0], r.lf_r)
    for j in range(Y):
        r.rt[j] = transposed(right[j])
    for i in range(2):
        r.tokt[i * half : (i + 1) * half] = transposed(tokbuf[i].reshape(N, chans)).reshape(half, X * RB, N)
    mix_rows(2)
    left = factor(r.lbuf, r.lf_r)
    for j in range(Y):
        r.lt[j, 0:BLK] = left[j]
        r.lt[j, BLK:] = transposed(left[j])
    mix_columns(0)
    mix_columns(1)
    mix_columns(2)
    back_rows(0)
    left_grads()
    back_rows(1)
    gate_back(0)
    weight_grads(0)
    y_got(r.lgl, r.lg_r)
    r.lgc[0] = sum4(r.lgl).astype(BF)
    rc(r.lgc.at[0], r.lgc.at[1], r.few_s.at[1], r.fc_r.at[1], s, sib).start()
    back_rows(2)
    conv_grads()
    gate_back(1)
    weight_grads(1)
    token_grads(r.tg_part, sib, early)
    weight_relay()
    gate_back(2)

    w_sib = half_of(sib, late)
    for k in (2, 1, 3, 0):
        of = lax.rem(y + k, Y)
        tgs[of] = (r.tg_part[of] + dot_nt(rows_of(of, late), w_sib)).astype(BF)
        rc(tgs.at[of], tgl.at[of], r.tgs_s.at[0], r.tgs_r.at[of], s, sib).start()
    got(r.kgx.at[pl.ds(0, X - 1)], r.kx_r.at[0])
    kgz, kgz_own = r.kgz, r.kgz_own
    kgz_own[...] = sum4(r.kgx)
    for k in reversed(by_distance(Z)):
        to = lax.rem(z + k, Z)
        rc(kgz_own, kgz.at[z], r.few_s.at[1], r.kz_r.at[0], dev(to * X + x, y), c).start()
    kgz[z] = kgz_own[...]

    weight_grads(2)
    right_grads()
    token_grads(r.tg_part, c, early + late)
    weight_sums(0)

    def y_copy(src, dst, recv, to):
        rc(src, dst, r.tg_s.at[0], recv, dev(g, to), c).start()

    for of in (across, ahead, behind, y):
        got(tgl.at[of], r.tgs_r.at[of])
        total = r.tg_part[of] + tgl[of].astype(F32)
        r.tg_part[of] = total
        tgy[of] = total.astype(BF).reshape(2, HB, chans)
        if of is across:
            y_copy(tgy.at[of, 0], r.tgq.at[0], r.tq_r.at[0], ahead)
            y_copy(tgy.at[of, 1], r.tgq.at[1], r.tq_r.at[1], behind)
        if of is ahead:
            y_copy(tgy.at[of, 1], tgr.at[0, 1], r.tg_r.at[0], ahead)
        if of is behind:
            y_copy(tgy.at[of, 0], tgr.at[1, 0], r.tg_r.at[0], behind)
    weight_sums(2)
    weight_sums(1)
    y_got(r.rgl, r.rg_r)
    r.rgc[0] = sum4(r.rgl).astype(BF)
    rc(r.rgc.at[0], r.rgc.at[1], r.few_s.at[1], r.fc_r.at[0], s, sib).start()
    got(kgz.at[pl.ds(0, Z - 1)], r.kz_r.at[0])
    kgy, kgy_own = r.kgy, r.kgy_own
    total = kgz[0]
    for i in range(1, Z):
        total = total + kgz[i]
    kgy_own[...] = total
    y_send(lambda to: kgy_own, kgy, r.few_s.at[1], r.ky_r)
    kgy[y] = total
    got(r.tgq.at[0], r.tq_r.at[0])
    tgy[ahead, 0] = (r.tg_part[ahead, 0:HB] + r.tgq[0].astype(F32)).astype(BF)
    y_copy(tgy.at[ahead, 0], tgr.at[0, 0], r.tg_r.at[0], ahead)
    got(r.tgq.at[1], r.tq_r.at[1])
    tgy[behind, 1] = (r.tg_part[behind, HB:] + r.tgq[1].astype(F32)).astype(BF)
    y_copy(tgy.at[behind, 1], tgr.at[1, 1], r.tg_r.at[0], behind)


    got(r.mland.at[:, pl.ds(0, Y - 1)], r.mm_r.at[0])
    for tile in range(Y * T // 2):
        top, bottom = whole(lambda yy, t: r.mland[t, yy], tile)
        r.mixed_v[0:HB, tile * CW : (tile + 1) * CW] = top.astype(BF)
        r.mixed_v[HB:BLK, tile * CW : (tile + 1) * CW] = bottom.astype(BF)

    row = lax.broadcasted_iota(jnp.int32, (Y * 16, RB), 0)
    col = lax.broadcasted_iota(jnp.int32, (Y * 16, RB), 1)
    spread = jnp.zeros((Y * 16, RB), F32)
    for a in range(Y):
        hit = (col >= R * a) & (col < R * (a + 1)) & (row - col == (16 - R) * a)
        spread = jnp.where(hit, 1.0, spread)
    spread = spread.astype(BF)
    for t in range(T):
        if t < T - 1:
            got(zland.at[t, pl.ds(0, Z - 1)], r.wz_r.at[t])
            parts = [zland[t, i] for i in range(Z)]
        else:
            got(r.wga.at[pl.ds(0, near_count)], r.wa_r.at[0])
            parts = [r.wga[zs_to[k] * X + i] for k in near_z for i in range(X)]
            if far_z:
                got(zland.at[t, pl.ds(0, len(far_z))], r.wz_r.at[t])
                parts += [zland[t, zs_to[k]] for k in far_z]
        total = parts[0].astype(F32)
        for block in parts[1:]:
            total = total + block.astype(F32)
        r.ymsg[:, t] = dot(spread, total.astype(BF)).astype(BF).reshape(Y, 16, CW)
        for k in (2, 1, 3):
            to = lax.rem(y + k, Y)
            rc(r.ymsg.at[to, t], r.yland.at[y, t], r.few_s.at[1], r.wb_r.at[0], dev(g, to), c).start()
    r.yland[y] = r.ymsg[y]

    stores = []

    def store(src, dst):
        copy = pltpu.make_async_copy(src, dst, r.in_s.at[len(stores)])
        copy.start()
        stores.append(copy)

    store(r.mixed_v, r.mixed_out)

    sent(tokbuf.at[0], r.ts_s.at[0])
    y_sent(tokbuf.at[0], r.ty_s.at[0])
    y_sent(r.wmsg, r.few_s.at[0])
    for i in range(2):
        sent(r.rbuf.at[pl.ds(0, Y - 1), 0], r.few_s.at[0])
        sent(r.lbuf.at[pl.ds(0, Y - 1), 0], r.few_s.at[0])
    y_sent(r.cmsg, r.few_s.at[0])
    for t in range(T):
        if t == T - 1:
            sent(wbuf.at[t, pl.ds(0, Z - 1)], r.gz_s.at[0])
            sent(wbuf.at[t, 0, pl.ds(0, X - 1)], r.gx_s.at[0])
        else:
            sent(wbuf.at[t, pl.ds(0, Z - 1), 0], r.gz_s.at[0])
            for i in range(X - 1):
                sent(wbuf.at[t, :, i], r.gx_s.at[0])
        sent(ext.at[t, pl.ds(0, 8)], r.few_s.at[0])
        sent(extg.at[t, pl.ds(0, 8)], r.few_s.at[0])
        sent(r.a1s.at[t, pl.ds(0, NG - 1)], r.a_s.at[0])
        sent(r.a2s.at[t, pl.ds(0, NG - 1)], r.a_s.at[0])
        if t < T - 1:
            for i in range(X - 1):
                sent(wgs.at[t, :, i], r.wx_s.at[t])
            sent(zland.at[t, pl.ds(0, Z - 1)], r.wz_s.at[0])
        else:
            sent(r.wga.at[pl.ds(0, near_count)], r.wx_s.at[t])
            if far_z:
                sent(r.wga.at[pl.ds(0, (X - 1) * len(far_z))], r.wx_s.at[t])
                sent(zland.at[t, pl.ds(0, len(far_z))], r.wz_s.at[0])
    sent(tgs, r.tgs_s.at[0])
    y_sent(tgs, r.tg_s.at[0])
    sent(r.kgx.at[pl.ds(0, X - 1)], r.few_s.at[1])
    sent(kgz.at[pl.ds(0, Z - 1)], r.few_s.at[1])
    for t in range(T):
        sent(r.mmsg.at[t, pl.ds(0, Y - 1)], r.few_s.at[1])
    y_sent(r.rgs, r.few_s.at[1])
    y_sent(r.lgs, r.few_s.at[1])

    got(r.rgc.at[1], r.fc_r.at[0])
    r.rg_v[0] = r.rgc[0].astype(F32) + r.rgc[1].astype(F32)
    store(r.rg_v, r.rg_out)
    got(r.lgc.at[1], r.fc_r.at[1])
    r.lg_v[0] = r.lgc[0].astype(F32) + r.lgc[1].astype(F32)
    store(r.lg_v, r.lg_out)
    y_got(kgy, r.ky_r)
    for tile in range(Y * T // 2):
        u, v = whole(lambda yy, t: kgy[yy, t], tile)
        r.cug_v[:, tile * CW : (tile + 1) * CW] = u[0:3]
        r.cvg_v[:, tile * CW : (tile + 1) * CW] = v[0:3]
    store(r.cug_v, r.cug_out)
    store(r.cvg_v, r.cvg_out)
    got(tgr, r.tg_r.at[0])
    for h in range(2):
        total = r.tg_part[y, h * HB : (h + 1) * HB] + tgr[0, h].astype(F32) + tgr[1, h].astype(F32)
        r.tg_v[h * HB : (h + 1) * HB, :] = total.astype(BF)
    store(r.tg_v, r.tg_out)
    y_got(r.yland, r.wb_r)
    for tile in range(Y * T // 2):
        u, v = whole(lambda yy, t: r.yland[yy, t], tile)
        r.pug_v[:, tile * CW : (tile + 1) * CW] = u[0:R]
        r.pvg_v[:, tile * CW : (tile + 1) * CW] = v[0:R]
    store(r.pug_v, r.pug_out)
    store(r.pvg_v, r.pvg_out)
    for i in range(2):
        sent(r.rgc.at[0], r.few_s.at[1])
    y_sent(r.ymsg, r.few_s.at[1])
    y_sent(kgy, r.few_s.at[1])
    for copy in stores:
        copy.wait()


def layer(Z, X, tokens, cotangent, proj_u, proj_v, right_factor, left_factor, conv_u, conv_v):
    BLK, chans = tokens.shape
    R = proj_u.shape[0]
    NG = Z * X
    CW = 2 * (chans // (Y * T))
    HB = BLK // 2
    N = Y * BLK
    RB = Y * R
    ins = dict(
        tok_in=tokens,
        cot_in=cotangent,
        pu_in=proj_u,
        pv_in=proj_v,
        rf_in=right_factor,
        lf_in=left_factor,
        cu_in=conv_u,
        cv_in=conv_v,
    )
    shape = jax.ShapeDtypeStruct
    outs = dict(
        mixed_out=shape(tokens.shape, BF),
        tg_out=shape(tokens.shape, BF),
        pug_out=shape(proj_u.shape, F32),
        pvg_out=shape(proj_v.shape, F32),
        rg_out=shape(right_factor.shape, F32),
        lg_out=shape(left_factor.shape, F32),
        cug_out=shape(conv_u.shape, F32),
        cvg_out=shape(conv_v.shape, F32),
    )
    scratch = dict(
        mixed_v=(tokens.shape, BF),
        tg_v=(tokens.shape, BF),
        pug_v=(proj_u.shape, F32),
        pvg_v=(proj_v.shape, F32),
        rg_v=(right_factor.shape, F32),
        lg_v=(left_factor.shape, F32),
        cug_v=(conv_u.shape, F32),
        cvg_v=(conv_v.shape, F32),
        pu=(proj_u.shape, BF),
        pv=(proj_v.shape, BF),
        cot=(cotangent.shape, BF),
        cu=(conv_u.shape, F32),
        cv=(conv_v.shape, F32),
        wpad=((2, 16, chans), F32),
        kpad=((2, 8, chans), F32),
        kk=((T, 8, CW), F32),
        wmsg=((Y, T, 16, CW), BF),
        wland=((Y, T, 16, CW), BF),
        cmsg=((Y, T, HB, CW), BF),
        cland=((Y, T, HB, CW), BF),
        tokbuf=((2, Y, 2, HB, chans), BF),
        rbuf=((Y, 2, HB, BLK), BF),
        lbuf=((Y, 2, HB, BLK), BF),
        rt=((Y, BLK, BLK), BF),
        lt=((Y, 2 * BLK, BLK), BF),
        wbuf=((T, Z, X, RB, CW), BF),
        to_msg1=((N, N), BF),
        from_msg1=((N, N), BF),
        to_msg2=((N, N), BF),
        from_msg2=((N, N), BF),
        cot2=((T, N, CW), F32),
        ext=((T, N + 8, CW), F32),
        extg=((T, N + 8, CW), F32),
        cvs=((T, N, CW), F32),
        zs=((T, N, CW), F32),
        ccb=((T, Y, BLK, CW), BF),
        gpb=((T, Y, BLK, CW), BF),
        vb=((N, CW), BF),
        xb=((T, N, CW), BF),
        a1s=((T, NG, 16, CW), BF),
        a1r=((T, NG, 16, CW), BF),
        a2s=((T, NG, 16, CW), BF),
        a2r=((T, NG, 16, CW), BF),
        tokt=((Z, X * RB, N), BF),
        lgs=((Y, BLK, BLK), BF),
        lgl=((Y, BLK, BLK), BF),
        lgc=((2, BLK, BLK), BF),
        rgs=((Y, BLK, BLK), BF),
        rgl=((Y, BLK, BLK), BF),
        rgc=((2, BLK, BLK), BF),
        mmsg=((T, Y, HB, CW), BF),
        mland=((T, Y, HB, CW), BF),
        kgs=((T, 8, CW), F32),
        kgx=((X, T, 8, CW), F32),
        kgz_own=((T, 8, CW), F32),
        kgz=((Z, T, 8, CW), F32),
        kgy_own=((T, 8, CW), F32),
        kgy=((Y, T, 8, CW), F32),
        tg_part=((Y, BLK, chans), F32),
        tgs=((Y, BLK, chans), BF),
        tgl=((Y, BLK, chans), BF),
        tgy=((Y, 2, HB, chans), BF),
        tgq=((2, HB, chans), BF),
        tgr=((2, 2, HB, chans), BF),
        wgs=((T, Z, X, RB, CW), BF),
        wgx=((T, Z, X, RB, CW), BF),
        wgq=((Z, RB, CW), BF),
        wga=((NG, RB, CW), BF),
        zsend=((T, Z, RB, CW), BF),
        zland=((T, Z, RB, CW), BF),
        ymsg=((Y, T, 16, CW), BF),
        yland=((Y, T, 16, CW), BF),
    )
    one = (1,)
    sems = dict(
        in_s=(11,),
        ts_s=one,
        ts_r=one,
        ty_s=one,
        ty_r=(Y, 2),
        gz_s=one,
        gz_r=(T, Z),
        gx_s=one,
        a_s=one,
        few_s=(2,),
        gx_r=(T,),
        h_r=(T,),
        a1_r=(T,),
        a2_r=(T,),
        wx_s=(T,),
        wq_r=(Z,),
        wz_s=one,
        wz_r=(T,),
        wa_r=one,
        kx_r=one,
        kz_r=one,
        tgs_s=one,
        tgs_r=(Y,),
        fc_r=(2,),
        wy_r=one,
        rf_r=(2,),
        cy_r=one,
        lf_r=(2,),
        lg_r=one,
        rg_r=one,
        mm_r=one,
        ky_r=one,
        tg_s=one,
        tg_r=one,
        tq_r=(2,),
        wb_r=one,
    )
    names = list(ins) + list(outs) + list(scratch) + list(sems)

    def body(*refs):
        kernel(Z, X, types.SimpleNamespace(**dict(zip(names, refs))))

    hbm = pl.BlockSpec(memory_space=pltpu.HBM)
    results = pl.pallas_call(
        body,
        out_shape=list(outs.values()),
        in_specs=[hbm] * len(ins),
        out_specs=[hbm] * len(outs),
        scratch_shapes=[pltpu.VMEM(sh, dt) for sh, dt in scratch.values()]
        + [pltpu.SemaphoreType.DMA(sh) for sh in sems.values()],
        compiler_params=pltpu.CompilerParams(
            collective_id=0, has_side_effects=True, vmem_limit_bytes=63 * 1024 * 1024
        ),
    )(*ins.values())

    count = len(outs)

    def write(*refs):
        froms, tos, held = refs[:count], refs[count : 2 * count], refs[2 * count : 3 * count]
        into, out_of = refs[3 * count :]
        first = [pltpu.make_async_copy(froms[i], held[i], into.at[i]) for i in range(count)]
        second = [pltpu.make_async_copy(held[i], tos[i], out_of.at[i]) for i in range(count)]
        for copy in first:
            copy.start()
        for before, after in zip(first, second):
            before.wait()
            after.start()
        for copy in second:
            copy.wait()

    return pl.pallas_call(
        write,
        out_shape=list(outs.values()),
        in_specs=[hbm] * count,
        out_specs=[hbm] * count,
        scratch_shapes=[pltpu.VMEM(o.shape, o.dtype) for o in outs.values()]
        + [pltpu.SemaphoreType.DMA((count,))] * 2,
    )(*results)


def solution(mesh):
    groups = mesh.shape["seq"] // Y
    specs = (
        P("seq", "ch"),
        P("seq", "ch"),
        P("seq", "ch"),
        P("seq", "ch"),
        P("seq", None, None),
        P("seq", None, None),
        P(None, "ch"),
        P(None, "ch"),
    )
    return jax.shard_map(
        functools.partial(layer, groups // X, X),
        mesh=mesh,
        in_specs=specs,
        out_specs=specs,
        check_vma=False,
    )
```
